32 devices in a mesh: dp: 8 (over z, y), head: 4 (over x, core).
Axes of the slice: x: 2, y: 2, z: 4, core: 2. Of those that a mesh axis runs over, the one named last changes fastest.
Arguments:
- tokens: bfloat16 [2, 4096, 512], P(None, ('dp', 'head')), may hold values from -6 to 6
- cotangent: bfloat16 [2, 4096, 512], P(None, ('dp', 'head')), may hold values from -6 to 6
- lengths: int32 [2, 8, 8], P(None, 'dp'), may hold values from 1 to 448, 512 in all within a row
- halting: int32 [2, 2, 4096], P(None, None, ('dp', 'head')), may hold values 0 or 1
- w_query: bfloat16 [512, 512], P(('dp', 'head')), may hold values from -0.25 to 0.25
- w_key: bfloat16 [512, 512], P(('dp', 'head')), may hold values from -0.25 to 0.25
- w_value: bfloat16 [512, 512], P(('dp', 'head')), may hold values from -0.25 to 0.25
- w_out: bfloat16 [512, 512], P(('dp', 'head')), may hold values from -4 to 4
- w_in: bfloat16 [512, 2048], P(('dp', 'head')), may hold values from -0.25 to 0.25
- w_hidden: bfloat16 [2048, 512], P(('dp', 'head')), may hold values from -0.125 to 0.125
- w_halt: bfloat16 [512], P(('dp', 'head')), may hold values from -0.25 to 0.25
- gain_attn: bfloat16 [512], P(('dp', 'head')), may hold values from 0.5 to 1.5
- shift_attn: bfloat16 [512], P(('dp', 'head')), may hold values from -3 to 3
- gain_ffn: bfloat16 [512], P(('dp', 'head')), may hold values from 0.5 to 1.5
- shift_ffn: bfloat16 [512], P(('dp', 'head')), may hold values from -3 to 3
Outputs:
- output: float32 [2, 4096, 512], P(None, ('dp', 'head'))
- input_grad: float32 [2, 4096, 512], P(None, ('dp', 'head'))
- grad_query: float32 [512, 512], P(('dp', 'head'))
- grad_key: float32 [512, 512], P(('dp', 'head'))
- grad_value: float32 [512, 512], P(('dp', 'head'))
- grad_out: float32 [512, 512], P(('dp', 'head'))
- grad_in: float32 [512, 2048], P(('dp', 'head'))
- grad_hidden: float32 [2048, 512], P(('dp', 'head'))
- grad_halt: float32 [512], P(('dp', 'head'))
- grad_gain_attn: float32 [512], P(('dp', 'head'))
- grad_shift_attn: float32 [512], P(('dp', 'head'))
- grad_gain_ffn: float32 [512], P(('dp', 'head'))
- grad_shift_ffn: float32 [512], P(('dp', 'head'))
The draws below stay inside these ranges and needn't reach their ends.
Inputs may be any that keep to these rules, and one draw needn't show every extreme that they name: Each row holds the 8 sentence lengths of one pack, in order; they sum to 512 and the longest is exactly 448.
All inputs are finite; a program needn't handle non-finite values. No bound on the sum of `halting` on one device may be relied on, other than what follows from the above.
Results may differ from the reference program's by a relative error of at most 0.025.
Values may be sent and summed in bfloat16 or wider, within the bound.
No kernel may reach another device: no remote copies, remote signals or barrier semaphores. Data moves between devices by JAX's collectives and lax.ppermute only.
A program may use at most 128 MiB of HBM per device.

```python
import math
import jax
import jax.numpy as jnp
import numpy as np
from jax import lax

D = 512
HEADS = 8
FF = 2048
HD = 64
TOK_DEV = 128
MB = 2
STEPS = 2
SENTS = 8
PACK = 512
PACKS = 8
TOKENS = 4096


def plant(values, own_key, low, top_value):
    index_at = [jax.random.randint(jax.random.fold_in(own_key, axis), (), 0, length) for axis, length in enumerate(values.shape)]
    main_axis = values.shape.index(max(values.shape))
    beside = index_at[:main_axis] + [(index_at[main_axis] + 1) % values.shape[main_axis]] + index_at[main_axis + 1:]
    return values.at[tuple(index_at)].set(low).at[tuple(beside)].set(top_value)


def shard_levels(stream_key, shape, pieces, smallest, top_value):
    level, own = 1.0, jax.random.fold_in(stream_key, 6)
    for axis_at, parts in pieces:
        heights = jnp.exp(jax.random.uniform(jax.random.fold_in(own, axis_at), (parts,), jnp.float32, smallest / len(pieces), top_value / len(pieces)))
        level = level * jnp.repeat(heights, shape[axis_at] // parts).reshape([-1 if axis == axis_at else 1 for axis in range(len(shape))])
    return level


def length_profile(amount, total, limit, lean):
    portions = [(1 << 20) // math.isqrt(rank ** lean) + 1 for rank in range(2, amount + 1)]
    rest, counts = total - limit - (amount - 1), [1] * (amount - 1)
    while rest > 0:
        free = [i for i in range(amount - 1) if counts[i] < limit]
        mass, remaining = sum([portions[i] for i in free]), rest
        for i in free:
            extra = min(limit - counts[i], max(1, remaining * portions[i] // mass), rest)
            counts[i] = counts[i] + extra
            rest = rest - extra
    return np.array([limit] + counts)


def uneven(stream_key, number_of, total, most, slope):
    if number_of == 2:
        one = jax.random.randint(stream_key, (), max(1, total - most), min(most, total - 1) + 1)
        return jnp.stack([one, total - one])
    sizes = jnp.asarray(length_profile(number_of, total, most, slope), jnp.int32)
    couples = (number_of - 1) // 2
    giver, sink = sizes[1:1 + 2 * couples:2], sizes[2:2 + 2 * couples:2]
    slack = jnp.minimum(giver - 1, most - sink)
    shifted = jax.random.randint(jax.random.fold_in(stream_key, 1), (couples,), 0, 1 << 20) % (slack + 1)
    sizes = sizes.at[1:1 + 2 * couples:2].set(giver - shifted).at[2:2 + 2 * couples:2].set(sink + shifted)
    return sizes[jax.random.permutation(jax.random.fold_in(stream_key, 2), number_of)]


def normal_values(stream_key, extent, scale, limit, pieces=(), kind=jnp.bfloat16):
    values = jax.random.normal(stream_key, extent, jnp.float32) * scale
    if len(pieces) > 0:
        values = shard_levels(stream_key, extent, pieces, -0.22, 0.18) * values
    return jnp.clip(values, min=-limit, max=limit).astype(kind)


def setup_inputs(seed: int = 0) -> dict:
    key_list = jax.random.split(jax.random.key(seed), 16)
    return {
        "tokens": normal_values(key_list[0], (MB, TOKENS, D), 1.0, 6.0, ((1, 32),)),
        "cotangent": normal_values(key_list[1], (MB, TOKENS, D), 1.0, 6.0, ((1, 32),)),
        "lengths": jax.vmap(lambda own: uneven(own, SENTS, PACK, PACK - TOK_DEV // 2, 2))(jax.random.split(key_list[2], MB * PACKS)).reshape((MB, PACKS, SENTS)).astype(jnp.int32),
        "halting": plant((jax.random.randint(key_list[3], (STEPS, MB, TOKENS), 0, 4) < 3).astype(jnp.int32), jax.random.fold_in(key_list[3], 1), 0, 1),
        "w_query": normal_values(key_list[4], (D, D), D ** -0.5, 0.25, ((0, 32),)),
        "w_key": normal_values(key_list[5], (D, D), D ** -0.5, 0.25, ((0, 32),)),
        "w_value": normal_values(key_list[6], (D, D), D ** -0.5, 0.25, ((0, 32),)),
        "w_out": normal_values(key_list[7], (D, D), 2 ** -0.5, 4.0, ((0, 32),)),
        "w_in": normal_values(key_list[8], (D, FF), D ** -0.5, 0.25, ((0, 32),)),
        "w_hidden": normal_values(key_list[9], (FF, D), FF ** -0.5, 0.125, ((0, 32),)),
        "w_halt": normal_values(key_list[10], (D,), D ** -0.5, 0.25, ((0, 32),)),
        "gain_attn": jnp.clip(1.0 + 0.1 * jax.random.normal(key_list[11], (D,), jnp.float32), 0.5, 1.5).astype(jnp.bfloat16),
        "shift_attn": normal_values(key_list[12], (D,), 0.5, 3.0, ((0, 32),)),
        "gain_ffn": jnp.clip(1.0 + 0.1 * jax.random.normal(key_list[13], (D,), jnp.float32), 0.5, 1.5).astype(jnp.bfloat16),
        "shift_ffn": normal_values(key_list[14], (D,), 0.5, 3.0, ((0, 32),)),
    }


@jax.custom_vjp
def low(v):
    return lax.optimization_barrier(v.astype(jnp.bfloat16)).astype(jnp.float32)

@jax.custom_vjp
def low_back(v):
    return v

def low_keep(v):
    return (low(v), None)

def low_pass(kept, grad):
    return (grad,)

def back_keep(v):
    return (v, None)

def back_low(kept, grad):
    return (low(grad),)
low.defvjp(low_keep, low_pass)
low_back.defvjp(back_keep, back_low)
EPSILON = 1e-06
HIGHEST = lax.Precision.HIGHEST

def signal(position, features, step_value):
    half_width = features // 2
    rates = jnp.exp(jnp.arange(half_width, dtype=jnp.float32) * (-jnp.log(10000.0) / max(half_width - 1, 1)))
    angles = position[:, None] * rates[None, :]
    step_angles = step_value * rates
    moving = jnp.concatenate([jnp.sin(angles), jnp.cos(angles)], axis=1)
    steady = jnp.concatenate([jnp.sin(step_angles), jnp.cos(step_angles)])
    return moving + steady[None, :]

def norm_apply(values, gain, shift):
    center = values - lax.optimization_barrier(jnp.mean(values, axis=-1, keepdims=True))
    spread = lax.optimization_barrier(jnp.mean(center * center, axis=-1, keepdims=True))
    return center * lax.rsqrt(spread + EPSILON) * gain + shift

def pack_layout(sizes, length):
    ends = jnp.cumsum(sizes).astype(jnp.int32)
    starts = (ends - sizes).astype(jnp.int32)
    places = jnp.arange(length, dtype=jnp.int32)
    segment = lax.optimization_barrier(jnp.sum((places[:, None] >= ends[None, :]).astype(jnp.int32), axis=1))
    begins = lax.optimization_barrier(jnp.max(jnp.where(starts[None, :] <= places[:, None], starts[None, :], 0), axis=1))
    return (segment, (places - begins).astype(jnp.float32))

def layer(params, inputs, segment):
    query_w, key_w, value_w, out_w, in_w, hidden_w, halt_w, gain_attn, shift_attn, gain_ffn, shift_ffn = params
    length = inputs.shape[0]
    rounded = low(inputs)
    queries = low_back(low(jnp.dot(rounded, query_w, precision=HIGHEST)))
    key_rows = low_back(low(jnp.dot(rounded, key_w, precision=HIGHEST)))
    value_rows = low_back(low(jnp.dot(rounded, value_w, precision=HIGHEST)))
    query_heads = queries.reshape(length, HEADS, HD)
    key_heads = key_rows.reshape(length, HEADS, HD)
    value_heads = value_rows.reshape(length, HEADS, HD)
    scores = low_back(jnp.einsum('qhd,khd->hqk', query_heads, key_heads, precision=HIGHEST) * HD ** (-0.5))
    same = (segment[:, None] == segment[None, :])[None]
    masked = jnp.where(same, scores, -1e+30)
    row_max = lax.optimization_barrier(jnp.max(masked, axis=-1, keepdims=True))
    exp_scores = jnp.exp(masked - row_max)
    attend = exp_scores / lax.optimization_barrier(jnp.sum(exp_scores, axis=-1, keepdims=True))
    context = jnp.einsum('hqk,khd->qhd', low(attend), value_heads, precision=HIGHEST).reshape(length, HEADS * HD)
    context = low_back(low(context))
    first_sum = inputs + low_back(jnp.dot(context, out_w, precision=HIGHEST))
    normed = norm_apply(first_sum, gain_attn, shift_attn)
    inner_part = low_back(jnp.dot(low(normed), in_w, precision=HIGHEST))
    hidden = low(jax.nn.gelu(inner_part))
    second_sum = normed + low_back(jnp.dot(hidden, hidden_w, precision=HIGHEST))
    return norm_apply(second_sum, gain_ffn, shift_ffn)

def forward_pack(params, carried, segment, position, halt_rows):
    halt_w = params[6]
    pooled = jnp.zeros_like(carried)
    for step_index in range(STEPS):
        running = halt_rows[step_index].astype(jnp.float32)[:, None]
        inputs = carried + signal(position, D, float(step_index))
        updated = layer(params, inputs, segment)
        halt_rate = jax.nn.sigmoid(jnp.dot(updated, halt_w, precision=HIGHEST))[:, None]
        pooled = pooled + running * halt_rate * updated
        carried = carried + running * (updated - carried)
    return carried + pooled

def reference(tokens, cotangent, lengths, halting, w_query, w_key, w_value, w_out, w_in, w_hidden, w_halt, gain_attn, shift_attn, gain_ffn, shift_ffn):
    params = tuple((member.astype(jnp.float32) for member in (w_query, w_key, w_value, w_out, w_in, w_hidden, w_halt, gain_attn, shift_attn, gain_ffn, shift_ffn)))
    packs = MB * PACKS
    states = tokens.astype(jnp.float32).reshape(packs, PACK, D)
    cotans = cotangent.astype(jnp.float32).reshape(packs, PACK, D)
    sizes_all = lengths.reshape(packs, SENTS)
    halts = jnp.transpose(halting.reshape(STEPS, packs, PACK), (1, 0, 2))

    def per_pack(totals, packed):
        carried, cotan, sizes, halt_rows = packed
        segment, position = pack_layout(sizes, PACK)

        def evaluate(weights, start_state):
            return forward_pack(weights, start_state, segment, position, halt_rows)
        result, pullback = jax.vjp(evaluate, params, carried)
        grad_params, grad_state = pullback(cotan)
        totals = tuple((old + new for old, new in zip(totals, grad_params)))
        return (totals, (result, grad_state))
    zeros = tuple((jnp.zeros_like(member) for member in params))
    totals, (results, grad_states) = lax.scan(per_pack, zeros, (states, cotans, sizes_all, halts))
    output = results.reshape(MB, TOKENS, D)
    input_grad = grad_states.reshape(MB, TOKENS, D)
    return (output, input_grad, totals[0], totals[1], totals[2], totals[3], totals[4], totals[5], totals[6], totals[7], totals[8], totals[9], totals[10])
```

```python
import functools

import jax
import jax.numpy as jnp
from jax import lax
from jax.experimental import pallas as pl
from jax.experimental.pallas import tpu as pltpu
from jax.sharding import PartitionSpec as P

HD = 64
EPSILON = 1e-06
F32 = jnp.float32
BF16 = jnp.bfloat16
LANES = 128
ROWS = 32
ATT_ROWS = 128
BLOCK = 512
VECS = 5
GELU_A = 0.7978845608028654
GELU_B = 0.044715


def dot(a, b, ca=1, cb=0):
    return lax.dot_general(a, b, (((ca,), (cb,)), ((), ())), preferred_element_type=F32)


def chunks(total, size):
    size = min(size, total)
    return [slice(i, i + size) for i in range(0, total, size)]


def wide(column):
    return jnp.broadcast_to(column, (column.shape[0], LANES))


def mean(values):
    return jnp.sum(values, axis=-1, keepdims=True) * (1.0 / values.shape[-1])


def fold(values):
    return jnp.sum(values.reshape(values.shape[0] // 8, 8, values.shape[1]), axis=0)


def head_mask(rows):
    lane = lax.broadcasted_iota(jnp.int32, (rows, LANES), 1)
    return lane < HD


def normalize(values):
    center = values - mean(values)
    inverse = lax.rsqrt(mean(center * center) + EPSILON)
    return center * inverse, inverse


def normalize_back(unit, inverse, grad):
    return inverse * (grad - mean(grad) - unit * mean(grad * unit))


def split_heads(values_ref, stacked_ref):
    rows = values_ref.shape[0]
    for part in chunks(rows, ATT_ROWS):
        first = head_mask(part.stop - part.start)
        for pair in range(stacked_ref.shape[0]):
            block = values_ref[part, pair * LANES : (pair + 1) * LANES].astype(F32)
            stacked_ref[pair, part, :] = jnp.where(first, block, 0.0).astype(BF16)
            stacked_ref[pair, rows + part.start : rows + part.stop, :] = jnp.where(
                first, 0.0, block
            ).astype(BF16)


def project(rown_ref, roth_ref, wa_ref, q_ref, q2_ref, k_ref, v_ref):
    rows, width = rown_ref.shape
    q_ref[...] = (
        dot(rown_ref[...], wa_ref[:, :width]).astype(BF16).astype(F32) * HD**-0.5
    ).astype(BF16)
    split_heads(q_ref, q2_ref)
    for at, source in ((0, rown_ref), (rows, roth_ref)):
        span = slice(at, at + source.shape[0])
        k_ref[span, :] = dot(source[...], wa_ref[:, width : 2 * width]).astype(BF16)
        v_ref[span, :] = dot(source[...], wa_ref[:, 2 * width : 3 * width]).astype(BF16)


def attend(q2_ref, k_ref, v_ref, segq_ref, segk_ref, bias_ref, p_ref, ctx_ref, o_ref):
    rows, length = bias_ref.shape
    for part in chunks(rows, ROWS):
        bias_ref[part, :] = jnp.where(segq_ref[part, :] == segk_ref[...], 0.0, -1e30)
    for pair in range(q2_ref.shape[0]):
        cols = slice(pair * LANES, (pair + 1) * LANES)
        for part in chunks(2 * rows, ATT_ROWS):
            size = part.stop - part.start
            base = part.start % rows
            scores = dot(q2_ref[pair, part, :], k_ref[:, cols], 1, 1)
            scores = scores + bias_ref[base : base + size, :]
            weights = jnp.exp(scores - jnp.max(scores, axis=-1, keepdims=True))
            inverse = 1.0 / jnp.sum(weights, axis=-1, keepdims=True)
            low = (weights * inverse).astype(BF16)
            p_ref[pair, part, :] = low
            o_ref[part, :] = dot(low, v_ref[:, cols])
        for part in chunks(rows, ATT_ROWS):
            first = head_mask(part.stop - part.start)
            second = o_ref[rows + part.start : rows + part.stop, :]
            ctx_ref[part, cols] = jnp.where(first, o_ref[part, :], second).astype(BF16)


def first_norm(x_ref, ctx_ref, wo_ref, vec_ref, acc_ref, n1_ref, r1_ref, nlow_ref):
    acc_ref[...] = dot(ctx_ref[...], wo_ref[...])
    for part in chunks(x_ref.shape[0], ROWS):
        unit, inverse = normalize(x_ref[part, :] + acc_ref[part, :])
        n1_ref[part, :] = unit
        r1_ref[part, :] = wide(inverse)
        nlow_ref[part, :] = (unit * vec_ref[1:2, :] + vec_ref[2:3, :]).astype(BF16)


def feed_forward(nlow_ref, win_ref, whid_ref, inner_ref, hid_ref, dg_ref, acc_ref):
    rows = nlow_ref.shape[0]
    for cols in chunks(hid_ref.shape[1], BLOCK):
        inner_ref[...] = dot(nlow_ref[...], win_ref[:, cols])
        for part in chunks(rows, ROWS):
            x = inner_ref[part, :]
            square = x * x
            t = jnp.tanh(x * (GELU_A + GELU_A * GELU_B * square))
            half = 0.5 + 0.5 * t
            hid_ref[part, cols] = (x * half).astype(BF16)
            slope = 0.5 * x * (1.0 - t * t) * (GELU_A + 3.0 * GELU_A * GELU_B * square)
            dg_ref[part, cols] = (half + slope).astype(BF16)
    acc_ref[...] = dot(hid_ref[...], whid_ref[...])


def second_norm(part, vec_ref, n1_ref, acc_ref):
    normed = n1_ref[part, :] * vec_ref[1:2, :] + vec_ref[2:3, :]
    unit, inverse = normalize(normed + acc_ref[part, :])
    updated = unit * vec_ref[3:4, :] + vec_ref[4:5, :]
    rate = jax.nn.sigmoid(jnp.sum(updated * vec_ref[0:1, :], axis=-1, keepdims=True))
    return unit, inverse, updated, rate


def tail_back(
    part, step, gs, gp, halt_ref, vec_ref, n2_ref, r2_ref, rate_ref, b2_ref, gsec_ref, base_ref, sums_ref
):
    keep = halt_ref[part, step : step + 1].astype(F32)
    unit = n2_ref[part, :]
    updated = unit * vec_ref[3:4, :] + vec_ref[4:5, :]
    rate = rate_ref[part, 0:1]
    logit = keep * jnp.sum(gp * updated, axis=-1, keepdims=True) * rate * (1.0 - rate)
    grad = keep * gs + (keep * rate) * gp + logit * vec_ref[0:1, :]
    base_ref[part, :] = gs - keep * gs
    sums_ref[0] += fold(logit * updated)
    sums_ref[3] += fold(grad * unit)
    sums_ref[4] += fold(grad)
    back = normalize_back(unit, r2_ref[part, 0:1], grad * vec_ref[3:4, :])
    gsec_ref[part, :] = back
    b2_ref[part, :] = back.astype(BF16)


def feed_back(b2_ref, dg_ref, win_ref, whid_ref, inner_ref, b1_ref, acc_ref):
    rows = b2_ref.shape[0]
    for cols in chunks(dg_ref.shape[1], BLOCK):
        inner_ref[...] = dot(b2_ref[...], whid_ref[cols, :], 1, 1)
        for part in chunks(rows, ROWS):
            b1_ref[part, cols] = (inner_ref[part, :] * dg_ref[part, cols].astype(F32)).astype(BF16)
    acc_ref[...] = dot(b1_ref[...], win_ref[...], 1, 1)


def middle_back(gsec_ref, acc_ref, vec_ref, n1_ref, r1_ref, b0_ref, base_ref, sums_ref):
    for part in chunks(gsec_ref.shape[0], ROWS):
        grad = gsec_ref[part, :] + acc_ref[part, :]
        unit = n1_ref[part, :]
        sums_ref[1] += fold(grad * unit)
        sums_ref[2] += fold(grad)
        back = normalize_back(unit, r1_ref[part, 0:1], grad * vec_ref[1:2, :])
        base_ref[part, :] += back
        b0_ref[part, :] = back.astype(BF16)


def attend_back(
    gctx_ref, g2_ref, q2_ref, k_ref, v_ref, p_ref, ctx_ref, ds_ref, dq2_ref, dqkv_ref, doth_ref
):
    rows, width = gctx_ref.shape
    split_heads(gctx_ref, g2_ref)
    for pair in range(q2_ref.shape[0]):
        cols = slice(pair * LANES, (pair + 1) * LANES)
        for part in chunks(2 * rows, ATT_ROWS):
            size = part.stop - part.start
            base = part.start % rows
            grad = g2_ref[pair, part, :]
            delta = jnp.sum(
                grad.astype(F32) * ctx_ref[base : base + size, cols].astype(F32),
                axis=-1,
                keepdims=True,
            )
            back = dot(grad, v_ref[:, cols], 1, 1)
            low = (p_ref[pair, part, :].astype(F32) * (back - delta)).astype(BF16)
            ds_ref[part, :] = low
            dq2_ref[part, :] = dot(low, k_ref[:, cols])
        for part in chunks(rows, ATT_ROWS):
            first = head_mask(part.stop - part.start)
            second = dq2_ref[rows + part.start : rows + part.stop, :]
            dqkv_ref[part, cols] = (
                jnp.where(first, dq2_ref[part, :], second) * HD**-0.5
            ).astype(BF16)
        for index, (left, right) in enumerate(
            ((ds_ref[...], q2_ref[pair]), (p_ref[pair], g2_ref[pair]))
        ):
            both = dot(left, right, 0, 0).astype(BF16)
            at = index * width + pair * LANES
            dqkv_ref[:, width + at : width + at + LANES] = both[:rows]
            doth_ref[:, at : at + LANES] = both[rows:]


def inputs_back(dqkv_ref, doth_ref, wa_ref, base_ref, gs_ref, goth_ref):
    width = base_ref.shape[1]
    gs_ref[...] = base_ref[...] + dot(dqkv_ref[...], wa_ref[:, : 3 * width], 1, 1)
    goth_ref[...] = dot(doth_ref[...], wa_ref[:, width : 3 * width], 1, 1).astype(BF16)


def attend_kernel(
    x_ref, rown_ref, roth_ref, wa_ref, vec_ref, segq_ref, segk_ref,
    q2_ref, k_ref, v_ref, p_ref, ctx_ref, n1_ref, r1_ref, nlow_ref,
    q_ref, bias_ref, o_ref, acc_ref,
):
    width = x_ref.shape[1]
    project(rown_ref, roth_ref, wa_ref, q_ref, q2_ref, k_ref, v_ref)
    attend(q2_ref, k_ref, v_ref, segq_ref, segk_ref, bias_ref, p_ref, ctx_ref, o_ref)
    first_norm(
        x_ref, ctx_ref, wa_ref.at[:, 3 * width : 4 * width], vec_ref, acc_ref, n1_ref, r1_ref, nlow_ref
    )


def ffn_kernel(
    nlow_ref, n1_ref, tok_ref, sig_ref, halt_ref, vec_ref, win_ref, whid_ref,
    hid_ref, dg_ref, n2_ref, r2_ref, rate_ref, state_ref, pooled_ref, x_ref, rown_ref,
    inner_ref, acc_ref,
):
    feed_forward(nlow_ref, win_ref, whid_ref, inner_ref, hid_ref, dg_ref, acc_ref)
    for part in chunks(tok_ref.shape[0], ROWS):
        unit, inverse, updated, rate = second_norm(part, vec_ref, n1_ref, acc_ref)
        keep = halt_ref[part, 0:1].astype(F32)
        n2_ref[part, :] = unit
        r2_ref[part, :] = wide(inverse)
        rate_ref[part, :] = wide(rate)
        pooled_ref[part, :] = (keep * rate) * updated
        state = tok_ref[part, :].astype(F32)
        state = state + keep * (updated - state)
        state_ref[part, :] = state
        inputs = state + sig_ref[part, :]
        x_ref[part, :] = inputs
        rown_ref[part, :] = inputs.astype(BF16)


def turn_kernel(
    x_ref, rown_ref, roth_ref, wa_ref, win_ref, whid_ref, vec_ref, segq_ref, segk_ref,
    state_ref, pooled_ref, cot_ref, halt_ref,
    out_ref, gs_ref, goth_ref, nlow_ref, hid_ref, b1_ref, b2_ref, ctx_ref, b0_ref, dqkv_ref, doth_ref, vg_ref,
    q_ref, q2_ref, k_ref, v_ref, p_ref, bias_ref, o_ref, acc_ref, n1_ref, r1_ref, inner_ref, dg_ref,
    n2_ref, r2_ref, rate_ref, gsec_ref, base_ref, sums_ref, gctx_ref, g2_ref, ds_ref,
):
    width = x_ref.shape[1]
    wo_ref = wa_ref.at[:, 3 * width : 4 * width]
    sums_ref[...] = jnp.zeros_like(sums_ref)
    project(rown_ref, roth_ref, wa_ref, q_ref, q2_ref, k_ref, v_ref)
    attend(q2_ref, k_ref, v_ref, segq_ref, segk_ref, bias_ref, p_ref, ctx_ref, o_ref)
    first_norm(x_ref, ctx_ref, wo_ref, vec_ref, acc_ref, n1_ref, r1_ref, nlow_ref)
    feed_forward(nlow_ref, win_ref, whid_ref, inner_ref, hid_ref, dg_ref, acc_ref)
    for part in chunks(x_ref.shape[0], ROWS):
        unit, inverse, updated, rate = second_norm(part, vec_ref, n1_ref, acc_ref)
        keep = halt_ref[part, 1:2].astype(F32)
        n2_ref[part, :] = unit
        r2_ref[part, :] = wide(inverse)
        rate_ref[part, :] = wide(rate)
        state = state_ref[part, :]
        state = state + keep * (updated - state)
        out_ref[part, :] = state + (pooled_ref[part, :] + (keep * rate) * updated)
        cot = cot_ref[part, :].astype(F32)
        tail_back(
            part, 1, cot, cot, halt_ref, vec_ref, n2_ref, r2_ref, rate_ref, b2_ref, gsec_ref, base_ref,
            sums_ref,
        )
    feed_back(b2_ref, dg_ref, win_ref, whid_ref, inner_ref, b1_ref, acc_ref)
    middle_back(gsec_ref, acc_ref, vec_ref, n1_ref, r1_ref, b0_ref, base_ref, sums_ref)
    gctx_ref[...] = dot(b0_ref[...], wo_ref[...], 1, 1).astype(BF16)
    attend_back(
        gctx_ref, g2_ref, q2_ref, k_ref, v_ref, p_ref, ctx_ref, ds_ref, o_ref, dqkv_ref, doth_ref
    )
    inputs_back(dqkv_ref, doth_ref, wa_ref, base_ref, gs_ref, goth_ref)
    vg_ref[...] = jnp.zeros_like(vg_ref)
    for index in range(VECS):
        vg_ref[index : index + 1, :] = jnp.sum(sums_ref[index], axis=0, keepdims=True)


def place(fast, me_ref, full_ref, outs, cols):
    if not fast:
        outs[0][:, cols] = full_ref[...]
        return
    keep_ref, send_ref = outs
    for relative in range(8):
        target = send_ref if relative % 2 else keep_ref
        target[relative // 2, :, :, cols] = full_ref[:, relative ^ me_ref[0]].astype(BF16)


def ffn_back_kernel(
    fast, me_ref, gs_ref, more_ref, cot_ref, halt_ref, vec_ref, win_ref, whid_ref, wo_ref,
    n2_ref, r2_ref, rate_ref, n1_ref, r1_ref, hid_ref, dg_ref, nlow_ref, ctx_ref,
    nlow1_ref, hid1_ref, b11_ref, b21_ref, ctx1_ref, b01_ref, vg1_ref,
    *rest,
):
    count = 2 if fast else 1
    hid_outs, rest = rest[:count], rest[count:]
    in_outs, rest = rest[:count], rest[count:]
    (dwo_ref, vg_ref, base_ref, gctx_ref) = rest[:4]
    b2_ref, gsec_ref, sums_ref, inner_ref, b1_ref, acc_ref, b0_ref, whole_ref, tall_ref = rest[4:]
    sums_ref[...] = jnp.zeros_like(sums_ref)
    width = gs_ref.shape[1]
    for part in chunks(gs_ref.shape[0], ROWS):
        tail_back(
            part, 0, gs_ref[part, :] + more_ref[part, :].astype(F32), cot_ref[part, :].astype(F32),
            halt_ref, vec_ref, n2_ref, r2_ref, rate_ref, b2_ref, gsec_ref, base_ref, sums_ref,
        )
    hidden_rows = hid_ref.shape[1] // 4
    for z in range(4):
        span = slice(z * hidden_rows, (z + 1) * hidden_rows)
        value = dot(hid_ref[:, span], b2_ref[...], 0, 0) + dot(hid1_ref[:, span], b21_ref[...], 0, 0)
        if fast:
            tall_ref[...] = value.reshape(tall_ref.shape)
            for relative in range(8):
                hid_outs[relative % 2][relative // 2, z] = tall_ref[relative ^ me_ref[0]].astype(BF16)
        else:
            hid_outs[0][span, :] = value
    feed_back(b2_ref, dg_ref, win_ref, whid_ref, inner_ref, b1_ref, acc_ref)
    for cols in chunks(dg_ref.shape[1], BLOCK):
        value = dot(nlow_ref[...], b1_ref[:, cols], 0, 0) + dot(nlow1_ref[...], b11_ref[:, cols], 0, 0)
        whole_ref[...] = value.reshape(whole_ref.shape)
        place(fast, me_ref, whole_ref, in_outs, cols)
    middle_back(gsec_ref, acc_ref, vec_ref, n1_ref, r1_ref, b0_ref, base_ref, sums_ref)
    gctx_ref[...] = dot(b0_ref[...], wo_ref[...], 1, 1).astype(BF16)
    dwo_ref[...] = dot(ctx_ref[...], b0_ref[...], 0, 0) + dot(ctx1_ref[...], b01_ref[...], 0, 0)
    vg_ref[...] = vg1_ref[...]
    for index in range(VECS):
        vg_ref[index : index + 1, :] += jnp.sum(sums_ref[index], axis=0, keepdims=True)


def attend_back_kernel(
    fast, me_ref, base_ref, gctx_ref, q2_ref, k_ref, v_ref, p_ref, ctx_ref, wa_ref,
    rown_ref, roth_ref, rown1_ref, roth1_ref, dqkv1_ref, doth1_ref, dwo_ref, vg_ref,
    gs_ref, goth_ref,
    *rest,
):
    count = 2 if fast else 1
    outs, rest = rest[:count], rest[count:]
    g2_ref, ds_ref, dq2_ref, dqkv_ref, doth_ref, whole_ref, flip_ref, thin_ref = rest
    attend_back(
        gctx_ref, g2_ref, q2_ref, k_ref, v_ref, p_ref, ctx_ref, ds_ref, dq2_ref, dqkv_ref, doth_ref
    )
    inputs_back(dqkv_ref, doth_ref, wa_ref, base_ref, gs_ref, goth_ref)
    width = base_ref.shape[1]
    for index in range(3):
        cols = slice(index * width, (index + 1) * width)
        value = dot(rown_ref[...], dqkv_ref[:, cols], 0, 0) + dot(
            rown1_ref[...], dqkv1_ref[:, cols], 0, 0
        )
        if index:
            other = slice((index - 1) * width, index * width)
            value = (
                value
                + dot(roth_ref[...], doth_ref[:, other], 0, 0)
                + dot(roth1_ref[...], doth1_ref[:, other], 0, 0)
            )
        whole_ref[...] = value.reshape(whole_ref.shape)
        place(fast, me_ref, whole_ref, outs, cols)
    whole_ref[...] = dwo_ref[...].reshape(whole_ref.shape)
    place(fast, me_ref, whole_ref, outs, slice(3 * width, 4 * width))
    flip_ref[...] = jnp.zeros_like(flip_ref)
    flip_ref[0:8, :] = vg_ref[...]
    thin_ref[...] = flip_ref[...].T.reshape(thin_ref.shape)
    place(fast, me_ref, thin_ref, outs, slice(4 * width, 4 * width + LANES))


def assemble_kernel(me_ref, *refs):
    pieces, out_ref = refs[:-1], refs[-1]
    half = out_ref.shape[0] // 2
    spans = (slice(0, 2 * half), slice(0, 2 * half), slice(0, 2 * half), slice(0, half), slice(half, 2 * half))
    for core in range(2):
        for index, bits in enumerate((0, 2, 4, 6, 6)):
            piece = pieces[core * 5 + index]
            out_ref[spans[index], pl.ds(me_ref[0] ^ (bits | core), 1)] = piece[...][:, None]


def add_core_kernel(keep_ref, got_ref, s11a_ref, s11b_ref, s10_ref, s01_ref, s00_ref):
    half = s11a_ref.shape[0]
    for z in range(keep_ref.shape[1]):
        for index, target in ((0, s00_ref), (1, s01_ref), (2, s10_ref)):
            total = keep_ref[index, z].astype(F32) + got_ref[index, z].astype(F32)
            target[z] = total.astype(BF16)
        total = (keep_ref[3, z].astype(F32) + got_ref[3, z].astype(F32)).astype(BF16)
        if z < half:
            s11a_ref[z] = total
        else:
            s11b_ref[z - half] = total


def add_half_kernel(s10_ref, gotx_ref, s01_ref, goty_ref, o10_ref, o01_ref):
    half = gotx_ref.shape[0]
    for z in range(half):
        o10_ref[z] = (s10_ref[z].astype(F32) + gotx_ref[z].astype(F32)).astype(BF16)
        o10_ref[half + z] = s10_ref[half + z]
        o01_ref[z] = s01_ref[z]
        o01_ref[half + z] = (s01_ref[half + z].astype(F32) + goty_ref[z].astype(F32)).astype(BF16)


def add_three_kernel(a_ref, b_ref, c_ref, o_ref):
    for z in range(a_ref.shape[0]):
        o_ref[z] = (a_ref[z].astype(F32) + b_ref[z].astype(F32) + c_ref[z].astype(F32)).astype(BF16)


def add_four_kernel(parts_ref, *outs):
    at = 0
    for out in outs:
        cols = slice(at, at + out.shape[1])
        total = parts_ref[0, :, cols].astype(F32)
        for z in range(1, parts_ref.shape[0]):
            total = total + parts_ref[z, :, cols].astype(F32)
        out[...] = total
        at = at + out.shape[1]


def vm():
    return pl.BlockSpec(memory_space=pltpu.VMEM)


def run(kernel, ins, outs, scratch=(), scalar=False, flops=0, limit=40):
    specs = [vm() for _ in ins]
    if scalar:
        specs[0] = pl.BlockSpec(memory_space=pltpu.SMEM)
    size = sum(v.size * v.dtype.itemsize for v in ins) + sum(
        functools.reduce(lambda a, b: a * b, s, 1) * jnp.dtype(t).itemsize for s, t in outs
    )
    return pl.pallas_call(
        kernel,
        out_shape=[jax.ShapeDtypeStruct(s, t) for s, t in outs],
        in_specs=specs,
        out_specs=[vm() for _ in outs],
        scratch_shapes=[pltpu.VMEM(s, t) for s, t in scratch],
        compiler_params=pltpu.CompilerParams(vmem_limit_bytes=limit * 1024 * 1024),
        cost_estimate=pl.CostEstimate(flops=flops, bytes_accessed=size, transcendentals=0),
    )(*ins)


AXES = ("dp", "head")


class Links:
    def __init__(self, model_rows):
        self.heads = lax.axis_size("head")
        self.pods = lax.axis_size("dp")
        self.count = self.heads * self.pods
        self.fast = self.heads == 4 and self.pods == 8 and model_rows == 16
        self.head = lax.axis_index("head")
        self.me = (lax.axis_index("dp") % 2) * 4 + self.head
        self.me_array = jnp.reshape(self.me, (1,)).astype(jnp.int32)
        self.lines = [[z * 2 + y for z in range(self.pods // 2)] for y in range(2)]

    def flip(self, value, bit):
        return lax.ppermute(value, AXES, [(i, i ^ bit) for i in range(self.count)])

    def flip_head(self, value, bit):
        return lax.ppermute(value, "head", [(i, i ^ bit) for i in range(self.heads)])

    def lines_swap(self, value):
        return lax.all_to_all(
            value, "dp", split_axis=0, concat_axis=0, axis_index_groups=self.lines, tiled=True
        )

    def gather(self, block):
        if not self.fast:
            return lax.all_gather(block, AXES, axis=0, tiled=True)
        rows, cols = block.shape
        own = self.lines_swap(jnp.broadcast_to(block[None], (4, rows, cols)))
        by_x = self.flip(own, 2)
        by_y = self.flip(own, 4)
        far = (self.flip(by_y[:2], 2), self.flip(by_x[2:], 4))
        pieces = [own, by_x, by_y, *far]
        pieces = pieces + [self.flip(piece, 1) for piece in pieces]
        (full,) = run(
            assemble_kernel, [self.me_array, *pieces], [((4, 8, rows, cols), BF16)], scalar=True
        )
        return full.reshape(32 * rows, cols)

    def scatter(self, parts, splits):
        if not self.fast:
            total = lax.psum_scatter(parts[0], AXES, scatter_dimension=0, tiled=True)
            ends = [sum(splits[: i + 1]) for i in range(len(splits))]
            return [total[:, end - size : end] for end, size in zip(ends, splits)]
        keep, send = parts
        rows, cols = keep.shape[2:]
        whole, half = ((4, rows, cols), BF16), ((2, rows, cols), BF16)
        s11a, s11b, s10, s01, s00 = run(
            add_core_kernel, [keep, self.flip(send, 1)], [half, half, whole, whole, whole]
        )
        s10, s01 = run(
            add_half_kernel, [s10, self.flip(s11a, 2), s01, self.flip(s11b, 4)], [whole, whole]
        )
        (s00,) = run(add_three_kernel, [s00, self.flip(s01, 2), self.flip(s10, 4)], [whole])
        return run(add_four_kernel, [self.lines_swap(s00)], [((rows, size), F32) for size in splits])

    def spread(self, own, group):
        held, bit = own[None], 1
        while bit < group:
            got = self.flip_head(held, bit)
            held = got if bit == 1 and group == 2 else jnp.concatenate([held, got], axis=0)
            bit = bit * 2
        if group > 2:
            held = held[1:]
        return held.reshape(-1, own.shape[1])

    def collapse(self, parts, group, rows):
        if group == 2:
            return self.flip_head(parts, 1)
        held = parts.reshape(group - 1, rows, -1)
        held = jnp.concatenate([jnp.zeros_like(held[:1]), held], axis=0).astype(F32)
        bit = group // 2
        while bit >= 1:
            held = held[:bit] + self.flip_head(held[bit : 2 * bit], bit)
            bit = bit // 2
        return held[0]


def body(
    tokens, cotangent, lengths, halting, w_query, w_key, w_value, w_out, w_in, w_hidden,
    w_halt, gain_attn, shift_attn, gain_ffn, shift_ffn,
):
    micro, local, width = tokens.shape
    steps = halting.shape[0]
    links = Links(w_query.shape[0])
    fast, heads = links.fast, links.heads
    group = heads // micro
    rows, length = micro * local, local * heads
    mine = links.head // group
    place_in = links.head % group
    wide_ff = w_in.shape[1]

    vectors = jnp.stack([w_halt, gain_attn, shift_attn, gain_ffn, shift_ffn], axis=1)
    vectors = jnp.pad(vectors, ((0, 0), (0, LANES - VECS)))
    full_a = links.gather(jnp.concatenate([w_query, w_key, w_value, w_out, vectors], axis=1))
    full_in = links.gather(w_in)
    full_hid = links.gather(w_hidden)
    vec = full_a[:, 4 * width : 4 * width + 8].astype(F32).T

    def regroup(both):
        own = lax.dynamic_index_in_dim(both, mine, 0, keepdims=False)
        other = lax.dynamic_index_in_dim(both, 1 - mine, 0, keepdims=False)
        return jnp.concatenate([own, links.flip_head(other, group)], axis=0)

    def ungroup(own):
        back = links.flip_head(own[local:], group)
        return jnp.where(mine == 0, jnp.stack([own[:local], back]), jnp.stack([back, own[:local]]))

    tok = regroup(tokens)
    flags = jnp.transpose(halting, (1, 2, 0)).astype(BF16)
    flags = jnp.pad(flags, ((0, 0), (0, 0), (0, LANES - steps)))
    marks = regroup(jnp.concatenate([cotangent, flags], axis=2))
    cot, halt = marks[:, :width], marks[:, width:]

    sizes = lax.dynamic_index_in_dim(lengths[:, 0], mine, 0, keepdims=False)
    ends = jnp.cumsum(sizes)
    starts = ends - sizes
    peers = mine * group + (place_in ^ jnp.arange(group, dtype=jnp.int32))
    blocks = jnp.stack([peers, peers ^ group], axis=1)
    places = (blocks[:, :, None] * local + jnp.arange(local, dtype=jnp.int32)).reshape(length)
    segment = jnp.sum((places[:, None] >= ends[None, :]).astype(jnp.int32), axis=1)
    own_places = places[:rows]
    begins = jnp.max(jnp.where(starts[None, :] <= own_places[:, None], starts[None, :], 0), axis=1)
    position = (own_places - begins).astype(F32)
    half_width = width // 2
    rates = jnp.exp(
        jnp.arange(half_width, dtype=F32) * (-jnp.log(10000.0) / max(half_width - 1, 1))
    )
    angles = position[:, None] * rates[None, :]
    moving = jnp.concatenate([jnp.sin(angles), jnp.cos(angles)], axis=1)
    steady = [
        jnp.concatenate([jnp.sin(step * rates), jnp.cos(step * rates)])[None, :] for step in (0.0, 1.0)
    ]
    segq, segk = segment[:rows, None], segment[None, :]

    x0 = tok.astype(F32) + (moving + steady[0])
    sig1 = moving + steady[1]
    rown0 = x0.astype(BF16)
    roth0 = links.spread(rown0, group)

    pairs = width // LANES
    row_f, row_b = ((rows, width), F32), ((rows, width), BF16)
    stat = ((rows, LANES), F32)
    others = length - rows
    long_b = ((length, width), BF16)
    q2_t = ((pairs, 2 * rows, LANES), BF16)
    p_t = ((pairs, 2 * rows, length), BF16)
    o_t = ((2 * rows, LANES), F32)
    bias_t = ((rows, length), F32)
    inner_t = ((rows, BLOCK), F32)
    ff_b = ((rows, wide_ff), BF16)
    sums_t = ((VECS, 8, width), F32)
    ds_t = ((2 * rows, length), BF16)
    dqkv_t = ((rows, 3 * width), BF16)
    doth_t = ((others, 2 * width), BF16)
    vg_t = ((8, width), F32)
    attn_flops = 2 * rows * width * (2 * width + 2 * 2 * length) + 4 * length * width * width
    ffn_flops = 4 * rows * width * wide_ff

    q2, k, v, p, ctx, n1, r1, nlow = run(
        attend_kernel,
        [x0, rown0, roth0, full_a, vec, segq, segk],
        [q2_t, long_b, long_b, p_t, row_b, row_f, stat, row_b],
        [row_b, bias_t, o_t, row_f],
        flops=attn_flops,
    )
    hid, dg, n2, r2, rate, state, pooled, x1, rown1 = run(
        ffn_kernel,
        [nlow, n1, tok, sig1, halt, vec, full_in, full_hid],
        [ff_b, ff_b, row_f, stat, stat, row_f, row_f, row_f, row_b],
        [inner_t, row_f],
        flops=ffn_flops,
    )
    roth1 = links.spread(rown1, group)
    out, gs, goth, nlow1, hid1, b11, b21, ctx1, b01, dqkv1, doth1, vg1 = run(
        turn_kernel,
        [x1, rown1, roth1, full_a, full_in, full_hid, vec, segq, segk, state, pooled, cot, halt],
        [row_f, row_f, ((others, width), BF16), row_b, ff_b, ff_b, row_b, row_b, row_b, dqkv_t, doth_t, vg_t],
        [
            row_b, q2_t, long_b, long_b, p_t, bias_t, o_t, row_f, row_f, stat, inner_t, ff_b,
            row_f, stat, stat, row_f, row_f, sums_t, row_b, q2_t, ds_t,
        ],
        flops=3 * (attn_flops + ffn_flops),
        limit=48,
    )
    more = links.collapse(goth, group, rows)
    output = ungroup(out)

    fine = width // links.count if fast else 0
    hid_parts = [((4, 4, 4 * fine, width), BF16)] * 2 if fast else [((wide_ff, width), F32)]
    in_parts = [((4, 4, fine, wide_ff), BF16)] * 2 if fast else [((width, wide_ff), F32)]
    a_cols = 4 * width + LANES
    a_parts = [((4, 4, fine, a_cols), BF16)] * 2 if fast else [((width, a_cols), F32)]
    block_shape = (4, 8, fine, BLOCK) if fast else (width, BLOCK)
    tall_shape = (8, 4 * fine, width) if fast else (8, width)
    full_o = full_a[:, 3 * width : 4 * width]
    got = run(
        functools.partial(ffn_back_kernel, fast),
        [
            links.me_array, gs, more, cot, halt, vec, full_in, full_hid, full_o,
            n2, r2, rate, n1, r1, hid, dg, nlow, ctx,
            nlow1, hid1, b11, b21, ctx1, b01, vg1,
        ],
        [*hid_parts, *in_parts, ((width, width), F32), vg_t, row_f, row_b],
        [
            row_b, row_f, sums_t, inner_t, ff_b, row_f, row_b, (block_shape, F32), (tall_shape, F32),
        ],
        scalar=True,
        flops=2 * ffn_flops,
        limit=48,
    )
    count = len(hid_parts)
    hid_parts, in_parts = got[:count], got[count : 2 * count]
    dwo, vg, base, gctx = got[2 * count :]
    (g_hidden,) = links.scatter(hid_parts, (width,))
    (g_in,) = links.scatter(in_parts, (wide_ff,))
    thin_shape = (4, 8, fine, LANES) if fast else (width, LANES)
    wide_shape = (4, 8, fine, width) if fast else (width, width)
    got = run(
        functools.partial(attend_back_kernel, fast),
        [
            links.me_array, base, gctx, q2, k, v, p, ctx, full_a,
            rown0, roth0, rown1, roth1, dqkv1, doth1, dwo, vg,
        ],
        [row_f, ((others, width), BF16), *a_parts],
        [
            q2_t, ds_t, o_t, dqkv_t, doth_t, (wide_shape, F32), ((LANES, width), F32), (thin_shape, F32),
        ],
        scalar=True,
        flops=2 * attn_flops,
        limit=48,
    )
    g0, goth0 = got[:2]
    g_query, g_key, g_value, g_out, g_vec = links.scatter(got[2:], (width,) * 4 + (LANES,))
    input_grad = ungroup(g0 + links.collapse(goth0, group, rows))
    return (
        output, input_grad, g_query, g_key, g_value, g_out, g_in, g_hidden,
        *[g_vec[:, index] for index in range(VECS)],
    )


def solution(mesh):
    whole = P(("dp", "head"))
    matrix = P(("dp", "head"), None)
    rows = P(None, ("dp", "head"), None)
    return jax.shard_map(
        body,
        mesh=mesh,
        in_specs=(rows, rows, P(None, "dp", None), P(None, None, ("dp", "head")))
        + (matrix,) * 6
        + (whole,) * 5,
        out_specs=(rows, rows) + (matrix,) * 6 + (whole,) * 5,
        check_vma=False,
    )
```

```python
import functools

import jax
import jax.numpy as jnp
from jax import lax
from jax.experimental import pallas as pl
from jax.experimental.pallas import tpu as pltpu
from jax.sharding import PartitionSpec as P

HD = 64
EPSILON = 1e-06
F32 = jnp.float32
BF16 = jnp.bfloat16
LANES = 128
ROWS = 32
ATT_ROWS = 128
BLOCK = 512
VECS = 5
MICRO = 1.15e9
GELU_A = 0.7978845608028654
GELU_B = 0.044715


def dot(a, b, ca=1, cb=0):
    return lax.dot_general(a, b, (((ca,), (cb,)), ((), ())), preferred_element_type=F32)


def chunks(total, size):
    size = min(size, total)
    return [slice(i, i + size) for i in range(0, total, size)]


def wide(column):
    return jnp.broadcast_to(column, (column.shape[0], LANES))


def mean(values):
    return jnp.sum(values, axis=-1, keepdims=True) * (1.0 / values.shape[-1])


def fold(values):
    return jnp.sum(values.reshape(values.shape[0] // 8, 8, values.shape[1]), axis=0)


class Flat:
    def __init__(self, ref):
        self.ref = ref

    def __getitem__(self, index):
        if index is Ellipsis:
            index = (slice(None), slice(None))
        value = self.ref[..., index[1]]
        return value.reshape(-1, value.shape[-1])[index[0]]


def rows_of(part, first_ref, second_ref):
    size = first_ref.shape[0]
    if part.start < size:
        return first_ref[part, :]
    return second_ref[part.start - size : part.stop - size, :]


def matrix(ref, index):
    value = ref[index]
    return value.reshape(-1, value.shape[-1])


def head_mask(rows):
    lane = lax.broadcasted_iota(jnp.int32, (rows, LANES), 1)
    return lane < HD


def normalize(values):
    center = values - mean(values)
    inverse = lax.rsqrt(mean(center * center) + EPSILON)
    return center * inverse, inverse


def normalize_back(unit, inverse, grad):
    return inverse * (grad - mean(grad) - unit * mean(grad * unit))


def split_heads(values_ref, stacked_ref):
    rows = values_ref.shape[0]
    for part in chunks(rows, ATT_ROWS):
        first = head_mask(part.stop - part.start)
        for pair in range(stacked_ref.shape[0]):
            block = values_ref[part, pair * LANES : (pair + 1) * LANES].astype(F32)
            stacked_ref[pair, part, :] = jnp.where(first, block, 0.0).astype(BF16)
            stacked_ref[pair, rows + part.start : rows + part.stop, :] = jnp.where(
                first, 0.0, block
            ).astype(BF16)


def project(rown_ref, roth_ref, wa_ref, q_ref, q2_ref, k_ref, v_ref):
    rows, width = rown_ref.shape
    q_ref[...] = (
        dot(rown_ref[...], matrix(wa_ref, 0)).astype(BF16).astype(F32) * HD**-0.5
    ).astype(BF16)
    split_heads(q_ref, q2_ref)
    for at, source in ((0, rown_ref), (rows, roth_ref)):
        span = slice(at, at + source.shape[0])
        k_ref[span, :] = dot(source[...], matrix(wa_ref, 1)).astype(BF16)
        v_ref[span, :] = dot(source[...], matrix(wa_ref, 2)).astype(BF16)


def set_bias(segq_ref, segk_ref, bias_ref):
    for part in chunks(bias_ref.shape[0], ROWS):
        bias_ref[part, :] = jnp.where(segq_ref[part, 0:1] == segk_ref[0:1, :], 0.0, -1e30)


def attend(q2_ref, k_ref, v_ref, bias_ref, p_ref, ctx_ref, o_ref):
    rows, length = bias_ref.shape
    for pair in range(q2_ref.shape[0]):
        cols = slice(pair * LANES, (pair + 1) * LANES)
        for part in chunks(2 * rows, ATT_ROWS):
            size = part.stop - part.start
            base = part.start % rows
            scores = dot(q2_ref[pair, part, :], k_ref[:, cols], 1, 1)
            scores = scores + bias_ref[base : base + size, :]
            weights = jnp.exp(scores - jnp.max(scores, axis=-1, keepdims=True))
            inverse = 1.0 / jnp.sum(weights, axis=-1, keepdims=True)
            low = (weights * inverse).astype(BF16)
            p_ref[pair, part, :] = low
            o_ref[part, :] = dot(low, v_ref[:, cols])
        for part in chunks(rows, ATT_ROWS):
            first = head_mask(part.stop - part.start)
            second = o_ref[rows + part.start : rows + part.stop, :]
            ctx_ref[part, cols] = jnp.where(first, o_ref[part, :], second).astype(BF16)


def first_norm(x_ref, ctx_ref, wa_ref, vec_ref, acc_ref, n1_ref, r1_ref, nlow_ref):
    acc_ref[...] = dot(ctx_ref[...], matrix(wa_ref, 3))
    for part in chunks(x_ref.shape[0], ROWS):
        unit, inverse = normalize(x_ref[part, :] + acc_ref[part, :])
        n1_ref[part, :] = unit
        r1_ref[part, :] = wide(inverse)
        nlow_ref[part, :] = (unit * vec_ref[1:2, :] + vec_ref[2:3, :]).astype(BF16)


def feed_forward(nlow_ref, win_ref, whid_ref, inner_ref, hid_ref, dg_ref, acc_ref):
    rows = nlow_ref.shape[0]
    for cols in chunks(hid_ref.shape[1], BLOCK):
        inner_ref[...] = dot(nlow_ref[...], matrix(win_ref, cols.start // BLOCK))
        for part in chunks(rows, ROWS):
            x = inner_ref[part, :]
            square = x * x
            t = jnp.tanh(x * (GELU_A + GELU_A * GELU_B * square))
            half = 0.5 + 0.5 * t
            hid_ref[part, cols] = (x * half).astype(BF16)
            slope = 0.5 * x * (1.0 - t * t) * (GELU_A + 3.0 * GELU_A * GELU_B * square)
            dg_ref[part, cols] = (half + slope).astype(BF16)
    acc_ref[...] = dot(hid_ref[...], whid_ref[...])


def second_norm(part, vec_ref, n1_ref, acc_ref):
    normed = n1_ref[part, :] * vec_ref[1:2, :] + vec_ref[2:3, :]
    unit, inverse = normalize(normed + acc_ref[part, :])
    updated = unit * vec_ref[3:4, :] + vec_ref[4:5, :]
    rate = jax.nn.sigmoid(jnp.sum(updated * vec_ref[0:1, :], axis=-1, keepdims=True))
    return unit, inverse, updated, rate


def tail_back(
    part, step, gs, gp, halt_ref, vec_ref, n2_ref, r2_ref, rate_ref, b2_ref, gsec_ref, base_ref, sums_ref
):
    width = n2_ref.shape[1]
    keep = halt_ref[part, width + step : width + step + 1].astype(F32)
    unit = n2_ref[part, :]
    updated = unit * vec_ref[3:4, :] + vec_ref[4:5, :]
    rate = rate_ref[part, 0:1]
    logit = keep * jnp.sum(gp * updated, axis=-1, keepdims=True) * rate * (1.0 - rate)
    grad = keep * gs + (keep * rate) * gp + logit * vec_ref[0:1, :]
    base_ref[part, :] = gs - keep * gs
    sums_ref[0] += fold(logit * updated)
    sums_ref[3] += fold(grad * unit)
    sums_ref[4] += fold(grad)
    back = normalize_back(unit, r2_ref[part, 0:1], grad * vec_ref[3:4, :])
    gsec_ref[part, :] = back
    b2_ref[part, :] = back.astype(BF16)


def feed_back(b2_ref, dg_ref, win_ref, whid_ref, inner_ref, b1_ref, acc_ref):
    rows = b2_ref.shape[0]
    for cols in chunks(dg_ref.shape[1], BLOCK):
        inner_ref[...] = dot(b2_ref[...], whid_ref[cols, :], 1, 1)
        for part in chunks(rows, ROWS):
            b1_ref[part, cols] = (inner_ref[part, :] * dg_ref[part, cols].astype(F32)).astype(BF16)
    total = None
    for cols in chunks(dg_ref.shape[1], BLOCK):
        value = dot(b1_ref[:, cols], matrix(win_ref, cols.start // BLOCK), 1, 1)
        total = value if total is None else total + value
    acc_ref[...] = total


def middle_back(gsec_ref, acc_ref, vec_ref, n1_ref, r1_ref, b0_ref, base_ref, sums_ref):
    for part in chunks(gsec_ref.shape[0], ROWS):
        grad = gsec_ref[part, :] + acc_ref[part, :]
        unit = n1_ref[part, :]
        sums_ref[1] += fold(grad * unit)
        sums_ref[2] += fold(grad)
        back = normalize_back(unit, r1_ref[part, 0:1], grad * vec_ref[1:2, :])
        base_ref[part, :] += back
        b0_ref[part, :] = back.astype(BF16)


def attend_back(
    gctx_ref, g2_ref, q2_ref, k_ref, v_ref, p_ref, ctx_ref, ds_ref, dq2_ref, dqkv_ref, doth_ref
):
    rows, width = gctx_ref.shape
    split_heads(gctx_ref, g2_ref)
    for pair in range(q2_ref.shape[0]):
        cols = slice(pair * LANES, (pair + 1) * LANES)
        for part in chunks(2 * rows, ATT_ROWS):
            size = part.stop - part.start
            base = part.start % rows
            grad = g2_ref[pair, part, :]
            delta = jnp.sum(
                grad.astype(F32) * ctx_ref[base : base + size, cols].astype(F32),
                axis=-1,
                keepdims=True,
            )
            back = dot(grad, v_ref[:, cols], 1, 1)
            low = (p_ref[pair, part, :].astype(F32) * (back - delta)).astype(BF16)
            ds_ref[part, :] = low
            dq2_ref[part, :] = dot(low, k_ref[:, cols])
        for part in chunks(rows, ATT_ROWS):
            first = head_mask(part.stop - part.start)
            second = dq2_ref[rows + part.start : rows + part.stop, :]
            dqkv_ref[part, cols] = (
                jnp.where(first, dq2_ref[part, :], second) * HD**-0.5
            ).astype(BF16)
        for index, (left, right) in enumerate(
            ((ds_ref[...], q2_ref[pair]), (p_ref[pair], g2_ref[pair]))
        ):
            both = dot(left, right, 0, 0).astype(BF16)
            at = index * width + pair * LANES
            dqkv_ref[:, width + at : width + at + LANES] = both[:rows]
            doth_ref[:, at : at + LANES] = both[rows:]


def inputs_back(dqkv_ref, doth_ref, wa_ref, base_ref, gs_ref, goth_ref):
    width = base_ref.shape[1]
    parts = [slice(index * width, (index + 1) * width) for index in range(3)]
    total = base_ref[...]
    for index, cols in enumerate(parts):
        total = total + dot(dqkv_ref[:, cols], matrix(wa_ref, index), 1, 1)
    gs_ref[...] = total
    total = dot(doth_ref[:, parts[0]], matrix(wa_ref, 1), 1, 1)
    goth_ref[...] = (total + dot(doth_ref[:, parts[1]], matrix(wa_ref, 2), 1, 1)).astype(BF16)


def fetch(pieces, targets, me_ref, sems):
    line, place_in = me_ref[0] // 8, me_ref[0] % 8
    count = len(pieces) // 2
    bits = (0, 2, 4, 6, 6)
    copies = []
    for index, piece in enumerate(pieces):
        core, kind = index // count, index % count
        start = 2 if kind == 4 else 0
        for z in range(piece.shape[0]):
            for first, target in targets:
                source = piece.at[z, first]
                place_of = place_in ^ (bits[kind] | core)
                copies.append(
                    pltpu.make_async_copy(
                        source, target(line ^ (start + z), place_of), sems.at[len(copies)]
                    )
                )
    for copy in copies:
        copy.start()
    return copies


def embed_kernel(place_ref, sizes_ref, tok_ref, got_ref, own_ref, x_ref, rown_ref, sig_ref, segq_ref, segk_ref):
    mine, place_in, group = place_ref[0], place_ref[1], place_ref[2]
    local = tok_ref.shape[0]
    half = x_ref.shape[1] // 2
    ends, starts, total = [], [], 0
    for index in range(sizes_ref.shape[1]):
        starts.append(total)
        total = total + sizes_ref[mine, index]
        ends.append(total)
    ones = jnp.exp(
        lax.broadcasted_iota(jnp.int32, (8, half), 1).astype(F32)
        * (-jnp.log(jnp.full((8, half), 10000.0, F32)) / max(half - 1, 1))
    )
    rates = ones[0:1, :]
    first_sin, first_cos = jnp.sin(rates), jnp.cos(rates)
    for part in chunks(x_ref.shape[0], ROWS):
        size = part.stop - part.start
        block = mine * group + place_in
        block = block if part.start < local else block ^ group
        at = block * local + part.start % local
        token = at + lax.broadcasted_iota(jnp.int32, (size, LANES), 0)
        segment = jnp.zeros((size, LANES), jnp.int32)
        begin = jnp.zeros((size, LANES), jnp.int32)
        for start, end in zip(starts, ends):
            segment = segment + jnp.where(token >= end, 1, 0)
            begin = jnp.maximum(begin, jnp.where(token >= start, start, 0))
        segq_ref[part, :] = segment
        angles = (token - begin).astype(F32)[:, 0:1] * rates
        if part.start < local:
            low = tok_ref[part, :]
        else:
            low = got_ref[part.start - local : part.stop - local, :]
        own_ref[part, :] = low
        for cols, moving, still, step in (
            (slice(0, half), jnp.sin(angles), 0.0, first_sin),
            (slice(half, 2 * half), jnp.cos(angles), 1.0, first_cos),
        ):
            inputs = low[:, cols].astype(F32) + (moving + still)
            x_ref[part, cols] = inputs
            rown_ref[part, cols] = inputs.astype(BF16)
            sig_ref[part, cols] = moving + step
    blocks = segk_ref.shape[1] // local
    for index in range(blocks):
        peer = mine * group + (place_in ^ (index // 2))
        peer = peer if index % 2 == 0 else peer ^ group
        token = peer * local + lax.broadcasted_iota(jnp.int32, (8, local), 1)
        segment = jnp.zeros((8, local), jnp.int32)
        for end in ends:
            segment = segment + jnp.where(token >= end, 1, 0)
        segk_ref[:, index * local : (index + 1) * local] = segment


def pull(sources, sems):
    copies = [
        pltpu.make_async_copy(source, target, sems.at[index]) for index, (source, target) in enumerate(sources)
    ]
    for copy in copies:
        copy.start()
    return copies


def sort_rows(place_ref, tok_ref, cot_ref, halt_ref, refs, sems):
    mine = place_ref[0]
    width = tok_ref.shape[2]
    send_ref, own_ref, send_cot_ref, own_cot_ref, flip_ref, flags_ref = refs
    moves = [(halt_ref, flags_ref)]
    for micro, low, cot in ((1 - mine, send_ref, send_cot_ref), (mine, own_ref, own_cot_ref)):
        moves.append((tok_ref.at[micro], low.at[:, :width]))
        moves.append((cot_ref.at[micro], cot))
    copies = pull(moves, sems)
    flip_ref[...] = jnp.zeros_like(flip_ref)
    for copy in copies:
        copy.wait()
    for target, micro in ((own_ref, mine), (send_ref, 1 - mine)):
        for step in range(halt_ref.shape[0]):
            flip_ref[step : step + 1, :] = flags_ref[step, pl.ds(micro, 1), :].astype(F32)
        target[:, width:] = flip_ref[...].T.astype(BF16)


def sort_kernel(place_ref, tok_ref, cot_ref, halt_ref, *refs):
    sort_rows(place_ref, tok_ref, cot_ref, halt_ref, refs[:6], refs[6])


def pack_kernel(place_ref, tok_ref, cot_ref, halt_ref, q_ref, k_ref, v_ref, o_ref, win_ref, whid_ref, *rest):
    vectors, rest = rest[:VECS], rest[VECS:]
    sorted_refs, (block_ref, tall_ref, flip_ref, flags_ref, turn_ref, low_ref, sems) = rest[:4], rest[4:]
    rows, width = q_ref.shape
    moves = [(vector, low_ref.at[index]) for index, vector in enumerate(vectors)]
    for index, source in enumerate((q_ref, k_ref, v_ref, o_ref)):
        moves.append((source, block_ref.at[index]))
    for index in range(4):
        moves.append((win_ref.at[:, index * BLOCK : (index + 1) * BLOCK], tall_ref.at[index]))
        moves.append((whid_ref.at[index * rows : (index + 1) * rows, :], tall_ref.at[4 + index]))
    copies = pull(moves, sems.at[:17])
    sort_rows(place_ref, tok_ref, cot_ref, halt_ref, [*sorted_refs, flip_ref, flags_ref], sems.at[17:])
    turn_ref[...] = jnp.zeros_like(turn_ref)
    for copy in copies:
        copy.wait()
    for index in range(VECS):
        turn_ref[index : index + 1, :rows] = low_ref[index].astype(F32)
    block_ref[4, :, :LANES] = turn_ref[...].T[:rows, :].astype(BF16)
    block_ref[4, :, LANES:] = jnp.zeros((rows, width - LANES), BF16)


def attend_kernel(
    fast, rown_ref, roth_ref, segq_ref, segk_ref, *rest,
):
    if fast:
        me_ref, pieces, rest = rest[0], rest[1:9], rest[9:]
        wa_ref, vec_ref, rest = rest[0], rest[1], rest[2:]
        q2_ref, k_ref, v_ref, p_ref, ctx_ref, q_ref, bias_ref, o_ref, sems = rest
        copies = fetch(pieces, [(slice(0, 5), lambda z, place: wa_ref.at[:, z, place])], me_ref, sems)
    else:
        wa_ref, q2_ref, k_ref, v_ref, p_ref, ctx_ref, q_ref, bias_ref, o_ref = rest
    set_bias(segq_ref, segk_ref, bias_ref)
    if fast:
        for copy in copies:
            copy.wait()
        vec_ref[...] = matrix(wa_ref, 4)[:, :LANES].astype(F32).T[0:8, :]
    project(rown_ref, roth_ref, wa_ref, q_ref, q2_ref, k_ref, v_ref)
    attend(q2_ref, k_ref, v_ref, bias_ref, p_ref, ctx_ref, o_ref)


def ffn_kernel(
    fast, x_ref, ctx_ref, tok_ref, sig_ref, vec_ref, wa_ref, *rest,
):
    if fast:
        me_ref, pieces, rest = rest[0], rest[1:11], rest[11:]
        (win_ref, full_ref), rest = rest[:2], rest[2:]
    else:
        (win_ref, whid_ref), rest = rest[:2], rest[2:]
    (
        n1_ref, r1_ref, nlow_ref, hid_ref, dg_ref, n2_ref, r2_ref, rate_ref, state_ref,
        pooled_ref, next_ref, rown_ref,
    ), rest = rest[:12], rest[12:]
    inner_ref, acc_ref = rest[:2]
    if fast:
        copies = fetch(
            pieces,
            [
                (slice(0, 4), lambda z, place: win_ref.at[:, z, place]),
                (slice(4, 8), lambda z, place: full_ref.at[z, place]),
            ],
            me_ref,
            rest[2],
        )
    width = x_ref.shape[1]
    first_norm(x_ref, ctx_ref, wa_ref, vec_ref, acc_ref, n1_ref, r1_ref, nlow_ref)
    if fast:
        for copy in copies:
            copy.wait()
        whid_ref = Flat(full_ref)
    feed_forward(nlow_ref, win_ref, whid_ref, inner_ref, hid_ref, dg_ref, acc_ref)
    for part in chunks(tok_ref.shape[0], ROWS):
        unit, inverse, updated, rate = second_norm(part, vec_ref, n1_ref, acc_ref)
        keep = tok_ref[part, width : width + 1].astype(F32)
        n2_ref[part, :] = unit
        r2_ref[part, :] = wide(inverse)
        rate_ref[part, :] = wide(rate)
        pooled_ref[part, :] = (keep * rate) * updated
        state = tok_ref[part, :width].astype(F32)
        state = state + keep * (updated - state)
        state_ref[part, :] = state
        inputs = state + sig_ref[part, :]
        next_ref[part, :] = inputs
        rown_ref[part, :] = inputs.astype(BF16)


def turn_kernel(
    x_ref, rown_ref, roth_ref, wa_ref, win_ref, whid_ref, vec_ref, segq_ref, segk_ref,
    state_ref, pooled_ref, tok_ref, own_cot_ref, got_cot_ref,
    out_ref, gs_ref, goth_ref, nlow_ref, hid_ref, b1_ref, b2_ref, ctx_ref, b0_ref, dqkv_ref, doth_ref, vg_ref,
    q_ref, q2_ref, k_ref, v_ref, p_ref, bias_ref, o_ref, acc_ref, n1_ref, r1_ref, inner_ref, dg_ref,
    n2_ref, r2_ref, rate_ref, gsec_ref, base_ref, sums_ref, gctx_ref, g2_ref, ds_ref,
):
    width = x_ref.shape[1]
    sums_ref[...] = jnp.zeros_like(sums_ref)
    set_bias(segq_ref, segk_ref, bias_ref)
    project(rown_ref, roth_ref, wa_ref, q_ref, q2_ref, k_ref, v_ref)
    attend(q2_ref, k_ref, v_ref, bias_ref, p_ref, ctx_ref, o_ref)
    first_norm(x_ref, ctx_ref, wa_ref, vec_ref, acc_ref, n1_ref, r1_ref, nlow_ref)
    feed_forward(nlow_ref, win_ref, whid_ref, inner_ref, hid_ref, dg_ref, acc_ref)
    for part in chunks(x_ref.shape[0], ROWS):
        unit, inverse, updated, rate = second_norm(part, vec_ref, n1_ref, acc_ref)
        keep = tok_ref[part, width + 1 : width + 2].astype(F32)
        n2_ref[part, :] = unit
        r2_ref[part, :] = wide(inverse)
        rate_ref[part, :] = wide(rate)
        state = state_ref[part, :]
        state = state + keep * (updated - state)
        out_ref[part, :] = state + (pooled_ref[part, :] + (keep * rate) * updated)
        cot = rows_of(part, own_cot_ref, got_cot_ref).astype(F32)
        tail_back(
            part, 1, cot, cot, tok_ref, vec_ref, n2_ref, r2_ref, rate_ref, b2_ref, gsec_ref, base_ref,
            sums_ref,
        )
    feed_back(b2_ref, dg_ref, win_ref, whid_ref, inner_ref, b1_ref, acc_ref)
    middle_back(gsec_ref, acc_ref, vec_ref, n1_ref, r1_ref, b0_ref, base_ref, sums_ref)
    gctx_ref[...] = dot(b0_ref[...], matrix(wa_ref, 3), 1, 1).astype(BF16)
    attend_back(
        gctx_ref, g2_ref, q2_ref, k_ref, v_ref, p_ref, ctx_ref, ds_ref, o_ref, dqkv_ref, doth_ref
    )
    inputs_back(dqkv_ref, doth_ref, wa_ref, base_ref, gs_ref, goth_ref)
    vg_ref[...] = jnp.zeros_like(vg_ref)
    for index in range(VECS):
        vg_ref[index : index + 1, :] = jnp.sum(sums_ref[index], axis=0, keepdims=True)


def place(fast, me_ref, value, scratch_ref, outs, chunk):
    if not fast:
        outs[0][chunk, :, : value.shape[1]] = value
        return
    cols = value.shape[1]
    scratch_ref[:, :, :, :cols] = value.reshape(scratch_ref.shape[:3] + (cols,))
    for relative in range(8):
        block = scratch_ref[:, relative ^ (me_ref[0] % 8), :, :cols].astype(BF16)
        outs[relative % 2][relative // 2, :, chunk, :, :cols] = block


def ffn_back_kernel(
    fast, me_ref, gs_ref, more_ref, tok_ref, own_cot_ref, got_cot_ref, vec_ref, win_ref, whid_ref, wa_ref,
    n2_ref, r2_ref, rate_ref, n1_ref, r1_ref, hid_ref, dg_ref, nlow_ref, ctx_ref,
    nlow1_ref, hid1_ref, b11_ref, b21_ref, ctx1_ref, b01_ref, vg1_ref,
    *rest,
):
    count = 2 if fast else 1
    outs, rest = rest[:count], rest[count:]
    base_ref, gctx_ref, vg_ref = rest[:3]
    b2_ref, gsec_ref, sums_ref, inner_ref, b1_ref, acc_ref, b0_ref, whole_ref, tall_ref = rest[3:]
    sums_ref[...] = jnp.zeros_like(sums_ref)
    width = gs_ref.shape[1]
    for part in chunks(gs_ref.shape[0], ROWS):
        tail_back(
            part, 0, gs_ref[part, :] + more_ref[part, :].astype(F32),
            rows_of(part, own_cot_ref, got_cot_ref).astype(F32), tok_ref, vec_ref, n2_ref, r2_ref, rate_ref, b2_ref, gsec_ref, base_ref, sums_ref,
        )
    hidden_rows = hid_ref.shape[1] // 4
    for z in range(4):
        span = slice(z * hidden_rows, (z + 1) * hidden_rows)
        value = dot(hid_ref[:, span], b2_ref[...], 0, 0) + dot(hid1_ref[:, span], b21_ref[...], 0, 0)
        if fast:
            tall_ref[...] = value.reshape(tall_ref.shape)
            for relative in range(8):
                block = tall_ref[relative ^ (me_ref[0] % 8)].astype(BF16)
                outs[relative % 2][relative // 2, z, 4:8] = block
        else:
            outs[0][4 + z] = value
    feed_back(b2_ref, dg_ref, win_ref, whid_ref, inner_ref, b1_ref, acc_ref)
    for cols in chunks(dg_ref.shape[1], BLOCK):
        value = dot(nlow_ref[...], b1_ref[:, cols], 0, 0) + dot(nlow1_ref[...], b11_ref[:, cols], 0, 0)
        place(fast, me_ref, value, whole_ref, outs, cols.start // BLOCK)
    middle_back(gsec_ref, acc_ref, vec_ref, n1_ref, r1_ref, b0_ref, base_ref, sums_ref)
    gctx_ref[...] = dot(b0_ref[...], matrix(wa_ref, 3), 1, 1).astype(BF16)
    value = dot(ctx_ref[...], b0_ref[...], 0, 0) + dot(ctx1_ref[...], b01_ref[...], 0, 0)
    place(fast, me_ref, value, whole_ref, outs, 8)
    vg_ref[...] = vg1_ref[...]
    for index in range(VECS):
        vg_ref[index : index + 1, :] += jnp.sum(sums_ref[index], axis=0, keepdims=True)


def attend_back_kernel(
    fast, me_ref, base_ref, gctx_ref, q2_ref, k_ref, v_ref, p_ref, ctx_ref, wa_ref,
    rown_ref, roth_ref, rown1_ref, roth1_ref, dqkv1_ref, doth1_ref, vg_ref,
    gs_ref, goth_ref,
    *rest,
):
    count = 2 if fast else 1
    outs, rest = rest[:count], rest[count:]
    g2_ref, ds_ref, dq2_ref, dqkv_ref, doth_ref, whole_ref, flip_ref = rest
    attend_back(
        gctx_ref, g2_ref, q2_ref, k_ref, v_ref, p_ref, ctx_ref, ds_ref, dq2_ref, dqkv_ref, doth_ref
    )
    inputs_back(dqkv_ref, doth_ref, wa_ref, base_ref, gs_ref, goth_ref)
    width = base_ref.shape[1]
    for index in range(3):
        cols = slice(index * width, (index + 1) * width)
        value = dot(rown_ref[...], dqkv_ref[:, cols], 0, 0) + dot(
            rown1_ref[...], dqkv1_ref[:, cols], 0, 0
        )
        if index:
            other = slice((index - 1) * width, index * width)
            value = (
                value
                + dot(roth_ref[...], doth_ref[:, other], 0, 0)
                + dot(roth1_ref[...], doth1_ref[:, other], 0, 0)
            )
        place(fast, me_ref, value, whole_ref, outs, index)
    flip_ref[...] = jnp.zeros_like(flip_ref)
    flip_ref[0:8, :] = vg_ref[...]
    place(fast, me_ref, flip_ref[...].T, whole_ref, outs, 3)


def add_core_kernel(keep_ref, got_ref, s11a_ref, s11b_ref, s10_ref, s01_ref, s00_ref):
    half = s11a_ref.shape[0]
    for z in range(keep_ref.shape[1]):
        for index, target in ((0, s00_ref), (1, s01_ref), (2, s10_ref)):
            total = keep_ref[index, z].astype(F32) + got_ref[index, z].astype(F32)
            target[z] = total.astype(BF16)
        total = (keep_ref[3, z].astype(F32) + got_ref[3, z].astype(F32)).astype(BF16)
        if z < half:
            s11a_ref[z] = total
        else:
            s11b_ref[z - half] = total


def add_half_kernel(s10_ref, gotx_ref, s01_ref, goty_ref, o10_ref, o01_ref):
    half = gotx_ref.shape[0]
    for z in range(half):
        o10_ref[z] = (s10_ref[z].astype(F32) + gotx_ref[z].astype(F32)).astype(BF16)
        o10_ref[half + z] = s10_ref[half + z]
        o01_ref[z] = s01_ref[z]
        o01_ref[half + z] = (s01_ref[half + z].astype(F32) + goty_ref[z].astype(F32)).astype(BF16)


def add_three_kernel(me_ref, a_ref, b_ref, c_ref, *outs):
    line = me_ref[0] // 8
    for z, out in enumerate(outs):
        at = line ^ z
        out[...] = (a_ref[at].astype(F32) + b_ref[at].astype(F32) + c_ref[at].astype(F32)).astype(BF16)


def total_of(parts, *index):
    total = parts[0][index].astype(F32)
    for part in parts[1:]:
        total = total + part[index].astype(F32)
    return total


def end_ffn_kernel(p0_ref, p1_ref, p2_ref, p3_ref, win_ref, whid_ref, wo_ref):
    parts = (p0_ref, p1_ref, p2_ref, p3_ref)
    rows = wo_ref.shape[0]
    for index in range(4):
        win_ref[:, index * BLOCK : (index + 1) * BLOCK] = total_of(parts, index)
        whid_ref[index * rows : (index + 1) * rows, :] = total_of(parts, 4 + index)
    wo_ref[...] = total_of(parts, 8)


def end_attend_kernel(p0_ref, p1_ref, p2_ref, p3_ref, q_ref, k_ref, v_ref, vec_ref, flip_ref):
    parts = (p0_ref, p1_ref, p2_ref, p3_ref)
    for index, target in enumerate((q_ref, k_ref, v_ref)):
        target[...] = total_of(parts, index)
    rows = q_ref.shape[0]
    flip_ref[...] = jnp.zeros_like(flip_ref)
    flip_ref[:rows, :] = total_of(parts, 3)[:, :LANES]
    vec_ref[...] = flip_ref[...].T[:8, :]


def vm():
    return pl.BlockSpec(memory_space=pltpu.VMEM)


def run(kernel, ins, outs, scratch=(), scalars=(), loose=(), sems=0, micros=1, spare=8):
    specs = [vm() for _ in ins]
    for index in scalars:
        specs[index] = pl.BlockSpec(memory_space=pltpu.SMEM)
    ins = list(ins)
    for index in loose:
        specs[index] = pl.BlockSpec(memory_space=pltpu.HBM)
        ins[index] = pltpu.with_memory_space_constraint(ins[index], pltpu.HBM)
    size = sum(v.size * v.dtype.itemsize for v in ins) + sum(
        functools.reduce(lambda a, b: a * b, s, 1) * jnp.dtype(t).itemsize for s, t in outs
    )
    buffers = [pltpu.VMEM(s, t) for s, t in scratch]
    need = sum(functools.reduce(lambda a, b: a * b, s, 1) * jnp.dtype(t).itemsize for s, t in scratch)
    if sems:
        buffers.append(pltpu.SemaphoreType.DMA((sems,)))
    return pl.pallas_call(
        kernel,
        out_shape=[jax.ShapeDtypeStruct(s, t) for s, t in outs],
        in_specs=specs,
        out_specs=[vm() for _ in outs],
        scratch_shapes=buffers,
        compiler_params=pltpu.CompilerParams(vmem_limit_bytes=need + spare * 1024 * 1024),
        cost_estimate=pl.CostEstimate(
            flops=int(micros * MICRO), bytes_accessed=size, transcendentals=0
        ),
    )(*ins)


AXES = ("dp", "head")


def after(value, *others):
    return lax.optimization_barrier((value, *others))[0]


class Links:
    def __init__(self, model_rows):
        self.heads = lax.axis_size("head")
        self.pods = lax.axis_size("dp")
        self.count = self.heads * self.pods
        self.fast = self.heads == 4 and self.pods == 8 and model_rows == 16
        self.head = lax.axis_index("head")
        self.me = lax.axis_index("dp") * self.heads + self.head
        self.me_array = jnp.reshape(self.me, (1,)).astype(jnp.int32)

    def flip(self, value, bit):
        return lax.ppermute(value, AXES, [(i, i ^ bit) for i in range(self.count)])

    def flip_head(self, value, bit):
        return lax.ppermute(value, "head", [(i, i ^ bit) for i in range(self.heads)])

    def along_z(self, block):
        return [block, *(self.flip(block, 8 * k) for k in (1, 2, 3))]

    def plane(self, own):
        return [own, *(self.flip(own, 2 * k) for k in (1, 2, 3))]

    def far(self, by_x, by_y):
        return [self.flip(by_y[:2], 2), self.flip(by_x[2:], 4)]

    def across(self, own):
        pieces = self.plane(own)
        return pieces + [self.flip(piece, 1) for piece in pieces]

    def scatter(self, parts):
        keep, send = parts
        block = keep.shape[2:]
        whole, half = ((4, *block), BF16), ((2, *block), BF16)
        s11a, s11b, s10, s01, s00 = run(
            add_core_kernel, [keep, self.flip(send, 1)], [half, half, whole, whole, whole]
        )
        s10, s01 = run(
            add_half_kernel, [s10, self.flip(s11a, 2), s01, self.flip(s11b, 4)], [whole, whole]
        )
        parts = run(
            add_three_kernel,
            [self.me_array, s00, self.flip(s01, 2), self.flip(s10, 4)],
            [(block, BF16)] * 4,
            scalars=(0,),
        )
        return [parts[0], *(self.flip(parts[k], 8 * k) for k in (1, 2, 3))]

    def spread(self, own, group):
        held, bit = own[None], 1
        while bit < group:
            got = self.flip_head(held, bit)
            held = got if bit == 1 and group == 2 else jnp.concatenate([held, got], axis=0)
            bit = bit * 2
        if group > 2:
            held = held[1:]
        return held.reshape(-1, own.shape[1])

    def collapse(self, parts, group, rows):
        if group == 2:
            return self.flip_head(parts, 1)
        held = parts.reshape(group - 1, rows, -1)
        held = jnp.concatenate([jnp.zeros_like(held[:1]), held], axis=0).astype(F32)
        bit = group // 2
        while bit >= 1:
            held = held[:bit] + self.flip_head(held[bit : 2 * bit], bit)
            bit = bit // 2
        return held[0]


def body(
    tokens, cotangent, lengths, halting, w_query, w_key, w_value, w_out, w_in, w_hidden,
    w_halt, gain_attn, shift_attn, gain_ffn, shift_ffn,
):
    micro, local, width = tokens.shape
    links = Links(w_query.shape[0])
    fast, heads = links.fast, links.heads
    group = heads // micro
    rows, length = micro * local, local * heads
    mine = links.head // group
    wide_ff = w_in.shape[1]
    fine = width // links.count
    matrices = (w_query, w_key, w_value, w_out, w_in, w_hidden)
    vectors = (w_halt, gain_attn, shift_attn, gain_ffn, shift_ffn)
    place_array = jnp.stack([mine, links.head % group, jnp.int32(group)]).astype(jnp.int32)

    pairs = width // LANES
    row_f, row_b = ((rows, width), F32), ((rows, width), BF16)
    stat = ((rows, LANES), F32)
    others = length - rows
    long_b = ((length, width), BF16)
    q2_t = ((pairs, 2 * rows, LANES), BF16)
    p_t = ((pairs, 2 * rows, length), BF16)
    o_t = ((2 * rows, LANES), F32)
    bias_t = ((rows, length), F32)
    inner_t = ((rows, BLOCK), F32)
    ff_b = ((rows, wide_ff), BF16)
    sums_t = ((VECS, 8, width), F32)
    ds_t = ((2 * rows, length), BF16)
    dqkv_t = ((rows, 3 * width), BF16)
    doth_t = ((others, 2 * width), BF16)
    vg_t = ((8, width), F32)
    segq_t, segk_t = ((rows, LANES), jnp.int32), ((8, length), jnp.int32)

    def ungroup(own):
        back = links.flip_head(own[local:], group)
        return jnp.where(mine == 0, jnp.stack([own[:local], back]), jnp.stack([back, own[:local]]))

    sort_in = [place_array, tokens, cotangent, halting]
    sort_out = [((local, width + LANES), BF16)] * 2 + [((local, width), BF16)] * 2
    sort_tmp = [((LANES, local), F32), (halting.shape, jnp.int32)]
    if fast:
        send_tok, own_tok, send_cot, own_cot, block_a, block_b = run(
            pack_kernel,
            [*sort_in, *matrices, *(vector[None] for vector in vectors)],
            [*sort_out, ((5, fine, BLOCK), BF16), ((8, fine, BLOCK), BF16)],
            [*sort_tmp, ((LANES, LANES), F32), ((VECS, 1, fine), BF16)],
            scalars=(0,),
            loose=range(1, 15),
            sems=22,
        )
        got_tok = links.flip_head(send_tok, group)
        line_a = links.along_z(block_a)
        own_a = after(jnp.stack(line_a), got_tok)
        pieces_a = links.across(own_a)
        own_b = after(jnp.stack(links.along_z(after(block_b, line_a[1]))), *pieces_a[1:4])
        plane_b = [own_b, links.flip(own_b, 2), links.flip(own_b, 4)]
    else:
        send_tok, own_tok, send_cot, own_cot = run(
            sort_kernel, sort_in, sort_out, sort_tmp, scalars=(0,), loose=(1, 2, 3), sems=5
        )
        full = [lax.all_gather(part, AXES, axis=0, tiled=True) for part in matrices]
        full_v = [lax.all_gather(part, AXES, axis=0, tiled=True) for part in vectors]
        full_a = jnp.stack(full[:4])
        full_in = jnp.transpose(full[4].reshape(width, wide_ff // BLOCK, BLOCK), (1, 0, 2))
        full_hid = full[5]
        vec = jnp.pad(jnp.stack(full_v), ((0, 8 - VECS), (0, 0))).astype(F32)

        got_tok = links.flip_head(send_tok, group)
    tok, x0, rown0, sig1, segq, segk = run(
        embed_kernel,
        [place_array, lengths[:, 0], own_tok, got_tok],
        [((rows, width + LANES), BF16), row_f, row_b, row_f, segq_t, segk_t],
        scalars=(0, 1),
    )
    roth0 = links.spread(rown0, group)

    attend_in = [rown0, roth0, segq, segk]
    attend_out = [q2_t, long_b, long_b, p_t, row_b]
    if fast:
        full_a, vec, q2, k, v, p, ctx = run(
            functools.partial(attend_kernel, True),
            [*attend_in, links.me_array, *pieces_a],
            [((5, 4, 8, fine, BLOCK), BF16), vg_t, *attend_out],
            [row_b, bias_t, o_t],
            scalars=(4,),
            loose=range(5, 13),
            sems=32,
            micros=8,
        )
        full_a = full_a.reshape(5, width, BLOCK)
    else:
        q2, k, v, p, ctx = run(
            functools.partial(attend_kernel, False),
            [*attend_in, full_a],
            attend_out,
            [row_b, bias_t, o_t],
            micros=8,
        )
    ffn_out = [row_f, stat, row_b, ff_b, ff_b, row_f, stat, stat, row_f, row_f, row_f, row_b]
    got_cot = links.flip_head(after(send_cot, roth0), group)
    sig1 = after(sig1, got_cot)
    ffn_in = [x0, ctx, tok, sig1, vec, full_a]
    if fast:
        plane_b = plane_b + links.far(after(plane_b[1], ctx), after(plane_b[2], ctx))
        pieces_b = plane_b + [links.flip(piece, 1) for piece in plane_b]
        full_in, full_hid, *got = run(
            functools.partial(ffn_kernel, True),
            [*ffn_in, links.me_array, *pieces_b],
            [((4, 4, 8, fine, BLOCK), BF16), ((4, 8, 4, fine, BLOCK), BF16), *ffn_out],
            [inner_t, row_f],
            scalars=(6,),
            loose=range(7, 17),
            sems=64,
            micros=5.5,
        )
        full_in = full_in.reshape(4, width, BLOCK)
        full_hid = full_hid.reshape(wide_ff, width)
    else:
        got = run(
            functools.partial(ffn_kernel, False),
            [*ffn_in, full_in, full_hid],
            ffn_out,
            [inner_t, row_f],
            micros=5.5,
        )
    n1, r1, nlow, hid, dg, n2, r2, rate, state, pooled, x1, rown1 = got
    roth1 = links.spread(rown1, group)
    out, gs, goth, nlow1, hid1, b11, b21, ctx1, b01, dqkv1, doth1, vg1 = run(
        turn_kernel,
        [x1, rown1, roth1, full_a, full_in, full_hid, vec, segq, segk, state, pooled, tok, own_cot, got_cot],
        [row_f, row_f, ((others, width), BF16), row_b, ff_b, ff_b, row_b, row_b, row_b, dqkv_t, doth_t, vg_t],
        [
            row_b, q2_t, long_b, long_b, p_t, bias_t, o_t, row_f, row_f, stat, inner_t, ff_b,
            row_f, stat, stat, row_f, row_f, sums_t, row_b, q2_t, ds_t,
        ],
        micros=15.7,
    )
    more = links.collapse(goth, group, rows)
    output = ungroup(out)

    ffn_parts = [((4, 4, 9, fine, BLOCK), BF16)] * 2 if fast else [((9, width, BLOCK), F32)]
    attend_parts = [((4, 4, 4, fine, BLOCK), BF16)] * 2 if fast else [((4, width, BLOCK), F32)]
    whole_shape = (4, 8, fine, BLOCK) if fast else (8, LANES)
    tall_shape = (8, 4, fine, width) if fast else (8, LANES)
    got = run(
        functools.partial(ffn_back_kernel, fast),
        [
            links.me_array, gs, more, tok, own_cot, got_cot, vec, full_in, full_hid, full_a,
            n2, r2, rate, n1, r1, hid, dg, nlow, ctx,
            nlow1, hid1, b11, b21, ctx1, b01, vg1,
        ],
        [*ffn_parts, row_f, row_b, vg_t],
        [
            row_b, row_f, sums_t, inner_t, ff_b, row_f, row_b, (whole_shape, F32), (tall_shape, F32),
        ],
        scalars=(0,),
        micros=5,
    )
    ffn_parts, (base, gctx, vg) = got[: len(ffn_parts)], got[len(ffn_parts) :]
    got = run(
        functools.partial(attend_back_kernel, fast),
        [
            links.me_array, base, gctx, q2, k, v, p, ctx, full_a,
            rown0, roth0, rown1, roth1, dqkv1, doth1, vg,
        ],
        [row_f, ((others, width), BF16), *attend_parts],
        [q2_t, ds_t, o_t, dqkv_t, doth_t, (whole_shape, F32), ((LANES, width), F32)],
        scalars=(0,),
        micros=6.3,
    )
    (g0, goth0), attend_parts = got[:2], got[2:]
    input_grad = ungroup(g0 + links.collapse(goth0, group, rows))
    if fast:
        g_in, g_hidden, g_out = run(
            end_ffn_kernel,
            links.scatter(ffn_parts),
            [((fine, wide_ff), F32), ((4 * fine, width), F32), ((fine, width), F32)],
        )
        g_query, g_key, g_value, g_vec = run(
            end_attend_kernel,
            links.scatter(attend_parts),
            [((fine, width), F32)] * 3 + [((8, LANES), F32)],
            [((LANES, LANES), F32)],
        )
        g_vectors = [g_vec[index, :fine] for index in range(VECS)]
    else:
        in_part, hid_part, out_part = ffn_parts[0][:4], ffn_parts[0][4:8], ffn_parts[0][8]
        sums = [
            attend_parts[0][0], attend_parts[0][1], attend_parts[0][2], out_part,
            jnp.transpose(in_part, (1, 0, 2)).reshape(width, wide_ff), hid_part.reshape(wide_ff, width),
            *(attend_parts[0][3, :, index] for index in range(VECS)),
        ]
        sums = [lax.psum_scatter(part, AXES, scatter_dimension=0, tiled=True) for part in sums]
        g_query, g_key, g_value, g_out, g_in, g_hidden, *g_vectors = sums
    return (output, input_grad, g_query, g_key, g_value, g_out, g_in, g_hidden, *g_vectors)


def solution(mesh):
    whole = P(("dp", "head"))
    matrix = P(("dp", "head"), None)
    rows = P(None, ("dp", "head"), None)
    return jax.shard_map(
        body,
        mesh=mesh,
        in_specs=(rows, rows, P(None, "dp", None), P(None, None, ("dp", "head")))
        + (matrix,) * 6
        + (whole,) * 5,
        out_specs=(rows, rows) + (matrix,) * 6 + (whole,) * 5,
        check_vma=False,
    )
```

```python
import functools

import jax
import jax.numpy as jnp
from jax import lax
from jax.experimental import pallas as pl
from jax.experimental.pallas import tpu as pltpu
from jax.sharding import PartitionSpec as P

HD = 64
EPSILON = 1e-06
F32 = jnp.float32
BF16 = jnp.bfloat16
LANES = 128
ROWS = 32
ATT_ROWS = 128
BLOCK = 512
VECS = 5
MIB = 1024 * 1024
SCOPED = 20 * MIB
MICRO = 1.15e9
GELU_A = 0.7978845608028654
GELU_B = 0.044715


def dot(a, b, ca=1, cb=0):
    return lax.dot_general(a, b, (((ca,), (cb,)), ((), ())), preferred_element_type=F32)


def chunks(total, size):
    size = min(size, total)
    return [slice(i, i + size) for i in range(0, total, size)]


def wide(column):
    return jnp.broadcast_to(column, (column.shape[0], LANES))


def mean(values):
    return jnp.sum(values, axis=-1, keepdims=True) * (1.0 / values.shape[-1])


def fold(values):
    return jnp.sum(values.reshape(values.shape[0] // 8, 8, values.shape[1]), axis=0)


class Flat:
    def __init__(self, ref):
        self.ref = ref

    def __getitem__(self, index):
        if index is Ellipsis:
            index = (slice(None), slice(None))
        value = self.ref[..., index[1]]
        return value.reshape(-1, value.shape[-1])[index[0]]


def matrix(ref, index):
    value = ref[index]
    return value.reshape(-1, value.shape[-1])


def head_mask(rows):
    lane = lax.broadcasted_iota(jnp.int32, (rows, LANES), 1)
    return lane < HD


def normalize(values):
    center = values - mean(values)
    inverse = lax.rsqrt(mean(center * center) + EPSILON)
    return center * inverse, inverse


def normalize_back(unit, inverse, grad):
    return inverse * (grad - mean(grad) - unit * mean(grad * unit))


def split_heads(values_ref, stacked_ref):
    rows = values_ref.shape[0]
    for part in chunks(rows, ATT_ROWS):
        first = head_mask(part.stop - part.start)
        for pair in range(stacked_ref.shape[0]):
            block = values_ref[part, pair * LANES : (pair + 1) * LANES].astype(F32)
            stacked_ref[pair, part, :] = jnp.where(first, block, 0.0).astype(BF16)
            stacked_ref[pair, rows + part.start : rows + part.stop, :] = jnp.where(
                first, 0.0, block
            ).astype(BF16)


def project(rown_ref, roth_ref, wa_ref, q_ref, q2_ref, k_ref, v_ref):
    rows, width = rown_ref.shape
    q_ref[...] = (
        dot(rown_ref[...], matrix(wa_ref, 0)).astype(BF16).astype(F32) * HD**-0.5
    ).astype(BF16)
    split_heads(q_ref, q2_ref)
    for at, source in ((0, rown_ref), (rows, roth_ref)):
        span = slice(at, at + source.shape[0])
        k_ref[span, :] = dot(source[...], matrix(wa_ref, 1)).astype(BF16)
        v_ref[span, :] = dot(source[...], matrix(wa_ref, 2)).astype(BF16)


def set_bias(segq_ref, segk_ref, bias_ref):
    for part in chunks(bias_ref.shape[0], ROWS):
        bias_ref[part, :] = jnp.where(segq_ref[part, 0:1] == segk_ref[0:1, :], 0.0, -1e30)


def attend(q2_ref, k_ref, v_ref, bias_ref, p_ref, ctx_ref, o_ref):
    rows, length = bias_ref.shape
    for pair in range(q2_ref.shape[0]):
        cols = slice(pair * LANES, (pair + 1) * LANES)
        for part in chunks(2 * rows, ATT_ROWS):
            size = part.stop - part.start
            base = part.start % rows
            scores = dot(q2_ref[pair, part, :], k_ref[:, cols], 1, 1)
            scores = scores + bias_ref[base : base + size, :]
            weights = jnp.exp(scores - jnp.max(scores, axis=-1, keepdims=True))
            inverse = 1.0 / jnp.sum(weights, axis=-1, keepdims=True)
            low = (weights * inverse).astype(BF16)
            p_ref[pair, part, :] = low
            o_ref[part, :] = dot(low, v_ref[:, cols])
        for part in chunks(rows, ATT_ROWS):
            first = head_mask(part.stop - part.start)
            second = o_ref[rows + part.start : rows + part.stop, :]
            ctx_ref[part, cols] = jnp.where(first, o_ref[part, :], second).astype(BF16)


def first_norm(x_ref, ctx_ref, wa_ref, vec_ref, acc_ref, n1_ref, r1_ref, nlow_ref):
    acc_ref[...] = dot(ctx_ref[...], matrix(wa_ref, 3))
    for part in chunks(x_ref.shape[0], ROWS):
        unit, inverse = normalize(x_ref[part, :] + acc_ref[part, :])
        n1_ref[part, :] = unit
        r1_ref[part, :] = wide(inverse)
        nlow_ref[part, :] = (unit * vec_ref[1:2, :] + vec_ref[2:3, :]).astype(BF16)


def feed_forward(nlow_ref, win_ref, whid_ref, inner_ref, hid_ref, dg_ref, acc_ref):
    rows = nlow_ref.shape[0]
    for cols in chunks(hid_ref.shape[1], BLOCK):
        inner_ref[...] = dot(nlow_ref[...], matrix(win_ref, cols.start // BLOCK))
        for part in chunks(rows, ROWS):
            x = inner_ref[part, :]
            square = x * x
            t = jnp.tanh(x * (GELU_A + GELU_A * GELU_B * square))
            half = 0.5 + 0.5 * t
            hid_ref[part, cols] = (x * half).astype(BF16)
            slope = 0.5 * x * (1.0 - t * t) * (GELU_A + 3.0 * GELU_A * GELU_B * square)
            dg_ref[part, cols] = (half + slope).astype(BF16)
    acc_ref[...] = dot(hid_ref[...], whid_ref[...])


def second_norm(part, vec_ref, n1_ref, acc_ref):
    normed = n1_ref[part, :] * vec_ref[1:2, :] + vec_ref[2:3, :]
    unit, inverse = normalize(normed + acc_ref[part, :])
    updated = unit * vec_ref[3:4, :] + vec_ref[4:5, :]
    rate = jax.nn.sigmoid(jnp.sum(updated * vec_ref[0:1, :], axis=-1, keepdims=True))
    return unit, inverse, updated, rate


def tail_back(
    part, step, gs, gp, halt_ref, vec_ref, n2_ref, r2_ref, rate_ref, b2_ref, gsec_ref, base_ref, sums_ref
):
    width = n2_ref.shape[1]
    keep = halt_ref[part, 2 * width + step : 2 * width + step + 1].astype(F32)
    unit = n2_ref[part, :]
    updated = unit * vec_ref[3:4, :] + vec_ref[4:5, :]
    rate = rate_ref[part, 0:1]
    logit = keep * jnp.sum(gp * updated, axis=-1, keepdims=True) * rate * (1.0 - rate)
    grad = keep * gs + (keep * rate) * gp + logit * vec_ref[0:1, :]
    base_ref[part, :] = gs - keep * gs
    sums_ref[0] += fold(logit * updated)
    sums_ref[3] += fold(grad * unit)
    sums_ref[4] += fold(grad)
    back = normalize_back(unit, r2_ref[part, 0:1], grad * vec_ref[3:4, :])
    gsec_ref[part, :] = back
    b2_ref[part, :] = back.astype(BF16)


def feed_back(b2_ref, dg_ref, win_ref, whid_ref, inner_ref, b1_ref, acc_ref):
    rows = b2_ref.shape[0]
    for cols in chunks(dg_ref.shape[1], BLOCK):
        inner_ref[...] = dot(b2_ref[...], whid_ref[cols, :], 1, 1)
        for part in chunks(rows, ROWS):
            b1_ref[part, cols] = (inner_ref[part, :] * dg_ref[part, cols].astype(F32)).astype(BF16)
    total = None
    for cols in chunks(dg_ref.shape[1], BLOCK):
        value = dot(b1_ref[:, cols], matrix(win_ref, cols.start // BLOCK), 1, 1)
        total = value if total is None else total + value
    acc_ref[...] = total


def middle_back(gsec_ref, acc_ref, vec_ref, n1_ref, r1_ref, b0_ref, base_ref, sums_ref):
    for part in chunks(gsec_ref.shape[0], ROWS):
        grad = gsec_ref[part, :] + acc_ref[part, :]
        unit = n1_ref[part, :]
        sums_ref[1] += fold(grad * unit)
        sums_ref[2] += fold(grad)
        back = normalize_back(unit, r1_ref[part, 0:1], grad * vec_ref[1:2, :])
        base_ref[part, :] += back
        b0_ref[part, :] = back.astype(BF16)


def attend_back(
    pairs, g2_ref, q2_ref, k_ref, v_ref, p_ref, ctx_ref, ds_ref, dq2_ref, dqkv_ref, doth_ref
):
    rows, width = ctx_ref.shape
    for pair in pairs:
        cols = slice(pair * LANES, (pair + 1) * LANES)
        for part in chunks(2 * rows, ATT_ROWS):
            size = part.stop - part.start
            base = part.start % rows
            grad = g2_ref[pair, part, :]
            delta = jnp.sum(
                grad.astype(F32) * ctx_ref[base : base + size, cols].astype(F32),
                axis=-1,
                keepdims=True,
            )
            back = dot(grad, v_ref[:, cols], 1, 1)
            low = (p_ref[pair, part, :].astype(F32) * (back - delta)).astype(BF16)
            ds_ref[part, :] = low
            dq2_ref[part, :] = dot(low, k_ref[:, cols])
        for part in chunks(rows, ATT_ROWS):
            first = head_mask(part.stop - part.start)
            second = dq2_ref[rows + part.start : rows + part.stop, :]
            dqkv_ref[part, cols] = (
                jnp.where(first, dq2_ref[part, :], second) * HD**-0.5
            ).astype(BF16)
        for index, (left, right) in enumerate(
            ((ds_ref[...], q2_ref[pair]), (p_ref[pair], g2_ref[pair]))
        ):
            both = dot(left, right, 0, 0).astype(BF16)
            at = index * width + pair * LANES
            dqkv_ref[:, width + at : width + at + LANES] = both[:rows]
            doth_ref[:, at : at + LANES] = both[rows:]


def inputs_back(dqkv_ref, doth_ref, wa_ref, base_ref, gs_ref, goth_ref):
    width = base_ref.shape[1]
    parts = [slice(index * width, (index + 1) * width) for index in range(3)]
    total = base_ref[...]
    for index, cols in enumerate(parts):
        total = total + dot(dqkv_ref[:, cols], matrix(wa_ref, index), 1, 1)
    gs_ref[...] = total
    total = dot(doth_ref[:, parts[0]], matrix(wa_ref, 1), 1, 1)
    goth_ref[...] = (total + dot(doth_ref[:, parts[1]], matrix(wa_ref, 2), 1, 1)).astype(BF16)


def fetch(pieces, cores, bits, start, store, me_ref):
    line, place_in = me_ref[0] // 8, me_ref[0] % 8
    for piece, core, bit in zip(pieces, cores, bits):
        for z in range(piece.shape[0]):
            store(piece, z, line ^ (start + z), place_in ^ (bit | core))


def embed_kernel(place_ref, sizes_ref, tok_ref, got_ref, own_ref, x_ref, rown_ref, sig_ref, segq_ref, segk_ref):
    mine, place_in, group = place_ref[1], place_ref[2], place_ref[3]
    local = tok_ref.shape[0]
    half = x_ref.shape[1] // 2
    ends, starts, total = [], [], 0
    for index in range(sizes_ref.shape[1]):
        starts.append(total)
        total = total + sizes_ref[mine, index]
        ends.append(total)
    ones = jnp.exp(
        lax.broadcasted_iota(jnp.int32, (8, half), 1).astype(F32)
        * (-jnp.log(jnp.full((8, half), 10000.0, F32)) / max(half - 1, 1))
    )
    rates = ones[0:1, :]
    first_sin, first_cos = jnp.sin(rates), jnp.cos(rates)
    for part in chunks(x_ref.shape[0], ROWS):
        size = part.stop - part.start
        block = mine * group + place_in
        block = block if part.start < local else block ^ group
        at = block * local + part.start % local
        token = at + lax.broadcasted_iota(jnp.int32, (size, LANES), 0)
        segment = jnp.zeros((size, LANES), jnp.int32)
        begin = jnp.zeros((size, LANES), jnp.int32)
        for start, end in zip(starts, ends):
            segment = segment + jnp.where(token >= end, 1, 0)
            begin = jnp.maximum(begin, jnp.where(token >= start, start, 0))
        segq_ref[part, :] = segment
        angles = (token - begin).astype(F32)[:, 0:1] * rates
        if part.start < local:
            low = tok_ref[part, :]
        else:
            low = got_ref[part.start - local : part.stop - local, :]
        own_ref[part, :] = low
        for cols, moving, still, step in (
            (slice(0, half), jnp.sin(angles), 0.0, first_sin),
            (slice(half, 2 * half), jnp.cos(angles), 1.0, first_cos),
        ):
            inputs = low[:, cols].astype(F32) + (moving + still)
            x_ref[part, cols] = inputs
            rown_ref[part, cols] = inputs.astype(BF16)
            sig_ref[part, cols] = moving + step
    blocks = segk_ref.shape[1] // local
    for index in range(blocks):
        peer = mine * group + (place_in ^ (index // 2))
        peer = peer if index % 2 == 0 else peer ^ group
        token = peer * local + lax.broadcasted_iota(jnp.int32, (8, local), 1)
        segment = jnp.zeros((8, local), jnp.int32)
        for end in ends:
            segment = segment + jnp.where(token >= end, 1, 0)
        segk_ref[:, index * local : (index + 1) * local] = segment


def pull(sources, sems):
    copies = [
        pltpu.make_async_copy(source, target, sems.at[index]) for index, (source, target) in enumerate(sources)
    ]
    for copy in copies:
        copy.start()
    return copies


def sort_rows(place_ref, tok_ref, cot_ref, halt_ref, refs, sems):
    mine = place_ref[1]
    width = tok_ref.shape[2]
    send_ref, own_ref, flip_ref, flags_ref = refs
    moves = [(halt_ref, flags_ref)]
    for micro, target in ((1 - mine, send_ref), (mine, own_ref)):
        moves.append((tok_ref.at[micro], target.at[:, :width]))
        moves.append((cot_ref.at[micro], target.at[:, width : 2 * width]))
    copies = pull(moves, sems)
    flip_ref[...] = jnp.zeros_like(flip_ref)
    for copy in copies:
        copy.wait()
    for target, micro in ((own_ref, mine), (send_ref, 1 - mine)):
        for step in range(halt_ref.shape[0]):
            flip_ref[step : step + 1, :] = flags_ref[step, pl.ds(micro, 1), :].astype(F32)
        target[:, 2 * width :] = flip_ref[...].T.astype(BF16)


def sort_kernel(place_ref, tok_ref, cot_ref, halt_ref, *refs):
    sort_rows(place_ref, tok_ref, cot_ref, halt_ref, refs[:4], refs[4])


def pack_kernel(place_ref, tok_ref, cot_ref, halt_ref, q_ref, k_ref, v_ref, o_ref, win_ref, whid_ref, *rest):
    vectors, rest = rest[:VECS], rest[VECS:]
    sorted_refs, (block_ref, tall_ref, flip_ref, flags_ref, turn_ref, low_ref, sems) = rest[:2], rest[2:]
    rows, width = q_ref.shape
    moves = [(vector, low_ref.at[index]) for index, vector in enumerate(vectors)]
    for index, source in enumerate((q_ref, k_ref, v_ref, o_ref)):
        moves.append((source, block_ref.at[index]))
    for index in range(4):
        moves.append((win_ref.at[:, index * BLOCK : (index + 1) * BLOCK], tall_ref.at[index]))
        moves.append((whid_ref.at[index * rows : (index + 1) * rows, :], tall_ref.at[4 + index]))
    copies = pull(moves, sems.at[:17])
    sort_rows(place_ref, tok_ref, cot_ref, halt_ref, [*sorted_refs, flip_ref, flags_ref], sems.at[17:])
    turn_ref[...] = jnp.zeros_like(turn_ref)
    for copy in copies:
        copy.wait()
    for index in range(VECS):
        turn_ref[index : index + 1, :rows] = low_ref[index].astype(F32)
    block_ref[4, :, :LANES] = turn_ref[...].T[:rows, :].astype(BF16)
    block_ref[4, :, LANES:] = jnp.zeros((rows, width - LANES), BF16)


def attend_kernel(
    fast, rown_ref, roth_ref, segq_ref, segk_ref, *rest,
):
    if fast:
        me_ref, plane, rest = rest[0], rest[1:9], rest[9:]
        wa_ref, vec_ref, q2_ref, k_ref, v_ref, p_ref, ctx_ref, q_ref, bias_ref, o_ref = rest

        def store(piece, z, line, place):
            for chunk in range(5):
                wa_ref[chunk, line, place] = piece[z, chunk]

        fetch(plane, (0, 0, 0, 0, 1, 1, 1, 1), (0, 2, 4, 6) * 2, 0, store, me_ref)
        vec_ref[...] = matrix(wa_ref, 4)[:, :LANES].astype(F32).T[0:8, :]
    else:
        wa_ref, q2_ref, k_ref, v_ref, p_ref, ctx_ref, q_ref, bias_ref, o_ref = rest
    set_bias(segq_ref, segk_ref, bias_ref)
    project(rown_ref, roth_ref, wa_ref, q_ref, q2_ref, k_ref, v_ref)
    attend(q2_ref, k_ref, v_ref, bias_ref, p_ref, ctx_ref, o_ref)


def ffn_kernel(
    fast, x_ref, ctx_ref, tok_ref, sig_ref, vec_ref, wa_ref, *rest,
):
    if fast:
        me_ref, near, far, rest = rest[0], rest[1:7], rest[7:11], rest[11:]
        (win_ref, full_ref), rest = rest[:2], rest[2:]
    else:
        (win_ref, whid_ref), rest = rest[:2], rest[2:]
    (
        n1_ref, r1_ref, nlow_ref, hid_ref, dg_ref, n2_ref, r2_ref, rate_ref, state_ref,
        pooled_ref, next_ref, rown_ref, inner_ref, acc_ref,
    ) = rest
    if fast:

        def store(piece, z, line, place):
            for chunk in range(4):
                win_ref[chunk, line, place] = piece[z, chunk]
                full_ref[line, place, chunk] = piece[z, 4 + chunk]

        fetch(near, (0, 0, 0, 1, 1, 1), (0, 2, 4, 0, 2, 4), 0, store, me_ref)
        fetch((far[0], far[2]), (0, 1), (6, 6), 0, store, me_ref)
        fetch((far[1], far[3]), (0, 1), (6, 6), 2, store, me_ref)
        whid_ref = Flat(full_ref)
    width = x_ref.shape[1]
    first_norm(x_ref, ctx_ref, wa_ref, vec_ref, acc_ref, n1_ref, r1_ref, nlow_ref)
    feed_forward(nlow_ref, win_ref, whid_ref, inner_ref, hid_ref, dg_ref, acc_ref)
    for part in chunks(tok_ref.shape[0], ROWS):
        unit, inverse, updated, rate = second_norm(part, vec_ref, n1_ref, acc_ref)
        keep = tok_ref[part, 2 * width : 2 * width + 1].astype(F32)
        n2_ref[part, :] = unit
        r2_ref[part, :] = wide(inverse)
        rate_ref[part, :] = wide(rate)
        pooled_ref[part, :] = (keep * rate) * updated
        state = tok_ref[part, :width].astype(F32)
        state = state + keep * (updated - state)
        state_ref[part, :] = state
        inputs = state + sig_ref[part, :]
        next_ref[part, :] = inputs
        rown_ref[part, :] = inputs.astype(BF16)


def turn_kernel(
    x_ref, rown_ref, roth_ref, wa_ref, win_ref, whid_ref, vec_ref, segq_ref, segk_ref,
    state_ref, pooled_ref, tok_ref,
    out_ref, gs_ref, goth_ref, nlow_ref, hid_ref, b1_ref, b2_ref, ctx_ref, b0_ref, dqkv_ref, doth_ref, vg_ref,
    q_ref, q2_ref, k_ref, v_ref, p_ref, bias_ref, o_ref, acc_ref, n1_ref, r1_ref, inner_ref, dg_ref,
    n2_ref, r2_ref, rate_ref, gsec_ref, base_ref, sums_ref, gctx_ref, g2_ref, ds_ref,
):
    width = x_ref.shape[1]
    sums_ref[...] = jnp.zeros_like(sums_ref)
    set_bias(segq_ref, segk_ref, bias_ref)
    project(rown_ref, roth_ref, wa_ref, q_ref, q2_ref, k_ref, v_ref)
    attend(q2_ref, k_ref, v_ref, bias_ref, p_ref, ctx_ref, o_ref)
    first_norm(x_ref, ctx_ref, wa_ref, vec_ref, acc_ref, n1_ref, r1_ref, nlow_ref)
    feed_forward(nlow_ref, win_ref, whid_ref, inner_ref, hid_ref, dg_ref, acc_ref)
    for part in chunks(x_ref.shape[0], ROWS):
        unit, inverse, updated, rate = second_norm(part, vec_ref, n1_ref, acc_ref)
        keep = tok_ref[part, 2 * width + 1 : 2 * width + 2].astype(F32)
        n2_ref[part, :] = unit
        r2_ref[part, :] = wide(inverse)
        rate_ref[part, :] = wide(rate)
        state = state_ref[part, :]
        state = state + keep * (updated - state)
        out_ref[part, :] = state + (pooled_ref[part, :] + (keep * rate) * updated)
        cot = tok_ref[part, width : 2 * width].astype(F32)
        tail_back(
            part, 1, cot, cot, tok_ref, vec_ref, n2_ref, r2_ref, rate_ref, b2_ref, gsec_ref, base_ref,
            sums_ref,
        )
    feed_back(b2_ref, dg_ref, win_ref, whid_ref, inner_ref, b1_ref, acc_ref)
    middle_back(gsec_ref, acc_ref, vec_ref, n1_ref, r1_ref, b0_ref, base_ref, sums_ref)
    gctx_ref[...] = dot(b0_ref[...], matrix(wa_ref, 3), 1, 1).astype(BF16)
    split_heads(gctx_ref, g2_ref)
    pairs = range(q2_ref.shape[0])
    attend_back(pairs, g2_ref, q2_ref, k_ref, v_ref, p_ref, ctx_ref, ds_ref, o_ref, dqkv_ref, doth_ref)
    inputs_back(dqkv_ref, doth_ref, wa_ref, base_ref, gs_ref, goth_ref)
    vg_ref[...] = jnp.zeros_like(vg_ref)
    for index in range(VECS):
        vg_ref[index : index + 1, :] = jnp.sum(sums_ref[index], axis=0, keepdims=True)


def place(fast, me_ref, value, scratch_ref, outs, at):
    cols = slice(at, at + value.shape[1])
    if not fast:
        outs[0][:, cols] = value
        return
    scratch_ref[:, :, :, : value.shape[1]] = value.reshape(scratch_ref.shape[:3] + value.shape[1:])
    for relative in range(8):
        block = scratch_ref[:, relative ^ (me_ref[0] % 8), :, : value.shape[1]].astype(BF16)
        outs[relative % 2][relative // 2, :, :, cols] = block


def hidden_back_kernel(
    fast, me_ref, gs_ref, more_ref, tok_ref, vec_ref,
    n2_ref, r2_ref, rate_ref, hid_ref, hid1_ref, b21_ref,
    b2_ref, gsec_ref, base_ref, sums_ref,
    *rest,
):
    outs, tall_ref = rest[:-1], rest[-1]
    sums_ref[...] = jnp.zeros_like(sums_ref)
    width = gs_ref.shape[1]
    for part in chunks(gs_ref.shape[0], ROWS):
        tail_back(
            part, 0, gs_ref[part, :] + more_ref[part, :].astype(F32),
            tok_ref[part, width : 2 * width].astype(F32), tok_ref, vec_ref,
            n2_ref, r2_ref, rate_ref, b2_ref, gsec_ref, base_ref, sums_ref,
        )
    hidden_rows = hid_ref.shape[1] // 4
    for z in range(4):
        span = slice(z * hidden_rows, (z + 1) * hidden_rows)
        value = dot(hid_ref[:, span], b2_ref[...], 0, 0) + dot(hid1_ref[:, span], b21_ref[...], 0, 0)
        if fast:
            tall_ref[...] = value.reshape(tall_ref.shape)
            for relative in range(8):
                block = tall_ref[relative ^ (me_ref[0] % 8)].astype(BF16)
                outs[relative % 2][relative // 2, z] = block
        else:
            outs[0][span, :] = value


def feed_back_kernel(
    b2_ref, gsec_ref, base0_ref, sums0_ref, vec_ref, win_ref, whid_ref, wa_ref, n1_ref, r1_ref, dg_ref,
    b1_ref, b0_ref, base_ref, gctx_ref, sums_ref, inner_ref, acc_ref,
):
    sums_ref[...] = sums0_ref[...]
    base_ref[...] = base0_ref[...]
    feed_back(b2_ref, dg_ref, win_ref, whid_ref, inner_ref, b1_ref, acc_ref)
    middle_back(gsec_ref, acc_ref, vec_ref, n1_ref, r1_ref, b0_ref, base_ref, sums_ref)
    gctx_ref[...] = dot(b0_ref[...], matrix(wa_ref, 3), 1, 1).astype(BF16)


def weights_back_kernel(
    fast, me_ref, b1_ref, b0_ref, sums_ref, nlow_ref, ctx_ref, nlow1_ref, b11_ref, ctx1_ref, b01_ref, vg1_ref,
    *rest,
):
    outs, (whole_ref, flip_ref) = rest[:-2], rest[-2:]
    width = ctx_ref.shape[1]
    for cols in chunks(b1_ref.shape[1], BLOCK):
        value = dot(nlow_ref[...], b1_ref[:, cols], 0, 0) + dot(nlow1_ref[...], b11_ref[:, cols], 0, 0)
        place(fast, me_ref, value, whole_ref, outs, cols.start)
    value = dot(ctx_ref[...], b0_ref[...], 0, 0) + dot(ctx1_ref[...], b01_ref[...], 0, 0)
    at = b1_ref.shape[1]
    place(fast, me_ref, value, whole_ref, outs, at)
    flip_ref[...] = jnp.zeros_like(flip_ref)
    flip_ref[0:8, :] = vg1_ref[...]
    for index in range(VECS):
        flip_ref[index : index + 1, :] += jnp.sum(sums_ref[index], axis=0, keepdims=True)
    place(fast, me_ref, flip_ref[...].T, whole_ref, outs, at + width)


def first_heads_kernel(
    gctx_ref, q2_ref, k_ref, v_ref, p_ref, ctx_ref, dqkv_ref, doth_ref, g2_ref, ds_ref, dq2_ref
):
    split_heads(gctx_ref, g2_ref)
    pairs = range(q2_ref.shape[0] // 2)
    attend_back(pairs, g2_ref, q2_ref, k_ref, v_ref, p_ref, ctx_ref, ds_ref, dq2_ref, dqkv_ref, doth_ref)


def last_heads_kernel(
    fast, me_ref, base_ref, gctx_ref, q2_ref, k_ref, v_ref, p_ref, ctx_ref, wa_ref,
    rown_ref, roth_ref, rown1_ref, roth1_ref, dqkv1_ref, doth1_ref, dqkv0_ref, doth0_ref,
    gs_ref, goth_ref,
    *rest,
):
    count = 2 if fast else 1
    outs, rest = rest[:count], rest[count:]
    g2_ref, ds_ref, dq2_ref, dqkv_ref, doth_ref, whole_ref = rest
    split_heads(gctx_ref, g2_ref)
    pairs = range(q2_ref.shape[0] // 2, q2_ref.shape[0])
    attend_back(pairs, g2_ref, q2_ref, k_ref, v_ref, p_ref, ctx_ref, ds_ref, dq2_ref, dqkv_ref, doth_ref)
    width = base_ref.shape[1]
    half = width // 2
    for index in range(3):
        at = slice(index * width, index * width + half)
        dqkv_ref[:, at] = dqkv0_ref[:, at]
        if index < 2:
            doth_ref[:, at] = doth0_ref[:, at]
    for index in range(3):
        cols = slice(index * width, (index + 1) * width)
        value = dot(rown_ref[...], dqkv_ref[:, cols], 0, 0) + dot(
            rown1_ref[...], dqkv1_ref[:, cols], 0, 0
        )
        if index:
            other = slice((index - 1) * width, index * width)
            value = (
                value
                + dot(roth_ref[...], doth_ref[:, other], 0, 0)
                + dot(roth1_ref[...], doth1_ref[:, other], 0, 0)
            )
        place(fast, me_ref, value, whole_ref, outs, cols.start)
    inputs_back(dqkv_ref, doth_ref, wa_ref, base_ref, gs_ref, goth_ref)


def stack_kernel(*refs):
    *parts, out_ref, sems = refs
    for copy in pull([(part, out_ref.at[index]) for index, part in enumerate(parts)], sems):
        copy.wait()


def halves_kernel(by_y_ref, by_x_ref, low_ref, high_ref, sems):
    half = low_ref.shape[0]
    moves = [(by_y_ref.at[pl.ds(0, half)], low_ref), (by_x_ref.at[pl.ds(half, half)], high_ref)]
    for copy in pull(moves, sems):
        copy.wait()


def return_kernel(info_ref, out_ref, in_ref, back_ref, out_both_ref, in_both_ref):
    local, width = back_ref.shape[0], out_ref.shape[1]
    for own_ref, target, cols in (
        (out_ref, out_both_ref, slice(0, width)),
        (in_ref, in_both_ref, slice(width, 2 * width)),
    ):
        target[info_ref[1]] = own_ref[:local, :]
        target[1 - info_ref[1]] = back_ref[:, cols].astype(F32)


def send_kernel(own_ref, more_ref, out_ref, total_ref, back_ref):
    local, width = back_ref.shape[0], own_ref.shape[1]
    for part in chunks(own_ref.shape[0], ROWS):
        total = own_ref[part, :] + more_ref[part, :].astype(F32)
        total_ref[part, :] = total
        if part.start >= local:
            target = slice(part.start - local, part.stop - local)
            back_ref[target, :width] = out_ref[part, :].astype(BF16)
            back_ref[target, width:] = total.astype(BF16)


def add_core_kernel(keep_ref, got_ref, s11a_ref, s11b_ref, s10_ref, s01_ref, s00_ref):
    half = s11a_ref.shape[0]
    for z in range(keep_ref.shape[1]):
        for index, target in ((0, s00_ref), (1, s01_ref), (2, s10_ref)):
            total = keep_ref[index, z].astype(F32) + got_ref[index, z].astype(F32)
            target[z] = total.astype(BF16)
        total = (keep_ref[3, z].astype(F32) + got_ref[3, z].astype(F32)).astype(BF16)
        if z < half:
            s11a_ref[z] = total
        else:
            s11b_ref[z - half] = total


def beside(target_ref, z, values, rows, width):
    for index in range(values.shape[0] // rows):
        target_ref[z, :, index * width : (index + 1) * width] = values[index * rows : (index + 1) * rows]


def add_half_kernel(a10_ref, ax_ref, a01_ref, ay_ref, b10_ref, bx_ref, b01_ref, by_ref, o10_ref, o01_ref):
    half = ax_ref.shape[0]
    rows, width = b10_ref.shape[1], a10_ref.shape[2]
    at = a10_ref.shape[1] // rows * width
    for z in range(2 * half):
        for tall_ref, tall_got_ref, low_ref, got_ref, out_ref, first in (
            (a10_ref, ax_ref, b10_ref, bx_ref, o10_ref, 0),
            (a01_ref, ay_ref, b01_ref, by_ref, o01_ref, half),
        ):
            if first <= z < first + half:
                tall = (tall_ref[z].astype(F32) + tall_got_ref[z - first].astype(F32)).astype(BF16)
                low = (low_ref[z].astype(F32) + got_ref[z - first].astype(F32)).astype(BF16)
            else:
                tall, low = tall_ref[z], low_ref[z]
            beside(out_ref, z, tall, rows, width)
            out_ref[z, :, at:] = low


def add_both_kernel(info_ref, a_ref, b_ref, got_x_ref, got_y_ref, own_ref, near_ref, next_ref, far_ref):
    line = info_ref[0] // 8
    rows, width = b_ref.shape[1], a_ref.shape[2]
    count = a_ref.shape[1] // rows
    for z, out_ref in enumerate((own_ref, near_ref, next_ref, far_ref)):
        at = line ^ z
        for index in range(count + 1):
            if index < count:
                cols = slice(index * width, (index + 1) * width)
                own = a_ref[at, index * rows : (index + 1) * rows]
            else:
                cols = slice(count * width, got_x_ref.shape[2])
                own = b_ref[at]
            total = own.astype(F32) + got_x_ref[at, :, cols].astype(F32) + got_y_ref[at, :, cols].astype(F32)
            out_ref[:, cols] = total.astype(BF16)


def add_pair_kernel(own_ref, got_ref, sum_ref):
    sum_ref[...] = (own_ref[...].astype(F32) + got_ref[...].astype(F32)).astype(BF16)


def add_core_all_kernel(keep_ref, got_ref, *outs):
    for z in range(keep_ref.shape[1]):
        for index, target in enumerate(outs):
            target[z] = (keep_ref[index, z].astype(F32) + got_ref[index, z].astype(F32)).astype(BF16)


def add_four_kernel(info_ref, a_ref, b_ref, c_ref, d_ref, own_ref, near_ref, next_ref, far_ref):
    line = info_ref[0] // 8
    for z, out_ref in enumerate((own_ref, near_ref, next_ref, far_ref)):
        at = line ^ z
        total = a_ref[at].astype(F32) + b_ref[at].astype(F32) + c_ref[at].astype(F32)
        out_ref[...] = (total + d_ref[at].astype(F32)).astype(BF16)


def end_both_kernel(own_ref, got_ref, far_ref, tall_ref, win_ref, wo_ref, *rest):
    vectors, flip_ref = rest[:-1], rest[-1]
    rows, width = far_ref.shape[0], tall_ref.shape[1]

    def total(cols):
        return own_ref[:, cols].astype(F32) + got_ref[:, cols].astype(F32) + far_ref[:, cols].astype(F32)

    at = tall_ref.shape[0] // rows * width
    for index in range(tall_ref.shape[0] // rows):
        tall_ref[index * rows : (index + 1) * rows, :] = total(slice(index * width, (index + 1) * width))
    for out in (win_ref, wo_ref):
        out[...] = total(slice(at, at + out.shape[1]))
        at = at + out.shape[1]
    flip_ref[...] = jnp.zeros_like(flip_ref)
    flip_ref[:rows, :] = total(slice(at, at + LANES))
    turned = flip_ref[...].T
    for index, vector in enumerate(vectors):
        vector[...] = turned[index : index + 1, :rows]


def end_kernel(own_ref, got_ref, far_ref, *outs):
    at = 0
    for out in outs:
        cols = slice(at, at + out.shape[1])
        out[...] = own_ref[:, cols].astype(F32) + got_ref[:, cols].astype(F32) + far_ref[:, cols].astype(F32)
        at = at + out.shape[1]


def vm():
    return pl.BlockSpec(memory_space=pltpu.VMEM)


def run(kernel, ins, outs, scratch=(), scalars=(), loose=(), pinned=(), far=(), sems=0, micros=0.05):
    specs = [vm() for _ in ins]
    for index in scalars:
        specs[index] = pl.BlockSpec(memory_space=pltpu.SMEM)
    ins = list(ins)
    for index in loose:
        specs[index] = pl.BlockSpec(memory_space=pl.ANY)
    for index in pinned:
        specs[index] = pl.BlockSpec(memory_space=pltpu.HBM)
        ins[index] = pltpu.with_memory_space_constraint(ins[index], pltpu.HBM)
    size = sum(v.size * v.dtype.itemsize for v in ins) + sum(
        functools.reduce(lambda a, b: a * b, s, 1) * jnp.dtype(t).itemsize for s, t in outs
    )
    buffers = [pltpu.VMEM(s, t) for s, t in scratch]
    need = sum(functools.reduce(lambda a, b: a * b, s, 1) * jnp.dtype(t).itemsize for s, t in scratch)
    if sems:
        buffers.append(pltpu.SemaphoreType.DMA((sems,)))
    return pl.pallas_call(
        kernel,
        out_shape=[jax.ShapeDtypeStruct(s, t) for s, t in outs],
        in_specs=specs,
        out_specs=[pl.BlockSpec(memory_space=pl.ANY) if index in far else vm() for index in range(len(outs))],
        scratch_shapes=buffers,
        compiler_params=pltpu.CompilerParams(vmem_limit_bytes=max(need + 8 * MIB, SCOPED)),
        cost_estimate=pl.CostEstimate(
            flops=int(micros * MICRO), bytes_accessed=size, transcendentals=0
        ),
    )(*ins)


AXES = ("dp", "head")


def after(value, *others):
    return lax.optimization_barrier((value, *others))[0]


class Links:
    def __init__(self, model_rows):
        self.heads = lax.axis_size("head")
        self.pods = lax.axis_size("dp")
        self.count = self.heads * self.pods
        self.fast = self.heads == 4 and self.pods == 8 and model_rows == 16
        self.head = lax.axis_index("head")
        self.me = lax.axis_index("dp") * self.heads + self.head

    def flip(self, value, bit):
        return lax.ppermute(value, AXES, [(i, i ^ bit) for i in range(self.count)])

    def flip_head(self, value, bit):
        return lax.ppermute(value, "head", [(i, i ^ bit) for i in range(self.heads)])

    def along_z(self, block):
        return [block, *(self.flip(block, 8 * k) for k in (1, 2, 3))]

    def stack(self, parts):
        (out,) = run(
            stack_kernel, parts, [((4, *parts[0].shape), BF16)], loose=range(4), far=(0,), sems=4
        )
        return out

    def core_sums(self, keep, got):
        block = keep.shape[2:]
        whole, half = ((4, *block), BF16), ((2, *block), BF16)
        return run(add_core_kernel, [keep, got], [half, half, whole, whole, whole])

    def line_first(self, kernel, parts, shape):
        own, near, following, far = run(kernel, [self.info, *parts], [(shape, BF16)] * 4, scalars=(0,))
        return own, far, self.flip(near, 8), self.flip(following, 8)

    def line_last(self, own, far, got, got_far):
        (far,) = run(add_pair_kernel, [after(far, got), got_far], [(far.shape, BF16)])
        return own, got, self.flip(far, 24)

    def spread(self, own, group):
        held, bit = own[None], 1
        while bit < group:
            got = self.flip_head(held, bit)
            held = got if bit == 1 and group == 2 else jnp.concatenate([held, got], axis=0)
            bit = bit * 2
        if group > 2:
            held = held[1:]
        return held.reshape(-1, own.shape[1])

    def collapse(self, parts, group, rows):
        if group == 2:
            return self.flip_head(parts, 1)
        held = parts.reshape(group - 1, rows, -1)
        held = jnp.concatenate([jnp.zeros_like(held[:1]), held], axis=0).astype(F32)
        bit = group // 2
        while bit >= 1:
            held = held[:bit] + self.flip_head(held[bit : 2 * bit], bit)
            bit = bit // 2
        return held[0]


def body(
    tokens, cotangent, lengths, halting, w_query, w_key, w_value, w_out, w_in, w_hidden,
    w_halt, gain_attn, shift_attn, gain_ffn, shift_ffn,
):
    micro, local, width = tokens.shape
    links = Links(w_query.shape[0])
    fast, heads = links.fast, links.heads
    group = heads // micro
    rows, length = micro * local, local * heads
    mine = links.head // group
    wide_ff = w_in.shape[1]
    fine = width // links.count
    matrices = (w_query, w_key, w_value, w_out, w_in, w_hidden)
    vectors = (w_halt, gain_attn, shift_attn, gain_ffn, shift_ffn)
    place_array = jnp.stack([links.me, mine, links.head % group, jnp.int32(group)]).astype(jnp.int32)
    links.info = place_array

    pairs = width // LANES
    row_f, row_b = ((rows, width), F32), ((rows, width), BF16)
    stat = ((rows, LANES), F32)
    others = length - rows
    long_b = ((length, width), BF16)
    q2_t = ((pairs, 2 * rows, LANES), BF16)
    p_t = ((pairs, 2 * rows, length), BF16)
    o_t = ((2 * rows, LANES), F32)
    bias_t = ((rows, length), F32)
    inner_t = ((rows, BLOCK), F32)
    ff_b = ((rows, wide_ff), BF16)
    sums_t = ((VECS, 8, width), F32)
    ds_t = ((2 * rows, length), BF16)
    dqkv_t = ((rows, 3 * width), BF16)
    doth_t = ((others, 2 * width), BF16)
    vg_t = ((8, width), F32)
    segq_t, segk_t = ((rows, LANES), jnp.int32), ((8, length), jnp.int32)

    sort_in = [place_array, tokens, cotangent, halting]
    sort_out = [((local, 2 * width + LANES), BF16)] * 2
    sort_tmp = [((LANES, local), F32), (halting.shape, jnp.int32)]
    if fast:
        send_tok, own_tok, block_a, block_b = run(
            pack_kernel,
            [*sort_in, *matrices, *(vector[None] for vector in vectors)],
            [*sort_out, ((5, fine, BLOCK), BF16), ((8, fine, BLOCK), BF16)],
            [*sort_tmp, ((LANES, LANES), F32), ((VECS, 1, fine), BF16)],
            scalars=(0,),
            pinned=range(1, 15),
            sems=22,
        )
        got_tok = links.flip_head(send_tok, group)
        line_a = links.along_z(block_a)
        own_a = after(links.stack(line_a), got_tok)
        plane_a = [own_a, *(links.flip(own_a, 2 * k) for k in (1, 2, 3))]
        plane_a = plane_a + [links.flip(piece, 1) for piece in plane_a]
        own_b = after(links.stack(links.along_z(after(block_b, line_a[1]))), *plane_a[1:4])
        by_x, by_y = links.flip(own_b, 2), links.flip(own_b, 4)
        near = [own_b, by_x, by_y]
        near = near + [links.flip(piece, 1) for piece in near]
    else:
        send_tok, own_tok = run(
            sort_kernel, sort_in, sort_out, sort_tmp, scalars=(0,), pinned=(1, 2, 3), sems=5
        )
        full = [lax.all_gather(part, AXES, axis=0, tiled=True) for part in matrices]
        full_v = [lax.all_gather(part, AXES, axis=0, tiled=True) for part in vectors]
        full_a = jnp.stack(full[:4])
        full_in = jnp.transpose(full[4].reshape(width, wide_ff // BLOCK, BLOCK), (1, 0, 2))
        full_hid = full[5]
        vec = jnp.pad(jnp.stack(full_v), ((0, 8 - VECS), (0, 0))).astype(F32)

        got_tok = links.flip_head(send_tok, group)
    tok, x0, rown0, sig1, segq, segk = run(
        embed_kernel,
        [place_array, lengths[:, 0], own_tok, got_tok],
        [((rows, 2 * width + LANES), BF16), row_f, row_b, row_f, segq_t, segk_t],
        scalars=(0, 1),
    )
    roth0 = links.spread(rown0, group)

    attend_in = [rown0, roth0, segq, segk]
    attend_out = [q2_t, long_b, long_b, p_t, row_b]
    if fast:
        full_a, vec, q2, k, v, p, ctx = run(
            functools.partial(attend_kernel, True),
            [*attend_in, links.info, *plane_a],
            [((5, 4, 8, fine, BLOCK), BF16), vg_t, *attend_out],
            [row_b, bias_t, o_t],
            scalars=(4,),
            micros=8,
        )
        full_a = full_a.reshape(5, width, BLOCK)
    else:
        q2, k, v, p, ctx = run(
            functools.partial(attend_kernel, False),
            [*attend_in, full_a],
            attend_out,
            [row_b, bias_t, o_t],
            micros=8,
        )
    ffn_out = [row_f, stat, row_b, ff_b, ff_b, row_f, stat, stat, row_f, row_f, row_f, row_b]
    ffn_in = [x0, ctx, tok, sig1, vec, full_a]
    if fast:
        by_x, by_y = after(by_x, ctx), after(by_y, ctx)
        halves = run(
            halves_kernel, [by_y, by_x], [((2, 8, fine, BLOCK), BF16)] * 2, loose=(0, 1), far=(0, 1), sems=2
        )
        far_b = [links.flip(halves[0], 2), links.flip(halves[1], 4)]
        far_b = far_b + [links.flip(piece, 1) for piece in far_b]
        full_in, full_hid, *got = run(
            functools.partial(ffn_kernel, True),
            [*ffn_in, links.info, *near, *far_b],
            [((4, 4, 8, fine, BLOCK), BF16), ((4, 8, 4, fine, BLOCK), BF16), *ffn_out],
            [inner_t, row_f],
            scalars=(6,),
            micros=5.5,
        )
        full_in = full_in.reshape(4, width, BLOCK)
        full_hid = full_hid.reshape(wide_ff, width)
    else:
        got = run(
            functools.partial(ffn_kernel, False),
            [*ffn_in, full_in, full_hid],
            ffn_out,
            [inner_t, row_f],
            micros=5.5,
        )
    n1, r1, nlow, hid, dg, n2, r2, rate, state, pooled, x1, rown1 = got
    roth1 = links.spread(rown1, group)
    out, gs, goth, nlow1, hid1, b11, b21, ctx1, b01, dqkv1, doth1, vg1 = run(
        turn_kernel,
        [x1, rown1, roth1, full_a, full_in, full_hid, vec, segq, segk, state, pooled, tok],
        [row_f, row_f, ((others, width), BF16), row_b, ff_b, ff_b, row_b, row_b, row_b, dqkv_t, doth_t, vg_t],
        [
            row_b, q2_t, long_b, long_b, p_t, bias_t, o_t, row_f, row_f, stat, inner_t, ff_b,
            row_f, stat, stat, row_f, row_f, sums_t, row_b, q2_t, ds_t,
        ],
        micros=15.7,
    )
    more = links.collapse(goth, group, rows)

    b_cols = wide_ff + width + LANES
    def parts_of(shape, whole):
        return [((4, 4, *shape), BF16)] * 2 if fast else [(whole, F32)]

    hid_out = parts_of((4 * fine, width), (wide_ff, width))
    in_out = parts_of((fine, b_cols), (width, b_cols))
    attend_outs = parts_of((fine, 3 * width), (width, 3 * width))
    whole_shape = (4, 8, fine, BLOCK) if fast else (8, LANES)
    tall_shape = (8, 4 * fine, width) if fast else (8, LANES)
    b2, gsec, base, sums, *hid_parts = run(
        functools.partial(hidden_back_kernel, fast),
        [links.info, gs, more, tok, vec, n2, r2, rate, hid, hid1, b21],
        [row_b, row_f, row_f, sums_t, *hid_out],
        [(tall_shape, F32)],
        scalars=(0,),
        micros=2,
    )
    b1, b0, base, gctx, sums = run(
        feed_back_kernel,
        [b2, gsec, base, sums, vec, full_in, full_hid, full_a, n1, r1, dg],
        [ff_b, row_b, row_f, row_b, sums_t],
        [inner_t, row_f],
        micros=2.2,
    )
    if fast:
        c_sums = links.core_sums(hid_parts[0], links.flip(hid_parts[1], 1))
        b1 = after(b1, c_sums[0])
    in_parts = run(
        functools.partial(weights_back_kernel, fast),
        [links.info, b1, b0, sums, nlow, ctx, nlow1, b11, ctx1, b01, vg1],
        in_out,
        [(whole_shape, F32), ((LANES, width), F32)],
        scalars=(0,),
        micros=2,
    )
    if fast:
        b_sums = links.core_sums(in_parts[0], links.flip(in_parts[1], 1))
        gctx = after(gctx, b_sums[0])
    dqkv0, doth0 = run(
        first_heads_kernel,
        [gctx, q2, k, v, p, ctx],
        [dqkv_t, doth_t],
        [q2_t, ds_t, o_t],
        micros=3,
    )
    if fast:
        c11a, c11b, c10, c01, c00 = c_sums
        b11a, b11b, b10, b01, b00 = b_sums
        halves = [
            after(c10, dqkv0), links.flip(c11a, 2), c01, links.flip(c11b, 4),
            b10, links.flip(b11a, 2), b01, links.flip(b11b, 4),
        ]
        both_t = ((4, fine, 4 * width + b_cols), BF16)
        both10, both01 = run(add_half_kernel, halves, [both_t] * 2)
        dqkv0 = after(dqkv0, both01)
    g0, goth0, *attend_parts = run(
        functools.partial(last_heads_kernel, fast),
        [
            links.info, base, gctx, q2, k, v, p, ctx, full_a,
            rown0, roth0, rown1, roth1, dqkv1, doth1, dqkv0, doth0,
        ],
        [row_f, ((others, width), BF16), *attend_outs],
        [q2_t, ds_t, o_t, dqkv_t, doth_t, (whole_shape, F32)],
        scalars=(0,),
        micros=4,
    )
    inputs, back = run(
        send_kernel,
        [g0, links.collapse(goth0, group, rows), out],
        [row_f, ((local, 2 * width), BF16)],
    )
    if fast:
        keep, got = attend_parts[0], links.flip(attend_parts[1], 1)
        a00, a01, a10, a11 = run(add_core_all_kernel, [keep, got], [(keep.shape[1:], BF16)] * 4)
        by_plane = [a00, links.flip(a11, 6), links.flip(a01, 2), links.flip(a10, 4)]
        both = links.line_first(
            add_both_kernel, [after(c00, a00), b00, links.flip(both01, 2), links.flip(both10, 4)], both_t[0][1:]
        )
        by_plane[0] = after(by_plane[0], both[0])
        attend_sums = links.line_first(add_four_kernel, by_plane, a00.shape[1:])
        both = links.line_last(both[0], after(both[1], attend_sums[0]), *both[2:])
        attend_sums = links.line_last(*attend_sums)
        back = after(back, attend_sums[0])
        g_hidden, g_in, g_out, *g_vectors = run(
            end_both_kernel,
            both,
            [((4 * fine, width), F32), ((fine, wide_ff), F32), ((fine, width), F32)] + [((1, fine), F32)] * VECS,
            [((LANES, LANES), F32)],
        )
        output, input_grad = run(
            return_kernel,
            [links.info, out, inputs, links.flip_head(back, group)],
            [((micro, local, width), F32)] * 2,
            scalars=(0,),
        )
        g_query, g_key, g_value = run(
            end_kernel,
            [after(attend_sums[0], output, g_hidden), *attend_sums[1:]],
            [((fine, width), F32)] * 3,
        )
        g_vectors = [vector.reshape(fine) for vector in g_vectors]
    else:
        sums = [
            *(attend_parts[0][:, index * width : (index + 1) * width] for index in range(3)),
            in_parts[0][:, wide_ff : wide_ff + width], in_parts[0][:, :wide_ff], hid_parts[0],
            in_parts[0][:, wide_ff + width :],
        ]
        sums = [lax.psum_scatter(part, AXES, scatter_dimension=0, tiled=True) for part in sums]
        g_query, g_key, g_value, g_out, g_in, g_hidden, g_vec = sums
        g_vectors = [g_vec[:, index] for index in range(VECS)]
        output, input_grad = run(
            return_kernel,
            [links.info, out, inputs, links.flip_head(back, group)],
            [((micro, local, width), F32)] * 2,
            scalars=(0,),
        )
    return (output, input_grad, g_query, g_key, g_value, g_out, g_in, g_hidden, *g_vectors)


def solution(mesh):
    whole = P(("dp", "head"))
    matrix = P(("dp", "head"), None)
    rows = P(None, ("dp", "head"), None)
    return jax.shard_map(
        body,
        mesh=mesh,
        in_specs=(rows, rows, P(None, "dp", None), P(None, None, ("dp", "head")))
        + (matrix,) * 6
        + (whole,) * 5,
        out_specs=(rows, rows) + (matrix,) * 6 + (whole,) * 5,
        check_vma=False,
    )
```

```python
import functools

import jax
import jax.numpy as jnp
from jax import lax
from jax.experimental import pallas as pl
from jax.experimental.pallas import tpu as pltpu
from jax.sharding import PartitionSpec as P

HD = 64
EPSILON = 1e-06
F32 = jnp.float32
BF16 = jnp.bfloat16
LANES = 128
ROWS = 32
ATT_ROWS = 256
BLOCK = 512
VECS = 5
MIB = 1024 * 1024
SCOPED = 20 * MIB
MICRO = 1.15e9
GELU_A = 0.7978845608028654
GELU_B = 0.044715


def dot(a, b, ca=1, cb=0):
    return lax.dot_general(a, b, (((ca,), (cb,)), ((), ())), preferred_element_type=F32)


def chunks(total, size):
    size = min(size, total)
    return [slice(i, i + size) for i in range(0, total, size)]


def wide(column):
    return jnp.broadcast_to(column, (column.shape[0], LANES))


def mean(values):
    return jnp.sum(values, axis=-1, keepdims=True) * (1.0 / values.shape[-1])


def fold(values):
    return jnp.sum(values.reshape(values.shape[0] // 8, 8, values.shape[1]), axis=0)


class Flat:
    def __init__(self, ref):
        self.ref = ref

    def __getitem__(self, index):
        if index is Ellipsis:
            index = (slice(None), slice(None))
        value = self.ref[..., index[1]]
        return value.reshape(-1, value.shape[-1])[index[0]]


def matrix(ref, index):
    value = ref[index]
    return value.reshape(-1, value.shape[-1])


def head_mask(rows):
    lane = lax.broadcasted_iota(jnp.int32, (rows, LANES), 1)
    return lane < HD


def normalize(values):
    center = values - mean(values)
    inverse = lax.rsqrt(mean(center * center) + EPSILON)
    return center * inverse, inverse


def normalize_back(unit, inverse, grad):
    return inverse * (grad - mean(grad) - unit * mean(grad * unit))


def split_heads(values_ref, stacked_ref):
    rows = values_ref.shape[0]
    for part in chunks(rows, ATT_ROWS):
        first = head_mask(part.stop - part.start)
        for pair in range(stacked_ref.shape[0]):
            block = values_ref[part, pair * LANES : (pair + 1) * LANES].astype(F32)
            stacked_ref[pair, part, :] = jnp.where(first, block, 0.0).astype(BF16)
            stacked_ref[pair, rows + part.start : rows + part.stop, :] = jnp.where(
                first, 0.0, block
            ).astype(BF16)


def project(rown_ref, roth_ref, wa_ref, q_ref, q2_ref, k_ref, v_ref):
    rows, width = rown_ref.shape
    q_ref[...] = (
        dot(rown_ref[...], matrix(wa_ref, 0)).astype(BF16).astype(F32) * HD**-0.5
    ).astype(BF16)
    split_heads(q_ref, q2_ref)
    for at, source in ((0, rown_ref), (rows, roth_ref)):
        span = slice(at, at + source.shape[0])
        k_ref[span, :] = dot(source[...], matrix(wa_ref, 1)).astype(BF16)
        v_ref[span, :] = dot(source[...], matrix(wa_ref, 2)).astype(BF16)


def set_bias(segq_ref, segk_ref, bias_ref):
    for part in chunks(bias_ref.shape[0], ROWS):
        bias_ref[part, :] = jnp.where(segq_ref[part, 0:1] == segk_ref[0:1, :], 0.0, -1e30)


def attend(q2_ref, k_ref, v_ref, bias_ref, p_ref, ctx_ref, o_ref):
    rows, length = bias_ref.shape
    for pair in range(q2_ref.shape[0]):
        cols = slice(pair * LANES, (pair + 1) * LANES)
        for part in chunks(2 * rows, 2 * rows):
            scores = dot(q2_ref[pair, part, :], k_ref[:, cols], 1, 1)
            scores = (scores.reshape(2, rows, length) + bias_ref[...][None]).reshape(2 * rows, length)
            weights = jnp.exp(scores - jnp.max(scores, axis=-1, keepdims=True))
            inverse = 1.0 / jnp.sum(weights, axis=-1, keepdims=True)
            low = (weights * inverse).astype(BF16)
            p_ref[pair, part, :] = low
            o_ref[part, :] = dot(low, v_ref[:, cols])
        for part in chunks(rows, ATT_ROWS):
            first = head_mask(part.stop - part.start)
            second = o_ref[rows + part.start : rows + part.stop, :]
            ctx_ref[part, cols] = jnp.where(first, o_ref[part, :], second).astype(BF16)


def first_norm(x_ref, ctx_ref, wa_ref, vec_ref, acc_ref, n1_ref, r1_ref, nlow_ref):
    acc_ref[...] = dot(ctx_ref[...], matrix(wa_ref, 3))
    for part in chunks(x_ref.shape[0], ROWS):
        unit, inverse = normalize(x_ref[part, :] + acc_ref[part, :])
        n1_ref[part, :] = unit
        r1_ref[part, :] = wide(inverse)
        nlow_ref[part, :] = (unit * vec_ref[1:2, :] + vec_ref[2:3, :]).astype(BF16)


def feed_forward(nlow_ref, win_ref, whid_ref, inner_ref, hid_ref, dg_ref, acc_ref):
    rows = nlow_ref.shape[0]
    for cols in chunks(hid_ref.shape[1], BLOCK):
        inner_ref[...] = dot(nlow_ref[...], matrix(win_ref, cols.start // BLOCK))
        for part in chunks(rows, ROWS):
            x = inner_ref[part, :]
            square = x * x
            t = jnp.tanh(x * (GELU_A + GELU_A * GELU_B * square))
            half = 0.5 + 0.5 * t
            hid_ref[part, cols] = (x * half).astype(BF16)
            slope = 0.5 * x * (1.0 - t * t) * (GELU_A + 3.0 * GELU_A * GELU_B * square)
            dg_ref[part, cols] = (half + slope).astype(BF16)
    acc_ref[...] = dot(hid_ref[...], whid_ref[...])


def second_norm(part, vec_ref, n1_ref, acc_ref):
    normed = n1_ref[part, :] * vec_ref[1:2, :] + vec_ref[2:3, :]
    unit, inverse = normalize(normed + acc_ref[part, :])
    updated = unit * vec_ref[3:4, :] + vec_ref[4:5, :]
    rate = jax.nn.sigmoid(jnp.sum(updated * vec_ref[0:1, :], axis=-1, keepdims=True))
    return unit, inverse, updated, rate


def tail_back(
    part, step, gs, gp, halt_ref, vec_ref, n2_ref, r2_ref, rate_ref, b2_ref, gsec_ref, base_ref, sums_ref
):
    width = n2_ref.shape[1]
    keep = halt_ref[part, 2 * width + step : 2 * width + step + 1].astype(F32)
    unit = n2_ref[part, :]
    updated = unit * vec_ref[3:4, :] + vec_ref[4:5, :]
    rate = rate_ref[part, 0:1]
    logit = keep * jnp.sum(gp * updated, axis=-1, keepdims=True) * rate * (1.0 - rate)
    grad = keep * gs + (keep * rate) * gp + logit * vec_ref[0:1, :]
    base_ref[part, :] = gs - keep * gs
    sums_ref[0] += fold(logit * updated)
    sums_ref[3] += fold(grad * unit)
    sums_ref[4] += fold(grad)
    back = normalize_back(unit, r2_ref[part, 0:1], grad * vec_ref[3:4, :])
    gsec_ref[part, :] = back
    b2_ref[part, :] = back.astype(BF16)


def feed_back(b2_ref, dg_ref, win_ref, whid_ref, inner_ref, b1_ref, acc_ref):
    rows = b2_ref.shape[0]
    for cols in chunks(dg_ref.shape[1], BLOCK):
        inner_ref[...] = dot(b2_ref[...], whid_ref[cols, :], 1, 1)
        for part in chunks(rows, ROWS):
            b1_ref[part, cols] = (inner_ref[part, :] * dg_ref[part, cols].astype(F32)).astype(BF16)
    total = None
    for cols in chunks(dg_ref.shape[1], BLOCK):
        value = dot(b1_ref[:, cols], matrix(win_ref, cols.start // BLOCK), 1, 1)
        total = value if total is None else total + value
    acc_ref[...] = total


def middle_back(gsec_ref, acc_ref, vec_ref, n1_ref, r1_ref, b0_ref, base_ref, sums_ref):
    for part in chunks(gsec_ref.shape[0], ROWS):
        grad = gsec_ref[part, :] + acc_ref[part, :]
        unit = n1_ref[part, :]
        sums_ref[1] += fold(grad * unit)
        sums_ref[2] += fold(grad)
        back = normalize_back(unit, r1_ref[part, 0:1], grad * vec_ref[1:2, :])
        base_ref[part, :] += back
        b0_ref[part, :] = back.astype(BF16)


def attend_back(
    pairs, g2_ref, q2_ref, k_ref, v_ref, p_ref, ctx_ref, ds_ref, dq2_ref, dqkv_ref, doth_ref
):
    rows, width = ctx_ref.shape
    for pair in pairs:
        cols = slice(pair * LANES, (pair + 1) * LANES)
        for part in chunks(2 * rows, 2 * rows):
            grad = g2_ref[pair, part, :]
            both = jnp.concatenate([ctx_ref[:, cols]] * 2, axis=0)
            delta = jnp.sum(grad.astype(F32) * both.astype(F32), axis=-1, keepdims=True)
            back = dot(grad, v_ref[:, cols], 1, 1)
            low = (p_ref[pair, part, :].astype(F32) * (back - delta)).astype(BF16)
            ds_ref[part, :] = low
            dq2_ref[part, :] = dot(low, k_ref[:, cols])
        for part in chunks(rows, ATT_ROWS):
            first = head_mask(part.stop - part.start)
            second = dq2_ref[rows + part.start : rows + part.stop, :]
            dqkv_ref[part, cols] = (
                jnp.where(first, dq2_ref[part, :], second) * HD**-0.5
            ).astype(BF16)
        for index, (left, right) in enumerate(
            ((ds_ref[...], q2_ref[pair]), (p_ref[pair], g2_ref[pair]))
        ):
            both = dot(right, left, 0, 0).T.astype(BF16)
            at = index * width + pair * LANES
            dqkv_ref[:, width + at : width + at + LANES] = both[:rows]
            doth_ref[:, at : at + LANES] = both[rows:]


def inputs_back(dqkv_ref, doth_ref, wa_ref, base_ref, gs_ref, goth_ref):
    width = base_ref.shape[1]
    parts = [slice(index * width, (index + 1) * width) for index in range(3)]
    total = base_ref[...]
    for index, cols in enumerate(parts):
        total = total + dot(dqkv_ref[:, cols], matrix(wa_ref, index), 1, 1)
    gs_ref[...] = total
    total = dot(doth_ref[:, parts[0]], matrix(wa_ref, 1), 1, 1)
    goth_ref[...] = (total + dot(doth_ref[:, parts[1]], matrix(wa_ref, 2), 1, 1)).astype(BF16)


def fetch(pieces, cores, bits, start, store, me_ref):
    line, place_in = me_ref[0] // 8, me_ref[0] % 8
    for piece, core, bit in zip(pieces, cores, bits):
        for z in range(piece.shape[0]):
            store(piece, z, line ^ (start + z), place_in ^ (bit | core))


def embed_kernel(place_ref, sizes_ref, tok_ref, got_ref, own_ref, x_ref, rown_ref, sig_ref, segq_ref, segk_ref):
    mine, place_in, group = place_ref[1], place_ref[2], place_ref[3]
    local = tok_ref.shape[0]
    half = x_ref.shape[1] // 2
    ends, starts, total = [], [], 0
    for index in range(sizes_ref.shape[1]):
        starts.append(total)
        total = total + sizes_ref[mine, index]
        ends.append(total)
    ones = jnp.exp(
        lax.broadcasted_iota(jnp.int32, (8, half), 1).astype(F32)
        * (-jnp.log(jnp.full((8, half), 10000.0, F32)) / max(half - 1, 1))
    )
    rates = ones[0:1, :]
    first_sin, first_cos = jnp.sin(rates), jnp.cos(rates)
    for part in chunks(x_ref.shape[0], ROWS):
        size = part.stop - part.start
        block = mine * group + place_in
        block = block if part.start < local else block ^ group
        at = block * local + part.start % local
        token = at + lax.broadcasted_iota(jnp.int32, (size, LANES), 0)
        segment = jnp.zeros((size, LANES), jnp.int32)
        begin = jnp.zeros((size, LANES), jnp.int32)
        for start, end in zip(starts, ends):
            segment = segment + jnp.where(token >= end, 1, 0)
            begin = jnp.maximum(begin, jnp.where(token >= start, start, 0))
        segq_ref[part, :] = segment
        angles = (token - begin).astype(F32)[:, 0:1] * rates
        if part.start < local:
            low = tok_ref[part, :]
        else:
            low = got_ref[part.start - local : part.stop - local, :]
        own_ref[part, :] = low
        for cols, moving, still, step in (
            (slice(0, half), jnp.sin(angles), 0.0, first_sin),
            (slice(half, 2 * half), jnp.cos(angles), 1.0, first_cos),
        ):
            inputs = low[:, cols].astype(F32) + (moving + still)
            x_ref[part, cols] = inputs
            rown_ref[part, cols] = inputs.astype(BF16)
            sig_ref[part, cols] = moving + step
    blocks = segk_ref.shape[1] // local
    for index in range(blocks):
        peer = mine * group + (place_in ^ (index // 2))
        peer = peer if index % 2 == 0 else peer ^ group
        token = peer * local + lax.broadcasted_iota(jnp.int32, (8, local), 1)
        segment = jnp.zeros((8, local), jnp.int32)
        for end in ends:
            segment = segment + jnp.where(token >= end, 1, 0)
        segk_ref[:, index * local : (index + 1) * local] = segment


def pull(sources, sems):
    copies = [
        pltpu.make_async_copy(source, target, sems.at[index]) for index, (source, target) in enumerate(sources)
    ]
    for copy in copies:
        copy.start()
    return copies


def sort_rows(place_ref, tok_ref, cot_ref, halt_ref, refs, sems):
    mine = place_ref[1]
    width = tok_ref.shape[2]
    send_ref, own_ref, flip_ref, flags_ref = refs
    moves = [(halt_ref, flags_ref)]
    for micro, target in ((1 - mine, send_ref), (mine, own_ref)):
        moves.append((tok_ref.at[micro], target.at[:, :width]))
        moves.append((cot_ref.at[micro], target.at[:, width : 2 * width]))
    copies = pull(moves, sems)
    flip_ref[...] = jnp.zeros_like(flip_ref)
    for copy in copies:
        copy.wait()
    for target, micro in ((own_ref, mine), (send_ref, 1 - mine)):
        for step in range(halt_ref.shape[0]):
            flip_ref[step : step + 1, :] = flags_ref[step, pl.ds(micro, 1), :].astype(F32)
        target[:, 2 * width :] = flip_ref[...].T.astype(BF16)


def sort_kernel(place_ref, tok_ref, cot_ref, halt_ref, *refs):
    sort_rows(place_ref, tok_ref, cot_ref, halt_ref, refs[:4], refs[4])


def pack_kernel(place_ref, tok_ref, cot_ref, halt_ref, q_ref, k_ref, v_ref, o_ref, win_ref, whid_ref, *rest):
    vectors, rest = rest[:VECS], rest[VECS:]
    sorted_refs, (block_ref, tall_ref, flip_ref, flags_ref, turn_ref, low_ref, sems) = rest[:2], rest[2:]
    rows, width = q_ref.shape
    moves = [(vector, low_ref.at[index]) for index, vector in enumerate(vectors)]
    for index, source in enumerate((q_ref, k_ref, v_ref, o_ref)):
        moves.append((source, block_ref.at[index]))
    for index in range(4):
        moves.append((win_ref.at[:, index * BLOCK : (index + 1) * BLOCK], tall_ref.at[index]))
        moves.append((whid_ref.at[index * rows : (index + 1) * rows, :], tall_ref.at[4 + index]))
    copies = pull(moves, sems.at[:17])
    sort_rows(place_ref, tok_ref, cot_ref, halt_ref, [*sorted_refs, flip_ref, flags_ref], sems.at[17:])
    turn_ref[...] = jnp.zeros_like(turn_ref)
    for copy in copies:
        copy.wait()
    for index in range(VECS):
        turn_ref[index : index + 1, :rows] = low_ref[index].astype(F32)
    block_ref[4, :, :LANES] = turn_ref[...].T[:rows, :].astype(BF16)
    block_ref[4, :, LANES:] = jnp.zeros((rows, width - LANES), BF16)


def attend_kernel(
    fast, rown_ref, roth_ref, segq_ref, segk_ref, *rest,
):
    if fast:
        me_ref, plane, rest = rest[0], rest[1:9], rest[9:]
        wa_ref, vec_ref, q2_ref, k_ref, v_ref, p_ref, ctx_ref, q_ref, bias_ref, o_ref = rest

        def store(piece, z, line, place):
            for chunk in range(5):
                wa_ref[chunk, line, place] = piece[z, chunk]

        fetch(plane, (0, 0, 0, 0, 1, 1, 1, 1), (0, 2, 4, 6) * 2, 0, store, me_ref)
        vec_ref[...] = matrix(wa_ref, 4)[:, :LANES].astype(F32).T[0:8, :]
    else:
        wa_ref, q2_ref, k_ref, v_ref, p_ref, ctx_ref, q_ref, bias_ref, o_ref = rest
    set_bias(segq_ref, segk_ref, bias_ref)
    project(rown_ref, roth_ref, wa_ref, q_ref, q2_ref, k_ref, v_ref)
    attend(q2_ref, k_ref, v_ref, bias_ref, p_ref, ctx_ref, o_ref)


def ffn_kernel(
    fast, x_ref, ctx_ref, tok_ref, sig_ref, vec_ref, wa_ref, *rest,
):
    if fast:
        me_ref, near, far, rest = rest[0], rest[1:7], rest[7:11], rest[11:]
        (win_ref, full_ref), rest = rest[:2], rest[2:]
    else:
        (win_ref, whid_ref), rest = rest[:2], rest[2:]
    (
        n1_ref, r1_ref, nlow_ref, hid_ref, dg_ref, n2_ref, r2_ref, rate_ref, state_ref,
        pooled_ref, next_ref, rown_ref, inner_ref, acc_ref,
    ) = rest
    if fast:

        def store(piece, z, line, place):
            for chunk in range(4):
                win_ref[chunk, line, place] = piece[z, chunk]
                full_ref[line, place, chunk] = piece[z, 4 + chunk]

        fetch(near, (0, 0, 0, 1, 1, 1), (0, 2, 4, 0, 2, 4), 0, store, me_ref)
        fetch((far[0], far[2]), (0, 1), (6, 6), 0, store, me_ref)
        fetch((far[1], far[3]), (0, 1), (6, 6), 2, store, me_ref)
        whid_ref = Flat(full_ref)
    width = x_ref.shape[1]
    first_norm(x_ref, ctx_ref, wa_ref, vec_ref, acc_ref, n1_ref, r1_ref, nlow_ref)
    feed_forward(nlow_ref, win_ref, whid_ref, inner_ref, hid_ref, dg_ref, acc_ref)
    for part in chunks(tok_ref.shape[0], ROWS):
        unit, inverse, updated, rate = second_norm(part, vec_ref, n1_ref, acc_ref)
        keep = tok_ref[part, 2 * width : 2 * width + 1].astype(F32)
        n2_ref[part, :] = unit
        r2_ref[part, :] = wide(inverse)
        rate_ref[part, :] = wide(rate)
        pooled_ref[part, :] = (keep * rate) * updated
        state = tok_ref[part, :width].astype(F32)
        state = state + keep * (updated - state)
        state_ref[part, :] = state
        inputs = state + sig_ref[part, :]
        next_ref[part, :] = inputs
        rown_ref[part, :] = inputs.astype(BF16)


def turn_kernel(
    x_ref, rown_ref, roth_ref, wa_ref, win_ref, whid_ref, vec_ref, segq_ref, segk_ref,
    state_ref, pooled_ref, tok_ref,
    out_ref, gs_ref, goth_ref, nlow_ref, hid_ref, b1_ref, b2_ref, ctx_ref, b0_ref, dqkv_ref, doth_ref, vg_ref,
    q_ref, q2_ref, k_ref, v_ref, p_ref, bias_ref, o_ref, acc_ref, n1_ref, r1_ref, inner_ref, dg_ref,
    n2_ref, r2_ref, rate_ref, gsec_ref, base_ref, sums_ref, gctx_ref, g2_ref, ds_ref,
):
    width = x_ref.shape[1]
    sums_ref[...] = jnp.zeros_like(sums_ref)
    set_bias(segq_ref, segk_ref, bias_ref)
    project(rown_ref, roth_ref, wa_ref, q_ref, q2_ref, k_ref, v_ref)
    attend(q2_ref, k_ref, v_ref, bias_ref, p_ref, ctx_ref, o_ref)
    first_norm(x_ref, ctx_ref, wa_ref, vec_ref, acc_ref, n1_ref, r1_ref, nlow_ref)
    feed_forward(nlow_ref, win_ref, whid_ref, inner_ref, hid_ref, dg_ref, acc_ref)
    for part in chunks(x_ref.shape[0], ROWS):
        unit, inverse, updated, rate = second_norm(part, vec_ref, n1_ref, acc_ref)
        keep = tok_ref[part, 2 * width + 1 : 2 * width + 2].astype(F32)
        n2_ref[part, :] = unit
        r2_ref[part, :] = wide(inverse)
        rate_ref[part, :] = wide(rate)
        state = state_ref[part, :]
        state = state + keep * (updated - state)
        out_ref[part, :] = state + (pooled_ref[part, :] + (keep * rate) * updated)
        cot = tok_ref[part, width : 2 * width].astype(F32)
        tail_back(
            part, 1, cot, cot, tok_ref, vec_ref, n2_ref, r2_ref, rate_ref, b2_ref, gsec_ref, base_ref,
            sums_ref,
        )
    feed_back(b2_ref, dg_ref, win_ref, whid_ref, inner_ref, b1_ref, acc_ref)
    middle_back(gsec_ref, acc_ref, vec_ref, n1_ref, r1_ref, b0_ref, base_ref, sums_ref)
    gctx_ref[...] = dot(b0_ref[...], matrix(wa_ref, 3), 1, 1).astype(BF16)
    split_heads(gctx_ref, g2_ref)
    pairs = range(q2_ref.shape[0])
    attend_back(pairs, g2_ref, q2_ref, k_ref, v_ref, p_ref, ctx_ref, ds_ref, o_ref, dqkv_ref, doth_ref)
    inputs_back(dqkv_ref, doth_ref, wa_ref, base_ref, gs_ref, goth_ref)
    vg_ref[...] = jnp.zeros_like(vg_ref)
    for index in range(VECS):
        vg_ref[index : index + 1, :] = jnp.sum(sums_ref[index], axis=0, keepdims=True)


def place(fast, me_ref, value, scratch_ref, outs, at):
    cols = slice(at, at + value.shape[1])
    if not fast:
        outs[0][:, cols] = value
        return
    scratch_ref[:, :, :, : value.shape[1]] = value.reshape(scratch_ref.shape[:3] + value.shape[1:])
    for relative in range(8):
        block = scratch_ref[:, relative ^ (me_ref[0] % 8), :, : value.shape[1]].astype(BF16)
        outs[relative % 2][relative // 2, :, :, cols] = block


def hidden_back_kernel(
    fast, me_ref, gs_ref, more_ref, tok_ref, vec_ref,
    n2_ref, r2_ref, rate_ref, hid_ref, hid1_ref, b21_ref,
    b2_ref, gsec_ref, base_ref, sums_ref,
    *rest,
):
    outs, tall_ref = rest[:-1], rest[-1]
    sums_ref[...] = jnp.zeros_like(sums_ref)
    width = gs_ref.shape[1]
    for part in chunks(gs_ref.shape[0], ROWS):
        tail_back(
            part, 0, gs_ref[part, :] + more_ref[part, :].astype(F32),
            tok_ref[part, width : 2 * width].astype(F32), tok_ref, vec_ref,
            n2_ref, r2_ref, rate_ref, b2_ref, gsec_ref, base_ref, sums_ref,
        )
    hidden_rows = hid_ref.shape[1] // 4
    for z in range(4):
        span = slice(z * hidden_rows, (z + 1) * hidden_rows)
        value = dot(hid_ref[:, span], b2_ref[...], 0, 0) + dot(hid1_ref[:, span], b21_ref[...], 0, 0)
        if fast:
            tall_ref[...] = value.reshape(tall_ref.shape)
            for relative in range(8):
                block = tall_ref[relative ^ (me_ref[0] % 8)].astype(BF16)
                outs[relative % 2][relative // 2, z] = block
        else:
            outs[0][span, :] = value


def feed_back_kernel(
    b2_ref, gsec_ref, base0_ref, sums0_ref, vec_ref, win_ref, whid_ref, wa_ref, n1_ref, r1_ref, dg_ref,
    b1_ref, b0_ref, base_ref, gctx_ref, sums_ref, inner_ref, acc_ref,
):
    sums_ref[...] = sums0_ref[...]
    base_ref[...] = base0_ref[...]
    feed_back(b2_ref, dg_ref, win_ref, whid_ref, inner_ref, b1_ref, acc_ref)
    middle_back(gsec_ref, acc_ref, vec_ref, n1_ref, r1_ref, b0_ref, base_ref, sums_ref)
    gctx_ref[...] = dot(b0_ref[...], matrix(wa_ref, 3), 1, 1).astype(BF16)


def weights_back_kernel(
    fast, me_ref, b1_ref, b0_ref, sums_ref, nlow_ref, ctx_ref, nlow1_ref, b11_ref, ctx1_ref, b01_ref, vg1_ref,
    *rest,
):
    outs, (whole_ref, flip_ref) = rest[:-2], rest[-2:]
    width = ctx_ref.shape[1]
    for cols in chunks(b1_ref.shape[1], BLOCK):
        value = dot(nlow_ref[...], b1_ref[:, cols], 0, 0) + dot(nlow1_ref[...], b11_ref[:, cols], 0, 0)
        place(fast, me_ref, value, whole_ref, outs, cols.start)
    value = dot(ctx_ref[...], b0_ref[...], 0, 0) + dot(ctx1_ref[...], b01_ref[...], 0, 0)
    at = b1_ref.shape[1]
    place(fast, me_ref, value, whole_ref, outs, at)
    flip_ref[...] = jnp.zeros_like(flip_ref)
    flip_ref[0:8, :] = vg1_ref[...]
    for index in range(VECS):
        flip_ref[index : index + 1, :] += jnp.sum(sums_ref[index], axis=0, keepdims=True)
    place(fast, me_ref, flip_ref[...].T, whole_ref, outs, at + width)


def heads_back_kernel(
    gctx_ref, q2_ref, k_ref, v_ref, p_ref, ctx_ref, dqkv_ref, doth_ref, g2_ref, ds_ref, dq2_ref
):
    split_heads(gctx_ref, g2_ref)
    pairs = range(q2_ref.shape[0])
    attend_back(pairs, g2_ref, q2_ref, k_ref, v_ref, p_ref, ctx_ref, ds_ref, dq2_ref, dqkv_ref, doth_ref)


def project_back_kernel(
    fast, me_ref, base_ref, wa_ref,
    rown_ref, roth_ref, rown1_ref, roth1_ref, dqkv1_ref, doth1_ref, dqkv_ref, doth_ref,
    gs_ref, goth_ref,
    *rest,
):
    outs, whole_ref = rest[:-1], rest[-1]
    width = base_ref.shape[1]
    for index in range(3):
        cols = slice(index * width, (index + 1) * width)
        value = dot(rown_ref[...], dqkv_ref[:, cols], 0, 0) + dot(
            rown1_ref[...], dqkv1_ref[:, cols], 0, 0
        )
        if index:
            other = slice((index - 1) * width, index * width)
            value = (
                value
                + dot(roth_ref[...], doth_ref[:, other], 0, 0)
                + dot(roth1_ref[...], doth1_ref[:, other], 0, 0)
            )
        place(fast, me_ref, value, whole_ref, outs, cols.start)
    inputs_back(dqkv_ref, doth_ref, wa_ref, base_ref, gs_ref, goth_ref)


def stack_kernel(*refs):
    *parts, out_ref, sems = refs
    for copy in pull([(part, out_ref.at[index]) for index, part in enumerate(parts)], sems):
        copy.wait()


def halves_kernel(by_y_ref, by_x_ref, low_ref, high_ref, sems):
    half = low_ref.shape[0]
    moves = [(by_y_ref.at[pl.ds(0, half)], low_ref), (by_x_ref.at[pl.ds(half, half)], high_ref)]
    for copy in pull(moves, sems):
        copy.wait()


def return_kernel(info_ref, out_ref, in_ref, back_ref, out_both_ref, in_both_ref):
    local, width = back_ref.shape[0], out_ref.shape[1]
    for own_ref, target, cols in (
        (out_ref, out_both_ref, slice(0, width)),
        (in_ref, in_both_ref, slice(width, 2 * width)),
    ):
        target[info_ref[1]] = own_ref[:local, :]
        target[1 - info_ref[1]] = back_ref[:, cols].astype(F32)


def send_kernel(own_ref, more_ref, out_ref, total_ref, back_ref):
    local, width = back_ref.shape[0], own_ref.shape[1]
    for part in chunks(own_ref.shape[0], ROWS):
        total = own_ref[part, :] + more_ref[part, :].astype(F32)
        total_ref[part, :] = total
        if part.start >= local:
            target = slice(part.start - local, part.stop - local)
            back_ref[target, :width] = out_ref[part, :].astype(BF16)
            back_ref[target, width:] = total.astype(BF16)


def add_core_kernel(keep_ref, got_ref, s11a_ref, s11b_ref, s10_ref, s01_ref, s00_ref):
    half = s11a_ref.shape[0]
    for z in range(keep_ref.shape[1]):
        for index, target in ((0, s00_ref), (1, s01_ref), (2, s10_ref)):
            total = keep_ref[index, z].astype(F32) + got_ref[index, z].astype(F32)
            target[z] = total.astype(BF16)
        total = (keep_ref[3, z].astype(F32) + got_ref[3, z].astype(F32)).astype(BF16)
        if z < half:
            s11a_ref[z] = total
        else:
            s11b_ref[z - half] = total


def beside(target_ref, z, values, rows, width):
    for index in range(values.shape[0] // rows):
        target_ref[z, :, index * width : (index + 1) * width] = values[index * rows : (index + 1) * rows]


def add_half_kernel(a10_ref, ax_ref, a01_ref, ay_ref, b10_ref, bx_ref, b01_ref, by_ref, o10_ref, o01_ref):
    half = ax_ref.shape[0]
    rows, width = b10_ref.shape[1], a10_ref.shape[2]
    at = a10_ref.shape[1] // rows * width
    for z in range(2 * half):
        for tall_ref, tall_got_ref, low_ref, got_ref, out_ref, first in (
            (a10_ref, ax_ref, b10_ref, bx_ref, o10_ref, 0),
            (a01_ref, ay_ref, b01_ref, by_ref, o01_ref, half),
        ):
            if first <= z < first + half:
                tall = (tall_ref[z].astype(F32) + tall_got_ref[z - first].astype(F32)).astype(BF16)
                low = (low_ref[z].astype(F32) + got_ref[z - first].astype(F32)).astype(BF16)
            else:
                tall, low = tall_ref[z], low_ref[z]
            beside(out_ref, z, tall, rows, width)
            out_ref[z, :, at:] = low


def add_both_kernel(info_ref, a_ref, b_ref, got_x_ref, got_y_ref, own_ref, near_ref, next_ref, far_ref):
    line = info_ref[0] // 8
    rows, width = b_ref.shape[1], a_ref.shape[2]
    count = a_ref.shape[1] // rows
    for z, out_ref in enumerate((own_ref, near_ref, next_ref, far_ref)):
        at = line ^ z
        for index in range(count + 1):
            if index < count:
                cols = slice(index * width, (index + 1) * width)
                own = a_ref[at, index * rows : (index + 1) * rows]
            else:
                cols = slice(count * width, got_x_ref.shape[2])
                own = b_ref[at]
            total = own.astype(F32) + got_x_ref[at, :, cols].astype(F32) + got_y_ref[at, :, cols].astype(F32)
            out_ref[:, cols] = total.astype(BF16)


def add_pair_kernel(own_ref, got_ref, sum_ref):
    sum_ref[...] = (own_ref[...].astype(F32) + got_ref[...].astype(F32)).astype(BF16)


def add_core_all_kernel(keep_ref, got_ref, *outs):
    for z in range(keep_ref.shape[1]):
        for index, target in enumerate(outs):
            target[z] = (keep_ref[index, z].astype(F32) + got_ref[index, z].astype(F32)).astype(BF16)


def add_four_kernel(info_ref, a_ref, b_ref, c_ref, d_ref, own_ref, near_ref, next_ref, far_ref):
    line = info_ref[0] // 8
    for z, out_ref in enumerate((own_ref, near_ref, next_ref, far_ref)):
        at = line ^ z
        total = a_ref[at].astype(F32) + b_ref[at].astype(F32) + c_ref[at].astype(F32)
        out_ref[...] = (total + d_ref[at].astype(F32)).astype(BF16)


def end_both_kernel(own_ref, got_ref, far_ref, tall_ref, win_ref, wo_ref, *rest):
    vectors, flip_ref = rest[:-1], rest[-1]
    rows, width = far_ref.shape[0], tall_ref.shape[1]

    def total(cols):
        return own_ref[:, cols].astype(F32) + got_ref[:, cols].astype(F32) + far_ref[:, cols].astype(F32)

    at = tall_ref.shape[0] // rows * width
    for index in range(tall_ref.shape[0] // rows):
        tall_ref[index * rows : (index + 1) * rows, :] = total(slice(index * width, (index + 1) * width))
    for out in (win_ref, wo_ref):
        out[...] = total(slice(at, at + out.shape[1]))
        at = at + out.shape[1]
    flip_ref[...] = jnp.zeros_like(flip_ref)
    flip_ref[:rows, :] = total(slice(at, at + LANES))
    turned = flip_ref[...].T
    for index, vector in enumerate(vectors):
        vector[...] = turned[index : index + 1, :rows]


def end_kernel(own_ref, got_ref, far_ref, *outs):
    at = 0
    for out in outs:
        cols = slice(at, at + out.shape[1])
        out[...] = own_ref[:, cols].astype(F32) + got_ref[:, cols].astype(F32) + far_ref[:, cols].astype(F32)
        at = at + out.shape[1]


def vm():
    return pl.BlockSpec(memory_space=pltpu.VMEM)


def run(kernel, ins, outs, scratch=(), scalars=(), loose=(), pinned=(), far=(), sems=0, micros=0.05):
    specs = [vm() for _ in ins]
    for index in scalars:
        specs[index] = pl.BlockSpec(memory_space=pltpu.SMEM)
    ins = list(ins)
    for index in loose:
        specs[index] = pl.BlockSpec(memory_space=pl.ANY)
    for index in pinned:
        specs[index] = pl.BlockSpec(memory_space=pltpu.HBM)
        ins[index] = pltpu.with_memory_space_constraint(ins[index], pltpu.HBM)
    size = sum(v.size * v.dtype.itemsize for v in ins) + sum(
        functools.reduce(lambda a, b: a * b, s, 1) * jnp.dtype(t).itemsize for s, t in outs
    )
    buffers = [pltpu.VMEM(s, t) for s, t in scratch]
    need = sum(functools.reduce(lambda a, b: a * b, s, 1) * jnp.dtype(t).itemsize for s, t in scratch)
    if sems:
        buffers.append(pltpu.SemaphoreType.DMA((sems,)))
    return pl.pallas_call(
        kernel,
        out_shape=[jax.ShapeDtypeStruct(s, t) for s, t in outs],
        in_specs=specs,
        out_specs=[pl.BlockSpec(memory_space=pl.ANY) if index in far else vm() for index in range(len(outs))],
        scratch_shapes=buffers,
        compiler_params=pltpu.CompilerParams(vmem_limit_bytes=max(need + 8 * MIB, SCOPED)),
        cost_estimate=pl.CostEstimate(
            flops=int(micros * MICRO), bytes_accessed=size, transcendentals=0
        ),
    )(*ins)


AXES = ("dp", "head")


def after(value, *others):
    return lax.optimization_barrier((value, *others))[0]


class Links:
    def __init__(self, model_rows):
        self.heads = lax.axis_size("head")
        self.pods = lax.axis_size("dp")
        self.count = self.heads * self.pods
        self.fast = self.heads == 4 and self.pods == 8 and model_rows == 16
        self.head = lax.axis_index("head")
        self.me = lax.axis_index("dp") * self.heads + self.head

    def flip(self, value, bit):
        return lax.ppermute(value, AXES, [(i, i ^ bit) for i in range(self.count)])

    def flip_head(self, value, bit):
        return lax.ppermute(value, "head", [(i, i ^ bit) for i in range(self.heads)])

    def along_z(self, block):
        return [block, *(self.flip(block, 8 * k) for k in (1, 2, 3))]

    def stack(self, parts):
        (out,) = run(
            stack_kernel, parts, [((4, *parts[0].shape), BF16)], loose=range(4), far=(0,), sems=4
        )
        return out

    def core_sums(self, keep, got):
        block = keep.shape[2:]
        whole, half = ((4, *block), BF16), ((2, *block), BF16)
        return run(add_core_kernel, [keep, got], [half, half, whole, whole, whole])

    def line_first(self, kernel, parts, shape):
        own, near, following, far = run(kernel, [self.info, *parts], [(shape, BF16)] * 4, scalars=(0,))
        return own, far, self.flip(near, 8), self.flip(following, 8)

    def line_last(self, own, far, got, got_far):
        (far,) = run(add_pair_kernel, [after(far, got), got_far], [(far.shape, BF16)])
        return own, got, self.flip(far, 24)

    def spread(self, own, group):
        held, bit = own[None], 1
        while bit < group:
            got = self.flip_head(held, bit)
            held = got if bit == 1 and group == 2 else jnp.concatenate([held, got], axis=0)
            bit = bit * 2
        if group > 2:
            held = held[1:]
        return held.reshape(-1, own.shape[1])

    def collapse(self, parts, group, rows):
        if group == 2:
            return self.flip_head(parts, 1)
        held = parts.reshape(group - 1, rows, -1)
        held = jnp.concatenate([jnp.zeros_like(held[:1]), held], axis=0).astype(F32)
        bit = group // 2
        while bit >= 1:
            held = held[:bit] + self.flip_head(held[bit : 2 * bit], bit)
            bit = bit // 2
        return held[0]


def body(
    tokens, cotangent, lengths, halting, w_query, w_key, w_value, w_out, w_in, w_hidden,
    w_halt, gain_attn, shift_attn, gain_ffn, shift_ffn,
):
    micro, local, width = tokens.shape
    links = Links(w_query.shape[0])
    fast, heads = links.fast, links.heads
    group = heads // micro
    rows, length = micro * local, local * heads
    mine = links.head // group
    wide_ff = w_in.shape[1]
    fine = width // links.count
    matrices = (w_query, w_key, w_value, w_out, w_in, w_hidden)
    vectors = (w_halt, gain_attn, shift_attn, gain_ffn, shift_ffn)
    place_array = jnp.stack([links.me, mine, links.head % group, jnp.int32(group)]).astype(jnp.int32)
    links.info = place_array

    pairs = width // LANES
    row_f, row_b = ((rows, width), F32), ((rows, width), BF16)
    stat = ((rows, LANES), F32)
    others = length - rows
    long_b = ((length, width), BF16)
    q2_t = ((pairs, 2 * rows, LANES), BF16)
    p_t = ((pairs, 2 * rows, length), BF16)
    o_t = ((2 * rows, LANES), F32)
    bias_t = ((rows, length), F32)
    inner_t = ((rows, BLOCK), F32)
    ff_b = ((rows, wide_ff), BF16)
    sums_t = ((VECS, 8, width), F32)
    ds_t = ((2 * rows, length), BF16)
    dqkv_t = ((rows, 3 * width), BF16)
    doth_t = ((others, 2 * width), BF16)
    vg_t = ((8, width), F32)
    segq_t, segk_t = ((rows, LANES), jnp.int32), ((8, length), jnp.int32)

    sort_in = [place_array, tokens, cotangent, halting]
    sort_out = [((local, 2 * width + LANES), BF16)] * 2
    sort_tmp = [((LANES, local), F32), (halting.shape, jnp.int32)]
    if fast:
        send_tok, own_tok, block_a, block_b = run(
            pack_kernel,
            [*sort_in, *matrices, *(vector[None] for vector in vectors)],
            [*sort_out, ((5, fine, BLOCK), BF16), ((8, fine, BLOCK), BF16)],
            [*sort_tmp, ((LANES, LANES), F32), ((VECS, 1, fine), BF16)],
            scalars=(0,),
            pinned=range(1, 15),
            sems=22,
        )
        got_tok = links.flip_head(send_tok, group)
        line_a = links.along_z(block_a)
        own_a = after(links.stack(line_a), got_tok)
        by_x, by_y = links.flip(own_a, 2), links.flip(own_a, 4)
        line_b = links.along_z(after(block_b, line_a[1]))
        plane_a = [own_a, by_x, by_y, links.flip(after(by_y, line_b[3]), 2)]
    else:
        send_tok, own_tok = run(
            sort_kernel, sort_in, sort_out, sort_tmp, scalars=(0,), pinned=(1, 2, 3), sems=5
        )
        full = [lax.all_gather(part, AXES, axis=0, tiled=True) for part in matrices]
        full_v = [lax.all_gather(part, AXES, axis=0, tiled=True) for part in vectors]
        full_a = jnp.stack(full[:4])
        full_in = jnp.transpose(full[4].reshape(width, wide_ff // BLOCK, BLOCK), (1, 0, 2))
        full_hid = full[5]
        vec = jnp.pad(jnp.stack(full_v), ((0, 8 - VECS), (0, 0))).astype(F32)

        got_tok = links.flip_head(send_tok, group)
    tok, x0, rown0, sig1, segq, segk = run(
        embed_kernel,
        [place_array, lengths[:, 0], own_tok, got_tok],
        [((rows, 2 * width + LANES), BF16), row_f, row_b, row_f, segq_t, segk_t],
        scalars=(0, 1),
    )
    roth0 = links.spread(rown0, group)
    if fast:
        own_b = after(links.stack(line_b), by_x, by_y, roth0)
        near = [own_b, links.flip(own_b, 2), links.flip(own_b, 4)]
        near = near + [links.flip(piece, 1) for piece in near]
        halves = run(
            halves_kernel,
            [near[2], near[1]],
            [((2, 8, fine, BLOCK), BF16)] * 2,
            loose=(0, 1),
            far=(0, 1),
            sems=2,
        )
        far_b = [links.flip(halves[0], 2), links.flip(halves[1], 4)]
        plane_a[3] = after(plane_a[3], halves[0])
        plane_a = plane_a + [links.flip(piece, 1) for piece in plane_a]

    attend_in = [rown0, roth0, segq, segk]
    attend_out = [q2_t, long_b, long_b, p_t, row_b]
    if fast:
        full_a, vec, q2, k, v, p, ctx = run(
            functools.partial(attend_kernel, True),
            [*attend_in, links.info, *plane_a],
            [((5, 4, 8, fine, BLOCK), BF16), vg_t, *attend_out],
            [row_b, bias_t, o_t],
            scalars=(4,),
            micros=8,
        )
        full_a = full_a.reshape(5, width, BLOCK)
    else:
        q2, k, v, p, ctx = run(
            functools.partial(attend_kernel, False),
            [*attend_in, full_a],
            attend_out,
            [row_b, bias_t, o_t],
            micros=8,
        )
    ffn_out = [row_f, stat, row_b, ff_b, ff_b, row_f, stat, stat, row_f, row_f, row_f, row_b]
    ffn_in = [x0, ctx, tok, sig1, vec, full_a]
    if fast:
        far_b = [after(piece, ctx) for piece in far_b]
        far_b = far_b + [links.flip(piece, 1) for piece in far_b]
        full_in, full_hid, *got = run(
            functools.partial(ffn_kernel, True),
            [*ffn_in, links.info, *near, *far_b],
            [((4, 4, 8, fine, BLOCK), BF16), ((4, 8, 4, fine, BLOCK), BF16), *ffn_out],
            [inner_t, row_f],
            scalars=(6,),
            micros=5.5,
        )
        full_in = full_in.reshape(4, width, BLOCK)
        full_hid = full_hid.reshape(wide_ff, width)
    else:
        got = run(
            functools.partial(ffn_kernel, False),
            [*ffn_in, full_in, full_hid],
            ffn_out,
            [inner_t, row_f],
            micros=5.5,
        )
    n1, r1, nlow, hid, dg, n2, r2, rate, state, pooled, x1, rown1 = got
    roth1 = links.spread(rown1, group)
    out, gs, goth, nlow1, hid1, b11, b21, ctx1, b01, dqkv1, doth1, vg1 = run(
        turn_kernel,
        [x1, rown1, roth1, full_a, full_in, full_hid, vec, segq, segk, state, pooled, tok],
        [row_f, row_f, ((others, width), BF16), row_b, ff_b, ff_b, row_b, row_b, row_b, dqkv_t, doth_t, vg_t],
        [
            row_b, q2_t, long_b, long_b, p_t, bias_t, o_t, row_f, row_f, stat, inner_t, ff_b,
            row_f, stat, stat, row_f, row_f, sums_t, row_b, q2_t, ds_t,
        ],
        micros=15.7,
    )
    more = links.collapse(goth, group, rows)

    b_cols = wide_ff + width + LANES
    def parts_of(shape, whole):
        return [((4, 4, *shape), BF16)] * 2 if fast else [(whole, F32)]

    hid_out = parts_of((4 * fine, width), (wide_ff, width))
    in_out = parts_of((fine, b_cols), (width, b_cols))
    attend_outs = parts_of((fine, 3 * width), (width, 3 * width))
    whole_shape = (4, 8, fine, BLOCK) if fast else (8, LANES)
    tall_shape = (8, 4 * fine, width) if fast else (8, LANES)
    b2, gsec, base, sums, *hid_parts = run(
        functools.partial(hidden_back_kernel, fast),
        [links.info, gs, more, tok, vec, n2, r2, rate, hid, hid1, b21],
        [row_b, row_f, row_f, sums_t, *hid_out],
        [(tall_shape, F32)],
        scalars=(0,),
        micros=2,
    )
    b1, b0, base, gctx, sums = run(
        feed_back_kernel,
        [b2, gsec, base, sums, vec, full_in, full_hid, full_a, n1, r1, dg],
        [ff_b, row_b, row_f, row_b, sums_t],
        [inner_t, row_f],
        micros=2.2,
    )
    if fast:
        c_sums = links.core_sums(hid_parts[0], links.flip(hid_parts[1], 1))
        b1 = after(b1, c_sums[0])
    in_parts = run(
        functools.partial(weights_back_kernel, fast),
        [links.info, b1, b0, sums, nlow, ctx, nlow1, b11, ctx1, b01, vg1],
        in_out,
        [(whole_shape, F32), ((LANES, width), F32)],
        scalars=(0,),
        micros=2,
    )
    if fast:
        b_sums = links.core_sums(in_parts[0], links.flip(in_parts[1], 1))
        gctx = after(gctx, b_sums[0])
    dqkv0, doth0 = run(
        heads_back_kernel,
        [gctx, q2, k, v, p, ctx],
        [dqkv_t, doth_t],
        [q2_t, ds_t, o_t],
        micros=3,
    )
    if fast:
        c11a, c11b, c10, c01, c00 = c_sums
        b11a, b11b, b10, b01, b00 = b_sums
        halves = [
            after(c10, dqkv0), links.flip(c11a, 2), c01, links.flip(c11b, 4),
            b10, links.flip(b11a, 2), b01, links.flip(b11b, 4),
        ]
        both_t = ((4, fine, 4 * width + b_cols), BF16)
        both10, both01 = run(add_half_kernel, halves, [both_t] * 2)
        dqkv0 = after(dqkv0, both01)
    g0, goth0, *attend_parts = run(
        functools.partial(project_back_kernel, fast),
        [links.info, base, full_a, rown0, roth0, rown1, roth1, dqkv1, doth1, dqkv0, doth0],
        [row_f, ((others, width), BF16), *attend_outs],
        [(whole_shape, F32)],
        scalars=(0,),
        micros=4,
    )
    inputs, back = run(
        send_kernel,
        [g0, links.collapse(goth0, group, rows), out],
        [row_f, ((local, 2 * width), BF16)],
    )
    if fast:
        keep, got = after(attend_parts[0], back), links.flip(attend_parts[1], 1)
        a00, a01, a10, a11 = run(add_core_all_kernel, [keep, got], [(keep.shape[1:], BF16)] * 4)
        by_plane = [a00, links.flip(a11, 6), links.flip(a01, 2), links.flip(a10, 4)]
        both = links.line_first(
            add_both_kernel, [after(c00, a00), b00, links.flip(both01, 2), links.flip(both10, 4)], both_t[0][1:]
        )
        first_sums = both[0]
        by_plane[0] = after(by_plane[0], both[0])
        attend_sums = links.line_first(add_four_kernel, by_plane, a00.shape[1:])
        both = links.line_last(both[0], after(both[1], attend_sums[0]), *both[2:])
        attend_sums = links.line_last(*attend_sums)
        back = after(back, first_sums)
        output, input_grad = run(
            return_kernel,
            [links.info, out, inputs, links.flip_head(back, group)],
            [((micro, local, width), F32)] * 2,
            scalars=(0,),
        )
        g_hidden, g_in, g_out, *g_vectors = run(
            end_both_kernel,
            [after(both[0], output), *both[1:]],
            [((4 * fine, width), F32), ((fine, wide_ff), F32), ((fine, width), F32)] + [((1, fine), F32)] * VECS,
            [((LANES, LANES), F32)],
        )
        g_query, g_key, g_value = run(
            end_kernel,
            [after(attend_sums[0], output, g_hidden), *attend_sums[1:]],
            [((fine, width), F32)] * 3,
        )
        g_vectors = [vector.reshape(fine) for vector in g_vectors]
    else:
        sums = [
            *(attend_parts[0][:, index * width : (index + 1) * width] for index in range(3)),
            in_parts[0][:, wide_ff : wide_ff + width], in_parts[0][:, :wide_ff], hid_parts[0],
            in_parts[0][:, wide_ff + width :],
        ]
        sums = [lax.psum_scatter(part, AXES, scatter_dimension=0, tiled=True) for part in sums]
        g_query, g_key, g_value, g_out, g_in, g_hidden, g_vec = sums
        g_vectors = [g_vec[:, index] for index in range(VECS)]
        output, input_grad = run(
            return_kernel,
            [links.info, out, inputs, links.flip_head(back, group)],
            [((micro, local, width), F32)] * 2,
            scalars=(0,),
        )
    return (output, input_grad, g_query, g_key, g_value, g_out, g_in, g_hidden, *g_vectors)


def solution(mesh):
    whole = P(("dp", "head"))
    matrix = P(("dp", "head"), None)
    rows = P(None, ("dp", "head"), None)
    return jax.shard_map(
        body,
        mesh=mesh,
        in_specs=(rows, rows, P(None, "dp", None), P(None, None, ("dp", "head")))
        + (matrix,) * 6
        + (whole,) * 5,
        out_specs=(rows, rows) + (matrix,) * 6 + (whole,) * 5,
        check_vma=False,
    )
```

```python
import functools

import jax
import jax.numpy as jnp
from jax import lax
from jax.experimental import pallas as pl
from jax.experimental.pallas import tpu as pltpu
from jax.sharding import PartitionSpec as P

HD = 64
EPSILON = 1e-06
F32 = jnp.float32
BF16 = jnp.bfloat16
LANES = 128
ROWS = 32
ATT_ROWS = 256
BLOCK = 512
VECS = 5
MIB = 1024 * 1024
SCOPED = 20 * MIB
MICRO = 1.15e9
GELU_A = 0.7978845608028654
GELU_B = 0.044715


def dot(a, b, ca=1, cb=0):
    return lax.dot_general(a, b, (((ca,), (cb,)), ((), ())), preferred_element_type=F32)


def chunks(total, size):
    size = min(size, total)
    return [slice(i, i + size) for i in range(0, total, size)]


def wide(column):
    return jnp.broadcast_to(column, (column.shape[0], LANES))


def mean(values):
    return jnp.sum(values, axis=-1, keepdims=True) * (1.0 / values.shape[-1])


def fold(values):
    return jnp.sum(values.reshape(values.shape[0] // 8, 8, values.shape[1]), axis=0)


class Flat:
    def __init__(self, ref):
        self.ref = ref

    def __getitem__(self, index):
        if index is Ellipsis:
            index = (slice(None), slice(None))
        value = self.ref[..., index[1]]
        return value.reshape(-1, value.shape[-1])[index[0]]


def matrix(ref, index):
    value = ref[index]
    return value.reshape(-1, value.shape[-1])


def head_mask(rows):
    lane = lax.broadcasted_iota(jnp.int32, (rows, LANES), 1)
    return lane < HD


def normalize(values):
    center = values - mean(values)
    inverse = lax.rsqrt(mean(center * center) + EPSILON)
    return center * inverse, inverse


def normalize_back(unit, inverse, grad):
    return inverse * (grad - mean(grad) - unit * mean(grad * unit))


def split_heads(values_ref, stacked_ref):
    rows = values_ref.shape[0]
    for part in chunks(rows, ATT_ROWS):
        first = head_mask(part.stop - part.start)
        for pair in range(stacked_ref.shape[0]):
            block = values_ref[part, pair * LANES : (pair + 1) * LANES].astype(F32)
            stacked_ref[pair, part, :] = jnp.where(first, block, 0.0).astype(BF16)
            stacked_ref[pair, rows + part.start : rows + part.stop, :] = jnp.where(
                first, 0.0, block
            ).astype(BF16)


def project(rown_ref, roth_ref, wa_ref, q_ref, q2_ref, k_ref, v_ref):
    rows, width = rown_ref.shape
    q_ref[...] = (
        dot(rown_ref[...], matrix(wa_ref, 0)).astype(BF16).astype(F32) * HD**-0.5
    ).astype(BF16)
    split_heads(q_ref, q2_ref)
    for at, source in ((0, rown_ref), (rows, roth_ref)):
        span = slice(at, at + source.shape[0])
        k_ref[span, :] = dot(source[...], matrix(wa_ref, 1)).astype(BF16)
        v_ref[span, :] = dot(source[...], matrix(wa_ref, 2)).astype(BF16)


def set_bias(segq_ref, segk_ref, bias_ref):
    for part in chunks(bias_ref.shape[0], ROWS):
        bias_ref[part, :] = jnp.where(segq_ref[part, 0:1] == segk_ref[0:1, :], 0.0, -1e30)


def attend(q2_ref, k_ref, v_ref, bias_ref, p_ref, ctx_ref, o_ref):
    rows, length = bias_ref.shape
    for pair in range(q2_ref.shape[0]):
        cols = slice(pair * LANES, (pair + 1) * LANES)
        for part in chunks(2 * rows, 2 * rows):
            scores = dot(q2_ref[pair, part, :], k_ref[:, cols], 1, 1)
            scores = (scores.reshape(2, rows, length) + bias_ref[...][None]).reshape(2 * rows, length)
            weights = jnp.exp(scores - jnp.max(scores, axis=-1, keepdims=True))
            inverse = 1.0 / jnp.sum(weights, axis=-1, keepdims=True)
            low = (weights * inverse).astype(BF16)
            p_ref[pair, part, :] = low
            o_ref[part, :] = dot(low, v_ref[:, cols])
        for part in chunks(rows, ATT_ROWS):
            first = head_mask(part.stop - part.start)
            second = o_ref[rows + part.start : rows + part.stop, :]
            ctx_ref[part, cols] = jnp.where(first, o_ref[part, :], second).astype(BF16)


def first_norm(x_ref, ctx_ref, wa_ref, vec_ref, acc_ref, n1_ref, r1_ref, nlow_ref):
    acc_ref[...] = dot(ctx_ref[...], matrix(wa_ref, 3))
    for part in chunks(x_ref.shape[0], ROWS):
        unit, inverse = normalize(x_ref[part, :] + acc_ref[part, :])
        n1_ref[part, :] = unit
        r1_ref[part, :] = wide(inverse)
        nlow_ref[part, :] = (unit * vec_ref[1:2, :] + vec_ref[2:3, :]).astype(BF16)


def feed_forward(nlow_ref, win_ref, whid_ref, inner_ref, hid_ref, dg_ref, acc_ref):
    rows = nlow_ref.shape[0]
    for cols in chunks(hid_ref.shape[1], BLOCK):
        inner_ref[...] = dot(nlow_ref[...], matrix(win_ref, cols.start // BLOCK))
        for part in chunks(rows, ROWS):
            x = inner_ref[part, :]
            square = x * x
            t = jnp.tanh(x * (GELU_A + GELU_A * GELU_B * square))
            half = 0.5 + 0.5 * t
            hid_ref[part, cols] = (x * half).astype(BF16)
            slope = 0.5 * x * (1.0 - t * t) * (GELU_A + 3.0 * GELU_A * GELU_B * square)
            dg_ref[part, cols] = (half + slope).astype(BF16)
    acc_ref[...] = dot(hid_ref[...], whid_ref[...])


def second_norm(part, vec_ref, n1_ref, acc_ref):
    normed = n1_ref[part, :] * vec_ref[1:2, :] + vec_ref[2:3, :]
    unit, inverse = normalize(normed + acc_ref[part, :])
    updated = unit * vec_ref[3:4, :] + vec_ref[4:5, :]
    rate = jax.nn.sigmoid(jnp.sum(updated * vec_ref[0:1, :], axis=-1, keepdims=True))
    return unit, inverse, updated, rate


def tail_back(
    part, step, gs, gp, halt_ref, vec_ref, n2_ref, r2_ref, rate_ref, b2_ref, gsec_ref, base_ref, sums_ref
):
    width = n2_ref.shape[1]
    keep = halt_ref[part, 2 * width + step : 2 * width + step + 1].astype(F32)
    unit = n2_ref[part, :]
    updated = unit * vec_ref[3:4, :] + vec_ref[4:5, :]
    rate = rate_ref[part, 0:1]
    logit = keep * jnp.sum(gp * updated, axis=-1, keepdims=True) * rate * (1.0 - rate)
    grad = keep * gs + (keep * rate) * gp + logit * vec_ref[0:1, :]
    base_ref[part, :] = gs - keep * gs
    sums_ref[0] += fold(logit * updated)
    sums_ref[3] += fold(grad * unit)
    sums_ref[4] += fold(grad)
    back = normalize_back(unit, r2_ref[part, 0:1], grad * vec_ref[3:4, :])
    gsec_ref[part, :] = back
    b2_ref[part, :] = back.astype(BF16)


def feed_back(b2_ref, dg_ref, win_ref, whid_ref, inner_ref, b1_ref, acc_ref):
    rows = b2_ref.shape[0]
    for cols in chunks(dg_ref.shape[1], BLOCK):
        inner_ref[...] = dot(b2_ref[...], whid_ref[cols, :], 1, 1)
        for part in chunks(rows, ROWS):
            b1_ref[part, cols] = (inner_ref[part, :] * dg_ref[part, cols].astype(F32)).astype(BF16)
    total = None
    for cols in chunks(dg_ref.shape[1], BLOCK):
        value = dot(b1_ref[:, cols], matrix(win_ref, cols.start // BLOCK), 1, 1)
        total = value if total is None else total + value
    acc_ref[...] = total


def middle_back(gsec_ref, acc_ref, vec_ref, n1_ref, r1_ref, b0_ref, base_ref, sums_ref):
    for part in chunks(gsec_ref.shape[0], ROWS):
        grad = gsec_ref[part, :] + acc_ref[part, :]
        unit = n1_ref[part, :]
        sums_ref[1] += fold(grad * unit)
        sums_ref[2] += fold(grad)
        back = normalize_back(unit, r1_ref[part, 0:1], grad * vec_ref[1:2, :])
        base_ref[part, :] += back
        b0_ref[part, :] = back.astype(BF16)


def attend_back(
    pairs, g2_ref, q2_ref, k_ref, v_ref, p_ref, ctx_ref, ds_ref, dq2_ref, dqkv_ref, doth_ref
):
    rows, width = ctx_ref.shape
    for pair in pairs:
        cols = slice(pair * LANES, (pair + 1) * LANES)
        for part in chunks(2 * rows, 2 * rows):
            grad = g2_ref[pair, part, :]
            both = jnp.concatenate([ctx_ref[:, cols]] * 2, axis=0)
            delta = jnp.sum(grad.astype(F32) * both.astype(F32), axis=-1, keepdims=True)
            back = dot(grad, v_ref[:, cols], 1, 1)
            low = (p_ref[pair, part, :].astype(F32) * (back - delta)).astype(BF16)
            ds_ref[part, :] = low
            dq2_ref[part, :] = dot(low, k_ref[:, cols])
        for part in chunks(rows, ATT_ROWS):
            first = head_mask(part.stop - part.start)
            second = dq2_ref[rows + part.start : rows + part.stop, :]
            dqkv_ref[part, cols] = (
                jnp.where(first, dq2_ref[part, :], second) * HD**-0.5
            ).astype(BF16)
        for index, (left, right) in enumerate(
            ((ds_ref[...], q2_ref[pair]), (p_ref[pair], g2_ref[pair]))
        ):
            both = dot(right, left, 0, 0).T.astype(BF16)
            at = index * width + pair * LANES
            dqkv_ref[:, width + at : width + at + LANES] = both[:rows]
            doth_ref[:, at : at + LANES] = both[rows:]


def inputs_back(dqkv_ref, doth_ref, wa_ref, base_ref, gs_ref, goth_ref):
    width = base_ref.shape[1]
    parts = [slice(index * width, (index + 1) * width) for index in range(3)]
    total = base_ref[...]
    for index, cols in enumerate(parts):
        total = total + dot(dqkv_ref[:, cols], matrix(wa_ref, index), 1, 1)
    gs_ref[...] = total
    total = dot(doth_ref[:, parts[0]], matrix(wa_ref, 1), 1, 1)
    goth_ref[...] = (total + dot(doth_ref[:, parts[1]], matrix(wa_ref, 2), 1, 1)).astype(BF16)


def fetch(pieces, cores, bits, start, store, me_ref):
    line, place_in = me_ref[0] // 8, me_ref[0] % 8
    for piece, core, bit in zip(pieces, cores, bits):
        for z in range(piece.shape[0]):
            store(piece, z, line ^ (start + z), place_in ^ (bit | core))


def embed_kernel(place_ref, sizes_ref, tok_ref, got_ref, own_ref, x_ref, rown_ref, sig_ref, segq_ref, segk_ref):
    mine, place_in, group = place_ref[1], place_ref[2], place_ref[3]
    local = tok_ref.shape[0]
    half = x_ref.shape[1] // 2
    ends, starts, total = [], [], 0
    for index in range(sizes_ref.shape[1]):
        starts.append(total)
        total = total + sizes_ref[mine, index]
        ends.append(total)
    ones = jnp.exp(
        lax.broadcasted_iota(jnp.int32, (8, half), 1).astype(F32)
        * (-jnp.log(jnp.full((8, half), 10000.0, F32)) / max(half - 1, 1))
    )
    rates = ones[0:1, :]
    first_sin, first_cos = jnp.sin(rates), jnp.cos(rates)
    for part in chunks(x_ref.shape[0], ROWS):
        size = part.stop - part.start
        block = mine * group + place_in
        block = block if part.start < local else block ^ group
        at = block * local + part.start % local
        token = at + lax.broadcasted_iota(jnp.int32, (size, LANES), 0)
        segment = jnp.zeros((size, LANES), jnp.int32)
        begin = jnp.zeros((size, LANES), jnp.int32)
        for start, end in zip(starts, ends):
            segment = segment + jnp.where(token >= end, 1, 0)
            begin = jnp.maximum(begin, jnp.where(token >= start, start, 0))
        segq_ref[part, :] = segment
        angles = (token - begin).astype(F32)[:, 0:1] * rates
        if part.start < local:
            low = tok_ref[part, :]
        else:
            low = got_ref[part.start - local : part.stop - local, :]
        own_ref[part, :] = low
        for cols, moving, still, step in (
            (slice(0, half), jnp.sin(angles), 0.0, first_sin),
            (slice(half, 2 * half), jnp.cos(angles), 1.0, first_cos),
        ):
            inputs = low[:, cols].astype(F32) + (moving + still)
            x_ref[part, cols] = inputs
            rown_ref[part, cols] = inputs.astype(BF16)
            sig_ref[part, cols] = moving + step
    blocks = segk_ref.shape[1] // local
    for index in range(blocks):
        peer = mine * group + (place_in ^ (index // 2))
        peer = peer if index % 2 == 0 else peer ^ group
        token = peer * local + lax.broadcasted_iota(jnp.int32, (8, local), 1)
        segment = jnp.zeros((8, local), jnp.int32)
        for end in ends:
            segment = segment + jnp.where(token >= end, 1, 0)
        segk_ref[:, index * local : (index + 1) * local] = segment


def pull(sources, sems):
    copies = [
        pltpu.make_async_copy(source, target, sems.at[index]) for index, (source, target) in enumerate(sources)
    ]
    for copy in copies:
        copy.start()
    return copies


def sort_rows(place_ref, tok_ref, cot_ref, halt_ref, refs, sems):
    mine = place_ref[1]
    width = tok_ref.shape[2]
    send_ref, own_ref, flip_ref, flags_ref = refs
    moves = [(halt_ref, flags_ref)]
    for micro, target in ((1 - mine, send_ref), (mine, own_ref)):
        moves.append((tok_ref.at[micro], target.at[:, :width]))
        moves.append((cot_ref.at[micro], target.at[:, width : 2 * width]))
    copies = pull(moves, sems)
    flip_ref[...] = jnp.zeros_like(flip_ref)
    for copy in copies:
        copy.wait()
    for target, micro in ((own_ref, mine), (send_ref, 1 - mine)):
        for step in range(halt_ref.shape[0]):
            flip_ref[step : step + 1, :] = flags_ref[step, pl.ds(micro, 1), :].astype(F32)
        target[:, 2 * width :] = flip_ref[...].T.astype(BF16)


def sort_kernel(place_ref, tok_ref, cot_ref, halt_ref, *refs):
    sort_rows(place_ref, tok_ref, cot_ref, halt_ref, refs[:4], refs[4])


def pack_kernel(place_ref, tok_ref, cot_ref, halt_ref, q_ref, k_ref, v_ref, o_ref, win_ref, whid_ref, *rest):
    vectors, rest = rest[:VECS], rest[VECS:]
    sorted_refs, (block_ref, tall_ref, flip_ref, flags_ref, turn_ref, low_ref, sems) = rest[:2], rest[2:]
    rows, width = q_ref.shape
    moves = [(vector, low_ref.at[index]) for index, vector in enumerate(vectors)]
    lanes = width // LANES
    for index, source in enumerate((q_ref, k_ref, v_ref, o_ref)):
        for part in range(lanes):
            cols = slice(part * LANES, (part + 1) * LANES)
            moves.append((source.at[:, cols], block_ref.at[index * lanes + part]))
    for index in range(4):
        moves.append((win_ref.at[:, index * BLOCK : (index + 1) * BLOCK], tall_ref.at[index]))
        moves.append((whid_ref.at[index * rows : (index + 1) * rows, :], tall_ref.at[4 + index]))
    count = len(moves)
    copies = pull(moves, sems.at[:count])
    sort_rows(place_ref, tok_ref, cot_ref, halt_ref, [*sorted_refs, flip_ref, flags_ref], sems.at[count:])
    turn_ref[...] = jnp.zeros_like(turn_ref)
    for copy in copies:
        copy.wait()
    for index in range(VECS):
        turn_ref[index : index + 1, :rows] = low_ref[index].astype(F32)
    block_ref[4 * lanes] = turn_ref[...].T[:rows, :].astype(BF16)


def attend_kernel(
    fast, rown_ref, roth_ref, segq_ref, segk_ref, *rest,
):
    if fast:
        me_ref, plane, rest = rest[0], rest[1:9], rest[9:]
        wa_ref, vec_ref, q2_ref, k_ref, v_ref, p_ref, ctx_ref, q_ref, bias_ref, o_ref = rest

        def store(piece, z, line, place):
            lanes = wa_ref.shape[4] // LANES
            for chunk in range(piece.shape[1]):
                cols = slice(chunk % lanes * LANES, (chunk % lanes + 1) * LANES)
                wa_ref[chunk // lanes, line, place, :, cols] = piece[z, chunk]

        fetch(plane, (0, 0, 0, 0, 1, 1, 1, 1), (0, 2, 4, 6) * 2, 0, store, me_ref)
        vec_ref[...] = matrix(wa_ref, 4)[:, :LANES].astype(F32).T[0:8, :]
    else:
        wa_ref, q2_ref, k_ref, v_ref, p_ref, ctx_ref, q_ref, bias_ref, o_ref = rest
    set_bias(segq_ref, segk_ref, bias_ref)
    project(rown_ref, roth_ref, wa_ref, q_ref, q2_ref, k_ref, v_ref)
    attend(q2_ref, k_ref, v_ref, bias_ref, p_ref, ctx_ref, o_ref)


def norm_kernel(x_ref, ctx_ref, vec_ref, wa_ref, n1_ref, r1_ref, nlow_ref, acc_ref):
    first_norm(x_ref, ctx_ref, wa_ref, vec_ref, acc_ref, n1_ref, r1_ref, nlow_ref)


def ffn_kernel(fast, n1_ref, nlow_ref, tok_ref, sig_ref, vec_ref, *rest):
    if fast:
        me_ref, near, far, rest = rest[0], rest[1:7], rest[7:11], rest[11:]
        (win_ref, full_ref), rest = rest[:2], rest[2:]
    else:
        (win_ref, whid_ref), rest = rest[:2], rest[2:]
    (
        hid_ref, dg_ref, n2_ref, r2_ref, rate_ref, state_ref, pooled_ref, next_ref, rown_ref,
        inner_ref, acc_ref,
    ) = rest
    if fast:

        def store(piece, z, line, place):
            for chunk in range(4):
                win_ref[chunk, line, place] = piece[z, chunk]
                full_ref[line, place, chunk] = piece[z, 4 + chunk]

        fetch(near, (0, 0, 0, 1, 1, 1), (0, 2, 4, 0, 2, 4), 0, store, me_ref)
        fetch((far[0], far[2]), (0, 1), (6, 6), 0, store, me_ref)
        fetch((far[1], far[3]), (0, 1), (6, 6), 2, store, me_ref)
        whid_ref = Flat(full_ref)
    width = n1_ref.shape[1]
    feed_forward(nlow_ref, win_ref, whid_ref, inner_ref, hid_ref, dg_ref, acc_ref)
    for part in chunks(tok_ref.shape[0], ROWS):
        unit, inverse, updated, rate = second_norm(part, vec_ref, n1_ref, acc_ref)
        keep = tok_ref[part, 2 * width : 2 * width + 1].astype(F32)
        n2_ref[part, :] = unit
        r2_ref[part, :] = wide(inverse)
        rate_ref[part, :] = wide(rate)
        pooled_ref[part, :] = (keep * rate) * updated
        state = tok_ref[part, :width].astype(F32)
        state = state + keep * (updated - state)
        state_ref[part, :] = state
        inputs = state + sig_ref[part, :]
        next_ref[part, :] = inputs
        rown_ref[part, :] = inputs.astype(BF16)


def turn_kernel(
    x_ref, rown_ref, roth_ref, wa_ref, win_ref, whid_ref, vec_ref, segq_ref, segk_ref,
    state_ref, pooled_ref, tok_ref,
    out_ref, gs_ref, goth_ref, nlow_ref, hid_ref, b1_ref, b2_ref, ctx_ref, b0_ref, dqkv_ref, doth_ref, vg_ref,
    q_ref, q2_ref, k_ref, v_ref, p_ref, bias_ref, o_ref, acc_ref, n1_ref, r1_ref, inner_ref, dg_ref,
    n2_ref, r2_ref, rate_ref, gsec_ref, base_ref, sums_ref, gctx_ref, g2_ref, ds_ref,
):
    width = x_ref.shape[1]
    sums_ref[...] = jnp.zeros_like(sums_ref)
    set_bias(segq_ref, segk_ref, bias_ref)
    project(rown_ref, roth_ref, wa_ref, q_ref, q2_ref, k_ref, v_ref)
    attend(q2_ref, k_ref, v_ref, bias_ref, p_ref, ctx_ref, o_ref)
    first_norm(x_ref, ctx_ref, wa_ref, vec_ref, acc_ref, n1_ref, r1_ref, nlow_ref)
    feed_forward(nlow_ref, win_ref, whid_ref, inner_ref, hid_ref, dg_ref, acc_ref)
    for part in chunks(x_ref.shape[0], ROWS):
        unit, inverse, updated, rate = second_norm(part, vec_ref, n1_ref, acc_ref)
        keep = tok_ref[part, 2 * width + 1 : 2 * width + 2].astype(F32)
        n2_ref[part, :] = unit
        r2_ref[part, :] = wide(inverse)
        rate_ref[part, :] = wide(rate)
        state = state_ref[part, :]
        state = state + keep * (updated - state)
        out_ref[part, :] = state + (pooled_ref[part, :] + (keep * rate) * updated)
        cot = tok_ref[part, width : 2 * width].astype(F32)
        tail_back(
            part, 1, cot, cot, tok_ref, vec_ref, n2_ref, r2_ref, rate_ref, b2_ref, gsec_ref, base_ref,
            sums_ref,
        )
    feed_back(b2_ref, dg_ref, win_ref, whid_ref, inner_ref, b1_ref, acc_ref)
    middle_back(gsec_ref, acc_ref, vec_ref, n1_ref, r1_ref, b0_ref, base_ref, sums_ref)
    gctx_ref[...] = dot(b0_ref[...], matrix(wa_ref, 3), 1, 1).astype(BF16)
    split_heads(gctx_ref, g2_ref)
    pairs = range(q2_ref.shape[0])
    attend_back(pairs, g2_ref, q2_ref, k_ref, v_ref, p_ref, ctx_ref, ds_ref, o_ref, dqkv_ref, doth_ref)
    inputs_back(dqkv_ref, doth_ref, wa_ref, base_ref, gs_ref, goth_ref)
    vg_ref[...] = jnp.zeros_like(vg_ref)
    for index in range(VECS):
        vg_ref[index : index + 1, :] = jnp.sum(sums_ref[index], axis=0, keepdims=True)


def place(fast, me_ref, value, scratch_ref, outs, at):
    cols = slice(at, at + value.shape[1])
    if not fast:
        outs[0][:, cols] = value
        return
    low = value.astype(BF16)
    scratch_ref[:, :, :, : value.shape[1]] = low.reshape(scratch_ref.shape[:3] + value.shape[1:])
    for relative in range(8):
        block = scratch_ref[:, relative ^ (me_ref[0] % 8), :, : value.shape[1]]
        outs[relative % 2][relative // 2, :, :, cols] = block


def hidden_back_kernel(
    fast, me_ref, gs_ref, more_ref, tok_ref, vec_ref,
    n2_ref, r2_ref, rate_ref, hid_ref, hid1_ref, b21_ref,
    b2_ref, gsec_ref, base_ref, sums_ref,
    *rest,
):
    outs, tall_ref = rest[:-1], rest[-1]
    sums_ref[...] = jnp.zeros_like(sums_ref)
    width = gs_ref.shape[1]
    for part in chunks(gs_ref.shape[0], ROWS):
        tail_back(
            part, 0, gs_ref[part, :] + more_ref[part, :].astype(F32),
            tok_ref[part, width : 2 * width].astype(F32), tok_ref, vec_ref,
            n2_ref, r2_ref, rate_ref, b2_ref, gsec_ref, base_ref, sums_ref,
        )
    hidden_rows = hid_ref.shape[1] // 4
    for z in range(4):
        span = slice(z * hidden_rows, (z + 1) * hidden_rows)
        value = dot(hid_ref[:, span], b2_ref[...], 0, 0) + dot(hid1_ref[:, span], b21_ref[...], 0, 0)
        if fast:
            tall_ref[...] = value.astype(BF16).reshape(tall_ref.shape)
            for relative in range(8):
                outs[relative % 2][relative // 2, z] = tall_ref[relative ^ (me_ref[0] % 8)]
        else:
            outs[0][span, :] = value


def feed_back_kernel(
    b2_ref, gsec_ref, base0_ref, sums0_ref, vec_ref, win_ref, whid_ref, wa_ref, n1_ref, r1_ref, dg_ref,
    b1_ref, b0_ref, base_ref, gctx_ref, sums_ref, inner_ref, acc_ref,
):
    sums_ref[...] = sums0_ref[...]
    base_ref[...] = base0_ref[...]
    feed_back(b2_ref, dg_ref, win_ref, whid_ref, inner_ref, b1_ref, acc_ref)
    middle_back(gsec_ref, acc_ref, vec_ref, n1_ref, r1_ref, b0_ref, base_ref, sums_ref)
    gctx_ref[...] = dot(b0_ref[...], matrix(wa_ref, 3), 1, 1).astype(BF16)


def weights_back_kernel(
    fast, me_ref, b1_ref, b0_ref, sums_ref, nlow_ref, ctx_ref, nlow1_ref, b11_ref, ctx1_ref, b01_ref, vg1_ref,
    *rest,
):
    outs, (whole_ref, flip_ref) = rest[:-2], rest[-2:]
    width = ctx_ref.shape[1]
    for cols in chunks(b1_ref.shape[1], BLOCK):
        value = dot(nlow_ref[...], b1_ref[:, cols], 0, 0) + dot(nlow1_ref[...], b11_ref[:, cols], 0, 0)
        place(fast, me_ref, value, whole_ref, outs, cols.start)
    value = dot(ctx_ref[...], b0_ref[...], 0, 0) + dot(ctx1_ref[...], b01_ref[...], 0, 0)
    at = b1_ref.shape[1]
    place(fast, me_ref, value, whole_ref, outs, at)
    flip_ref[...] = jnp.zeros_like(flip_ref)
    flip_ref[0:8, :] = vg1_ref[...]
    for index in range(VECS):
        flip_ref[index : index + 1, :] += jnp.sum(sums_ref[index], axis=0, keepdims=True)
    place(fast, me_ref, flip_ref[...].T, whole_ref, outs, at + width)


def heads_back_kernel(
    gctx_ref, q2_ref, k_ref, v_ref, p_ref, ctx_ref, dqkv_ref, doth_ref, g2_ref, ds_ref, dq2_ref
):
    split_heads(gctx_ref, g2_ref)
    pairs = range(q2_ref.shape[0])
    attend_back(pairs, g2_ref, q2_ref, k_ref, v_ref, p_ref, ctx_ref, ds_ref, dq2_ref, dqkv_ref, doth_ref)


def project_back_kernel(
    fast, me_ref, base_ref, wa_ref,
    rown_ref, roth_ref, rown1_ref, roth1_ref, dqkv1_ref, doth1_ref, dqkv_ref, doth_ref,
    gs_ref, goth_ref,
    *rest,
):
    outs, whole_ref = rest[:-1], rest[-1]
    width = base_ref.shape[1]
    for index in range(3):
        cols = slice(index * width, (index + 1) * width)
        value = dot(rown_ref[...], dqkv_ref[:, cols], 0, 0) + dot(
            rown1_ref[...], dqkv1_ref[:, cols], 0, 0
        )
        if index:
            other = slice((index - 1) * width, index * width)
            value = (
                value
                + dot(roth_ref[...], doth_ref[:, other], 0, 0)
                + dot(roth1_ref[...], doth1_ref[:, other], 0, 0)
            )
        place(fast, me_ref, value, whole_ref, outs, cols.start)
    inputs_back(dqkv_ref, doth_ref, wa_ref, base_ref, gs_ref, goth_ref)


def stack_kernel(*refs):
    *parts, out_ref, sems = refs
    for copy in pull([(part, out_ref.at[index]) for index, part in enumerate(parts)], sems):
        copy.wait()


def halves_kernel(by_y_ref, by_x_ref, low_ref, high_ref, sems):
    half = low_ref.shape[0]
    moves = [(by_y_ref.at[pl.ds(0, half)], low_ref), (by_x_ref.at[pl.ds(half, half)], high_ref)]
    for copy in pull(moves, sems):
        copy.wait()


def return_kernel(info_ref, out_ref, in_ref, back_ref, out_both_ref, in_both_ref):
    local, width = back_ref.shape[0], out_ref.shape[1]
    for own_ref, target, cols in (
        (out_ref, out_both_ref, slice(0, width)),
        (in_ref, in_both_ref, slice(width, 2 * width)),
    ):
        target[info_ref[1]] = own_ref[:local, :]
        target[1 - info_ref[1]] = back_ref[:, cols].astype(F32)


def send_kernel(own_ref, more_ref, out_ref, total_ref, back_ref):
    local, width = back_ref.shape[0], own_ref.shape[1]
    for part in chunks(own_ref.shape[0], ROWS):
        total = own_ref[part, :] + more_ref[part, :].astype(F32)
        total_ref[part, :] = total
        if part.start >= local:
            target = slice(part.start - local, part.stop - local)
            back_ref[target, :width] = out_ref[part, :].astype(BF16)
            back_ref[target, width:] = total.astype(BF16)


def add_core_kernel(keep_ref, got_ref, s11a_ref, s11b_ref, s10_ref, s01_ref, s00_ref):
    half = s11a_ref.shape[0]
    for z in range(keep_ref.shape[1]):
        for index, target in ((0, s00_ref), (1, s01_ref), (2, s10_ref)):
            total = keep_ref[index, z].astype(F32) + got_ref[index, z].astype(F32)
            target[z] = total.astype(BF16)
        total = (keep_ref[3, z].astype(F32) + got_ref[3, z].astype(F32)).astype(BF16)
        if z < half:
            s11a_ref[z] = total
        else:
            s11b_ref[z - half] = total


def beside(target_ref, z, values, rows, width):
    for index in range(values.shape[0] // rows):
        target_ref[z, :, index * width : (index + 1) * width] = values[index * rows : (index + 1) * rows]


def add_half_kernel(a10_ref, ax_ref, a01_ref, ay_ref, b10_ref, bx_ref, b01_ref, by_ref, o10_ref, o01_ref):
    half = ax_ref.shape[0]
    rows, width = b10_ref.shape[1], a10_ref.shape[2]
    at = a10_ref.shape[1] // rows * width
    for z in range(2 * half):
        for tall_ref, tall_got_ref, low_ref, got_ref, out_ref, first in (
            (a10_ref, ax_ref, b10_ref, bx_ref, o10_ref, 0),
            (a01_ref, ay_ref, b01_ref, by_ref, o01_ref, half),
        ):
            if first <= z < first + half:
                tall = (tall_ref[z].astype(F32) + tall_got_ref[z - first].astype(F32)).astype(BF16)
                low = (low_ref[z].astype(F32) + got_ref[z - first].astype(F32)).astype(BF16)
            else:
                tall, low = tall_ref[z], low_ref[z]
            beside(out_ref, z, tall, rows, width)
            out_ref[z, :, at:] = low


def add_both_kernel(info_ref, a_ref, b_ref, got_x_ref, got_y_ref, own_ref, near_ref, next_ref, far_ref):
    line = info_ref[0] // 8
    rows, width = b_ref.shape[1], a_ref.shape[2]
    count = a_ref.shape[1] // rows
    for z, out_ref in enumerate((own_ref, near_ref, next_ref, far_ref)):
        at = line ^ z
        for index in range(count + 1):
            if index < count:
                cols = slice(index * width, (index + 1) * width)
                own = a_ref[at, index * rows : (index + 1) * rows]
            else:
                cols = slice(count * width, got_x_ref.shape[2])
                own = b_ref[at]
            total = own.astype(F32) + got_x_ref[at, :, cols].astype(F32) + got_y_ref[at, :, cols].astype(F32)
            out_ref[:, cols] = total.astype(BF16)


def add_pair_kernel(own_ref, got_ref, sum_ref):
    sum_ref[...] = (own_ref[...].astype(F32) + got_ref[...].astype(F32)).astype(BF16)


def add_core_all_kernel(keep_ref, got_ref, *outs):
    for z in range(keep_ref.shape[1]):
        for index, target in enumerate(outs):
            target[z] = (keep_ref[index, z].astype(F32) + got_ref[index, z].astype(F32)).astype(BF16)


def add_four_kernel(info_ref, a_ref, b_ref, c_ref, d_ref, own_ref, near_ref, next_ref, far_ref):
    line = info_ref[0] // 8
    for z, out_ref in enumerate((own_ref, near_ref, next_ref, far_ref)):
        at = line ^ z
        total = a_ref[at].astype(F32) + b_ref[at].astype(F32) + c_ref[at].astype(F32)
        out_ref[...] = (total + d_ref[at].astype(F32)).astype(BF16)


def end_both_kernel(own_ref, got_ref, far_ref, tall_ref, win_ref, wo_ref, *rest):
    vectors, flip_ref = rest[:-1], rest[-1]
    rows, width = far_ref.shape[0], tall_ref.shape[1]

    def total(cols):
        return own_ref[:, cols].astype(F32) + got_ref[:, cols].astype(F32) + far_ref[:, cols].astype(F32)

    at = tall_ref.shape[0] // rows * width
    for index in range(tall_ref.shape[0] // rows):
        tall_ref[index * rows : (index + 1) * rows, :] = total(slice(index * width, (index + 1) * width))
    for out in (win_ref, wo_ref):
        out[...] = total(slice(at, at + out.shape[1]))
        at = at + out.shape[1]
    flip_ref[...] = jnp.zeros_like(flip_ref)
    flip_ref[:rows, :] = total(slice(at, at + LANES))
    turned = flip_ref[...].T
    for index, vector in enumerate(vectors):
        vector[...] = turned[index : index + 1, :rows]


def end_kernel(a_ref, b_ref, c_ref, d_ref, *outs):
    at = 0
    for out in outs:
        cols = slice(at, at + out.shape[1])
        total = a_ref[:, cols].astype(F32) + b_ref[:, cols].astype(F32)
        out[...] = total + c_ref[:, cols].astype(F32) + d_ref[:, cols].astype(F32)
        at = at + out.shape[1]


def vm():
    return pl.BlockSpec(memory_space=pltpu.VMEM)


def run(kernel, ins, outs, scratch=(), scalars=(), loose=(), pinned=(), far=(), sems=0, micros=0.05):
    specs = [vm() for _ in ins]
    for index in scalars:
        specs[index] = pl.BlockSpec(memory_space=pltpu.SMEM)
    ins = list(ins)
    for index in loose:
        specs[index] = pl.BlockSpec(memory_space=pl.ANY)
    for index in pinned:
        specs[index] = pl.BlockSpec(memory_space=pltpu.HBM)
        ins[index] = pltpu.with_memory_space_constraint(ins[index], pltpu.HBM)
    size = sum(v.size * v.dtype.itemsize for v in ins) + sum(
        functools.reduce(lambda a, b: a * b, s, 1) * jnp.dtype(t).itemsize for s, t in outs
    )
    buffers = [pltpu.VMEM(s, t) for s, t in scratch]
    need = sum(functools.reduce(lambda a, b: a * b, s, 1) * jnp.dtype(t).itemsize for s, t in scratch)
    if sems:
        buffers.append(pltpu.SemaphoreType.DMA((sems,)))
    return pl.pallas_call(
        kernel,
        out_shape=[jax.ShapeDtypeStruct(s, t) for s, t in outs],
        in_specs=specs,
        out_specs=[pl.BlockSpec(memory_space=pl.ANY) if index in far else vm() for index in range(len(outs))],
        scratch_shapes=buffers,
        compiler_params=pltpu.CompilerParams(vmem_limit_bytes=max(need + 8 * MIB, SCOPED)),
        cost_estimate=pl.CostEstimate(
            flops=int(micros * MICRO), bytes_accessed=size, transcendentals=0
        ),
    )(*ins)


AXES = ("dp", "head")


def after(value, *others):
    return lax.optimization_barrier((value, *others))[0]


class Links:
    def __init__(self, model_rows):
        self.heads = lax.axis_size("head")
        self.pods = lax.axis_size("dp")
        self.count = self.heads * self.pods
        self.fast = self.heads == 4 and self.pods == 8 and model_rows == 16
        self.head = lax.axis_index("head")
        self.me = lax.axis_index("dp") * self.heads + self.head

    def flip(self, value, bit):
        return lax.ppermute(value, AXES, [(i, i ^ bit) for i in range(self.count)])

    def flip_head(self, value, bit):
        return lax.ppermute(value, "head", [(i, i ^ bit) for i in range(self.heads)])

    def along_z(self, block):
        return [block, *(self.flip(block, 8 * k) for k in (1, 2, 3))]

    def stack(self, parts):
        (out,) = run(
            stack_kernel, parts, [((4, *parts[0].shape), BF16)], loose=range(4), far=(0,), sems=4
        )
        return out

    def core_sums(self, keep, got):
        block = keep.shape[2:]
        whole, half = ((4, *block), BF16), ((2, *block), BF16)
        return run(add_core_kernel, [keep, got], [half, half, whole, whole, whole])

    def line_parts(self, kernel, parts, shape):
        return run(kernel, [self.info, *parts], [(shape, BF16)] * 4, scalars=(0,))

    def line_first(self, kernel, parts, shape):
        own, near, following, far = self.line_parts(kernel, parts, shape)
        return own, far, self.flip(near, 8), self.flip(following, 8)

    def line_last(self, own, far, got, got_far):
        (far,) = run(add_pair_kernel, [after(far, got), got_far], [(far.shape, BF16)])
        return own, got, self.flip(far, 24)

    def spread(self, own, group):
        held, bit = own[None], 1
        while bit < group:
            got = self.flip_head(held, bit)
            held = got if bit == 1 and group == 2 else jnp.concatenate([held, got], axis=0)
            bit = bit * 2
        if group > 2:
            held = held[1:]
        return held.reshape(-1, own.shape[1])

    def collapse(self, parts, group, rows):
        if group == 2:
            return self.flip_head(parts, 1)
        held = parts.reshape(group - 1, rows, -1)
        held = jnp.concatenate([jnp.zeros_like(held[:1]), held], axis=0).astype(F32)
        bit = group // 2
        while bit >= 1:
            held = held[:bit] + self.flip_head(held[bit : 2 * bit], bit)
            bit = bit // 2
        return held[0]


def body(
    tokens, cotangent, lengths, halting, w_query, w_key, w_value, w_out, w_in, w_hidden,
    w_halt, gain_attn, shift_attn, gain_ffn, shift_ffn,
):
    micro, local, width = tokens.shape
    links = Links(w_query.shape[0])
    fast, heads = links.fast, links.heads
    group = heads // micro
    rows, length = micro * local, local * heads
    mine = links.head // group
    wide_ff = w_in.shape[1]
    fine = width // links.count
    matrices = (w_query, w_key, w_value, w_out, w_in, w_hidden)
    vectors = (w_halt, gain_attn, shift_attn, gain_ffn, shift_ffn)
    place_array = jnp.stack([links.me, mine, links.head % group, jnp.int32(group)]).astype(jnp.int32)
    links.info = place_array

    pairs = width // LANES
    row_f, row_b = ((rows, width), F32), ((rows, width), BF16)
    stat = ((rows, LANES), F32)
    others = length - rows
    long_b = ((length, width), BF16)
    q2_t = ((pairs, 2 * rows, LANES), BF16)
    p_t = ((pairs, 2 * rows, length), BF16)
    o_t = ((2 * rows, LANES), F32)
    bias_t = ((rows, length), F32)
    inner_t = ((rows, BLOCK), F32)
    ff_b = ((rows, wide_ff), BF16)
    sums_t = ((VECS, 8, width), F32)
    ds_t = ((2 * rows, length), BF16)
    dqkv_t = ((rows, 3 * width), BF16)
    doth_t = ((others, 2 * width), BF16)
    vg_t = ((8, width), F32)
    segq_t, segk_t = ((rows, LANES), jnp.int32), ((8, length), jnp.int32)

    sort_in = [place_array, tokens, cotangent, halting]
    sort_out = [((local, 2 * width + LANES), BF16)] * 2
    sort_tmp = [((LANES, local), F32), (halting.shape, jnp.int32)]
    if fast:
        send_tok, own_tok, block_a, block_b = run(
            pack_kernel,
            [*sort_in, *matrices, *(vector[None] for vector in vectors)],
            [*sort_out, ((4 * pairs + 1, fine, LANES), BF16), ((8, fine, BLOCK), BF16)],
            [*sort_tmp, ((LANES, LANES), F32), ((VECS, 1, fine), BF16)],
            scalars=(0,),
            pinned=range(1, 15),
            sems=18 + 4 * pairs,
        )
        got_tok = links.flip_head(send_tok, group)
        line_a = links.along_z(block_a)
        own_a = after(links.stack(line_a), got_tok)
        by_x, by_y = links.flip(own_a, 2), links.flip(own_a, 4)
        line_b = links.along_z(after(block_b, line_a[1]))
        plane_a = [own_a, by_x, by_y, links.flip(after(by_y, line_b[3]), 2)]
    else:
        send_tok, own_tok = run(
            sort_kernel, sort_in, sort_out, sort_tmp, scalars=(0,), pinned=(1, 2, 3), sems=5
        )
        full = [lax.all_gather(part, AXES, axis=0, tiled=True) for part in matrices]
        full_v = [lax.all_gather(part, AXES, axis=0, tiled=True) for part in vectors]
        full_a = jnp.stack(full[:4])
        full_in = jnp.transpose(full[4].reshape(width, wide_ff // BLOCK, BLOCK), (1, 0, 2))
        full_hid = full[5]
        vec = jnp.pad(jnp.stack(full_v), ((0, 8 - VECS), (0, 0))).astype(F32)

        got_tok = links.flip_head(send_tok, group)
    tok, x0, rown0, sig1, segq, segk = run(
        embed_kernel,
        [place_array, lengths[:, 0], own_tok, got_tok],
        [((rows, 2 * width + LANES), BF16), row_f, row_b, row_f, segq_t, segk_t],
        scalars=(0, 1),
    )
    roth0 = links.spread(rown0, group)
    if fast:
        own_b = after(links.stack(line_b), by_x, by_y, roth0)
        near = [own_b, links.flip(own_b, 2), links.flip(own_b, 4)]
        near = near + [links.flip(piece, 1) for piece in near]
        halves = run(
            halves_kernel,
            [near[2], near[1]],
            [((2, 8, fine, BLOCK), BF16)] * 2,
            loose=(0, 1),
            far=(0, 1),
            sems=2,
        )
        far_b = [links.flip(halves[0], 2), links.flip(halves[1], 4)]
        plane_a[3] = after(plane_a[3], halves[0])
        plane_a = plane_a + [links.flip(piece, 1) for piece in plane_a]

    attend_in = [rown0, roth0, segq, segk]
    attend_out = [q2_t, long_b, long_b, p_t, row_b]
    if fast:
        full_a, vec, q2, k, v, p, ctx = run(
            functools.partial(attend_kernel, True),
            [*attend_in, links.info, *plane_a],
            [((5, 4, 8, fine, BLOCK), BF16), vg_t, *attend_out],
            [row_b, bias_t, o_t],
            scalars=(4,),
            micros=8,
        )
        full_a = full_a.reshape(5, width, BLOCK)
    else:
        q2, k, v, p, ctx = run(
            functools.partial(attend_kernel, False),
            [*attend_in, full_a],
            attend_out,
            [row_b, bias_t, o_t],
            micros=8,
        )
    n1, r1, nlow = run(norm_kernel, [x0, ctx, vec, full_a], [row_f, stat, row_b], [row_f], micros=1)
    ffn_out = [ff_b, ff_b, row_f, stat, stat, row_f, row_f, row_f, row_b]
    ffn_in = [n1, nlow, tok, sig1, vec]
    if fast:
        far_b = [after(piece, ctx) for piece in far_b]
        far_b = far_b + [links.flip(piece, 1) for piece in far_b]
        full_in, full_hid, *got = run(
            functools.partial(ffn_kernel, True),
            [*ffn_in, links.info, *near, *far_b],
            [((4, 4, 8, fine, BLOCK), BF16), ((4, 8, 4, fine, BLOCK), BF16), *ffn_out],
            [inner_t, row_f],
            scalars=(5,),
            micros=5.5,
        )
        full_in = full_in.reshape(4, width, BLOCK)
        full_hid = full_hid.reshape(wide_ff, width)
    else:
        got = run(
            functools.partial(ffn_kernel, False),
            [*ffn_in, full_in, full_hid],
            ffn_out,
            [inner_t, row_f],
            micros=5.5,
        )
    hid, dg, n2, r2, rate, state, pooled, x1, rown1 = got
    roth1 = links.spread(rown1, group)
    out, gs, goth, nlow1, hid1, b11, b21, ctx1, b01, dqkv1, doth1, vg1 = run(
        turn_kernel,
        [x1, rown1, roth1, full_a, full_in, full_hid, vec, segq, segk, state, pooled, tok],
        [row_f, row_f, ((others, width), BF16), row_b, ff_b, ff_b, row_b, row_b, row_b, dqkv_t, doth_t, vg_t],
        [
            row_b, q2_t, long_b, long_b, p_t, bias_t, o_t, row_f, row_f, stat, inner_t, ff_b,
            row_f, stat, stat, row_f, row_f, sums_t, row_b, q2_t, ds_t,
        ],
        micros=15.7,
    )
    more = links.collapse(goth, group, rows)

    b_cols = wide_ff + width + LANES
    def parts_of(shape, whole):
        return [((4, 4, *shape), BF16)] * 2 if fast else [(whole, F32)]

    hid_out = parts_of((4 * fine, width), (wide_ff, width))
    in_out = parts_of((fine, b_cols), (width, b_cols))
    attend_outs = parts_of((fine, 3 * width), (width, 3 * width))
    whole_shape = (4, 8, fine, BLOCK) if fast else (16, LANES)
    tall_shape = (8, 4 * fine, width) if fast else (16, LANES)
    b2, gsec, base, sums, *hid_parts = run(
        functools.partial(hidden_back_kernel, fast),
        [links.info, gs, more, tok, vec, n2, r2, rate, hid, hid1, b21],
        [row_b, row_f, row_f, sums_t, *hid_out],
        [(tall_shape, BF16)],
        scalars=(0,),
        micros=2,
    )
    b1, b0, base, gctx, sums = run(
        feed_back_kernel,
        [b2, gsec, base, sums, vec, full_in, full_hid, full_a, n1, r1, dg],
        [ff_b, row_b, row_f, row_b, sums_t],
        [inner_t, row_f],
        micros=2.2,
    )
    if fast:
        c_sums = links.core_sums(hid_parts[0], links.flip(hid_parts[1], 1))
        b1 = after(b1, c_sums[0])
    in_parts = run(
        functools.partial(weights_back_kernel, fast),
        [links.info, b1, b0, sums, nlow, ctx, nlow1, b11, ctx1, b01, vg1],
        in_out,
        [(whole_shape, BF16), ((LANES, width), F32)],
        scalars=(0,),
        micros=2,
    )
    if fast:
        b_sums = links.core_sums(in_parts[0], links.flip(in_parts[1], 1))
        gctx = after(gctx, b_sums[0])
    dqkv0, doth0 = run(
        heads_back_kernel,
        [gctx, q2, k, v, p, ctx],
        [dqkv_t, doth_t],
        [q2_t, ds_t, o_t],
        micros=3,
    )
    g0, goth0, *attend_parts = run(
        functools.partial(project_back_kernel, fast),
        [links.info, base, full_a, rown0, roth0, rown1, roth1, dqkv1, doth1, dqkv0, doth0],
        [row_f, ((others, width), BF16), *attend_outs],
        [(whole_shape, BF16)],
        scalars=(0,),
    )
    if fast:
        c11a, c11b, c10, c01, c00 = c_sums
        b11a, b11b, b10, b01, b00 = b_sums
        halves = [
            after(c10, g0), links.flip(c11a, 2), c01, links.flip(c11b, 4),
            b10, links.flip(b11a, 2), b01, links.flip(b11b, 4),
        ]
        both_t = ((4, fine, 4 * width + b_cols), BF16)
        both10, both01 = run(add_half_kernel, halves, [both_t] * 2)
        goth0, send_a = after(goth0, both01), after(attend_parts[1], both01)
    inputs, back = run(
        send_kernel,
        [g0, links.collapse(goth0, group, rows), out],
        [row_f, ((local, 2 * width), BF16)],
    )
    if fast:
        keep, got = after(attend_parts[0], back), links.flip(send_a, 1)
        a00, a01, a10, a11 = run(add_core_all_kernel, [keep, got], [(keep.shape[1:], BF16)] * 4)
        by_plane = [a00, links.flip(a11, 6), links.flip(a01, 2), links.flip(a10, 4)]
        both = links.line_first(
            add_both_kernel, [after(c00, a00), b00, links.flip(both01, 2), links.flip(both10, 4)], both_t[0][1:]
        )
        first_sums = both[0]
        by_plane[0] = after(by_plane[0], both[0])
        attend_sums = links.line_parts(add_four_kernel, by_plane, a00.shape[1:])
        both = links.line_last(both[0], after(both[1], attend_sums[0]), *both[2:])
        attend_sums = [attend_sums[0], *(links.flip(attend_sums[k], 8 * k) for k in (1, 2, 3))]
        back = after(back, first_sums)
        output, input_grad = run(
            return_kernel,
            [links.info, out, inputs, links.flip_head(back, group)],
            [((micro, local, width), F32)] * 2,
            scalars=(0,),
        )
        g_hidden, g_in, g_out, *g_vectors = run(
            end_both_kernel,
            [after(both[0], output), *both[1:]],
            [((4 * fine, width), F32), ((fine, wide_ff), F32), ((fine, width), F32)] + [((1, fine), F32)] * VECS,
            [((LANES, LANES), F32)],
        )
        g_query, g_key, g_value = run(
            end_kernel,
            [after(attend_sums[0], output, g_hidden), *attend_sums[1:]],
            [((fine, width), F32)] * 3,
        )
        g_vectors = [vector.reshape(fine) for vector in g_vectors]
    else:
        sums = [
            *(attend_parts[0][:, index * width : (index + 1) * width] for index in range(3)),
            in_parts[0][:, wide_ff : wide_ff + width], in_parts[0][:, :wide_ff], hid_parts[0],
            in_parts[0][:, wide_ff + width :],
        ]
        sums = [lax.psum_scatter(part, AXES, scatter_dimension=0, tiled=True) for part in sums]
        g_query, g_key, g_value, g_out, g_in, g_hidden, g_vec = sums
        g_vectors = [g_vec[:, index] for index in range(VECS)]
        output, input_grad = run(
            return_kernel,
            [links.info, out, inputs, links.flip_head(back, group)],
            [((micro, local, width), F32)] * 2,
            scalars=(0,),
        )
    return (output, input_grad, g_query, g_key, g_value, g_out, g_in, g_hidden, *g_vectors)


def solution(mesh):
    whole = P(("dp", "head"))
    matrix = P(("dp", "head"), None)
    rows = P(None, ("dp", "head"), None)
    return jax.shard_map(
        body,
        mesh=mesh,
        in_specs=(rows, rows, P(None, "dp", None), P(None, None, ("dp", "head")))
        + (matrix,) * 6
        + (whole,) * 5,
        out_specs=(rows, rows) + (matrix,) * 6 + (whole,) * 5,
        check_vma=False,
    )
```

```python
import functools

import jax
import jax.numpy as jnp
from jax import lax
from jax.experimental import pallas as pl
from jax.experimental.pallas import tpu as pltpu
from jax.sharding import PartitionSpec as P

HD = 64
EPSILON = 1e-06
F32 = jnp.float32
BF16 = jnp.bfloat16
LANES = 128
ROWS = 32
ATT_ROWS = 256
BLOCK = 512
VECS = 5
MIB = 1024 * 1024
SCOPED = 20 * MIB
MICRO = 1.15e9
GELU_A = 0.7978845608028654
GELU_B = 0.044715


def dot(a, b, ca=1, cb=0):
    return lax.dot_general(a, b, (((ca,), (cb,)), ((), ())), preferred_element_type=F32)


def chunks(total, size):
    size = min(size, total)
    return [slice(i, i + size) for i in range(0, total, size)]


def wide(column):
    return jnp.broadcast_to(column, (column.shape[0], LANES))


def mean(values):
    return jnp.sum(values, axis=-1, keepdims=True) * (1.0 / values.shape[-1])


def fold(values):
    return jnp.sum(values.reshape(values.shape[0] // 8, 8, values.shape[1]), axis=0)


class Flat:
    def __init__(self, ref):
        self.ref = ref

    def __getitem__(self, index):
        if index is Ellipsis:
            index = (slice(None), slice(None))
        value = self.ref[..., index[1]]
        return value.reshape(-1, value.shape[-1])[index[0]]


def matrix(ref, index):
    value = ref[index]
    return value.reshape(-1, value.shape[-1])


def head_mask(rows):
    lane = lax.broadcasted_iota(jnp.int32, (rows, LANES), 1)
    return lane < HD


def normalize(values):
    center = values - mean(values)
    inverse = lax.rsqrt(mean(center * center) + EPSILON)
    return center * inverse, inverse


def normalize_back(unit, inverse, grad):
    return inverse * (grad - mean(grad) - unit * mean(grad * unit))


def split_heads(values_ref, stacked_ref):
    rows = values_ref.shape[0]
    for part in chunks(rows, ATT_ROWS):
        first = head_mask(part.stop - part.start)
        for pair in range(stacked_ref.shape[0]):
            block = values_ref[part, pair * LANES : (pair + 1) * LANES].astype(F32)
            stacked_ref[pair, part, :] = jnp.where(first, block, 0.0).astype(BF16)
            stacked_ref[pair, rows + part.start : rows + part.stop, :] = jnp.where(
                first, 0.0, block
            ).astype(BF16)


def project(rown_ref, roth_ref, wa_ref, q_ref, q2_ref, k_ref, v_ref):
    rows, width = rown_ref.shape
    q_ref[...] = (
        dot(rown_ref[...], matrix(wa_ref, 0)).astype(BF16).astype(F32) * HD**-0.5
    ).astype(BF16)
    split_heads(q_ref, q2_ref)
    for at, source in ((0, rown_ref), (rows, roth_ref)):
        span = slice(at, at + source.shape[0])
        k_ref[span, :] = dot(source[...], matrix(wa_ref, 1)).astype(BF16)
        v_ref[span, :] = dot(source[...], matrix(wa_ref, 2)).astype(BF16)


def set_bias(segq_ref, segk_ref, bias_ref):
    for part in chunks(bias_ref.shape[0], ROWS):
        bias_ref[part, :] = jnp.where(segq_ref[part, 0:1] == segk_ref[0:1, :], 0.0, -1e30)


def attend(q2_ref, k_ref, v_ref, bias_ref, p_ref, ctx_ref, o_ref):
    rows, length = bias_ref.shape
    for pair in range(q2_ref.shape[0]):
        cols = slice(pair * LANES, (pair + 1) * LANES)
        for part in chunks(2 * rows, 2 * rows):
            scores = dot(q2_ref[pair, part, :], k_ref[:, cols], 1, 1)
            scores = (scores.reshape(2, rows, length) + bias_ref[...][None]).reshape(2 * rows, length)
            weights = jnp.exp(scores - jnp.max(scores, axis=-1, keepdims=True))
            inverse = 1.0 / jnp.sum(weights, axis=-1, keepdims=True)
            low = (weights * inverse).astype(BF16)
            p_ref[pair, part, :] = low
            o_ref[part, :] = dot(low, v_ref[:, cols])
        for part in chunks(rows, ATT_ROWS):
            first = head_mask(part.stop - part.start)
            second = o_ref[rows + part.start : rows + part.stop, :]
            ctx_ref[part, cols] = jnp.where(first, o_ref[part, :], second).astype(BF16)


def first_norm(x_ref, ctx_ref, wa_ref, vec_ref, acc_ref, n1_ref, r1_ref, nlow_ref):
    acc_ref[...] = dot(ctx_ref[...], matrix(wa_ref, 3))
    for part in chunks(x_ref.shape[0], ROWS):
        unit, inverse = normalize(x_ref[part, :] + acc_ref[part, :])
        n1_ref[part, :] = unit
        r1_ref[part, :] = wide(inverse)
        nlow_ref[part, :] = (unit * vec_ref[1:2, :] + vec_ref[2:3, :]).astype(BF16)


def feed_forward(nlow_ref, win_ref, whid_ref, inner_ref, hid_ref, dg_ref, acc_ref):
    rows = nlow_ref.shape[0]
    for cols in chunks(hid_ref.shape[1], BLOCK):
        inner_ref[...] = dot(nlow_ref[...], matrix(win_ref, cols.start // BLOCK))
        for part in chunks(rows, ROWS):
            x = inner_ref[part, :]
            square = x * x
            t = jnp.tanh(x * (GELU_A + GELU_A * GELU_B * square))
            half = 0.5 + 0.5 * t
            hid_ref[part, cols] = (x * half).astype(BF16)
            slope = 0.5 * x * (1.0 - t * t) * (GELU_A + 3.0 * GELU_A * GELU_B * square)
            dg_ref[part, cols] = (half + slope).astype(BF16)
    acc_ref[...] = dot(hid_ref[...], whid_ref[...])


def second_norm(part, vec_ref, n1_ref, acc_ref):
    normed = n1_ref[part, :] * vec_ref[1:2, :] + vec_ref[2:3, :]
    unit, inverse = normalize(normed + acc_ref[part, :])
    updated = unit * vec_ref[3:4, :] + vec_ref[4:5, :]
    rate = jax.nn.sigmoid(jnp.sum(updated * vec_ref[0:1, :], axis=-1, keepdims=True))
    return unit, inverse, updated, rate


def tail_back(
    part, step, gs, gp, halt_ref, vec_ref, n2_ref, r2_ref, rate_ref, b2_ref, gsec_ref, base_ref, sums_ref
):
    width = n2_ref.shape[1]
    keep = halt_ref[part, 2 * width + step : 2 * width + step + 1].astype(F32)
    unit = n2_ref[part, :]
    updated = unit * vec_ref[3:4, :] + vec_ref[4:5, :]
    rate = rate_ref[part, 0:1]
    logit = keep * jnp.sum(gp * updated, axis=-1, keepdims=True) * rate * (1.0 - rate)
    grad = keep * gs + (keep * rate) * gp + logit * vec_ref[0:1, :]
    base_ref[part, :] = gs - keep * gs
    sums_ref[0] += fold(logit * updated)
    sums_ref[3] += fold(grad * unit)
    sums_ref[4] += fold(grad)
    back = normalize_back(unit, r2_ref[part, 0:1], grad * vec_ref[3:4, :])
    gsec_ref[part, :] = back
    b2_ref[part, :] = back.astype(BF16)


def feed_back(b2_ref, dg_ref, win_ref, whid_ref, inner_ref, b1_ref, acc_ref):
    rows = b2_ref.shape[0]
    for cols in chunks(dg_ref.shape[1], BLOCK):
        inner_ref[...] = dot(b2_ref[...], whid_ref[cols, :], 1, 1)
        for part in chunks(rows, ROWS):
            b1_ref[part, cols] = (inner_ref[part, :] * dg_ref[part, cols].astype(F32)).astype(BF16)
    total = None
    for cols in chunks(dg_ref.shape[1], BLOCK):
        value = dot(b1_ref[:, cols], matrix(win_ref, cols.start // BLOCK), 1, 1)
        total = value if total is None else total + value
    acc_ref[...] = total


def middle_back(gsec_ref, acc_ref, vec_ref, n1_ref, r1_ref, b0_ref, base_ref, sums_ref):
    for part in chunks(gsec_ref.shape[0], ROWS):
        grad = gsec_ref[part, :] + acc_ref[part, :]
        unit = n1_ref[part, :]
        sums_ref[1] += fold(grad * unit)
        sums_ref[2] += fold(grad)
        back = normalize_back(unit, r1_ref[part, 0:1], grad * vec_ref[1:2, :])
        base_ref[part, :] += back
        b0_ref[part, :] = back.astype(BF16)


def attend_back(
    pairs, g2_ref, q2_ref, k_ref, v_ref, p_ref, ctx_ref, ds_ref, dq2_ref, dqkv_ref, doth_ref
):
    rows, width = ctx_ref.shape
    for pair in pairs:
        cols = slice(pair * LANES, (pair + 1) * LANES)
        for part in chunks(2 * rows, 2 * rows):
            grad = g2_ref[pair, part, :]
            both = jnp.concatenate([ctx_ref[:, cols]] * 2, axis=0)
            delta = jnp.sum(grad.astype(F32) * both.astype(F32), axis=-1, keepdims=True)
            back = dot(grad, v_ref[:, cols], 1, 1)
            low = (p_ref[pair, part, :].astype(F32) * (back - delta)).astype(BF16)
            ds_ref[part, :] = low
            dq2_ref[part, :] = dot(low, k_ref[:, cols])
        for part in chunks(rows, ATT_ROWS):
            first = head_mask(part.stop - part.start)
            second = dq2_ref[rows + part.start : rows + part.stop, :]
            dqkv_ref[part, cols] = (
                jnp.where(first, dq2_ref[part, :], second) * HD**-0.5
            ).astype(BF16)
        for index, (left, right) in enumerate(
            ((ds_ref[...], q2_ref[pair]), (p_ref[pair], g2_ref[pair]))
        ):
            both = dot(right, left, 0, 0).T.astype(BF16)
            at = index * width + pair * LANES
            dqkv_ref[:, width + at : width + at + LANES] = both[:rows]
            doth_ref[:, at : at + LANES] = both[rows:]


def inputs_back(dqkv_ref, doth_ref, wa_ref, base_ref, gs_ref, goth_ref):
    width = base_ref.shape[1]
    parts = [slice(index * width, (index + 1) * width) for index in range(3)]
    total = base_ref[...]
    for index, cols in enumerate(parts):
        total = total + dot(dqkv_ref[:, cols], matrix(wa_ref, index), 1, 1)
    gs_ref[...] = total
    total = dot(doth_ref[:, parts[0]], matrix(wa_ref, 1), 1, 1)
    goth_ref[...] = (total + dot(doth_ref[:, parts[1]], matrix(wa_ref, 2), 1, 1)).astype(BF16)


def fetch(pieces, cores, bits, start, store, me_ref):
    line, place_in = me_ref[0] // 8, me_ref[0] % 8
    for piece, core, bit in zip(pieces, cores, bits):
        for z in range(piece.shape[0]):
            store(piece, z, line ^ (start + z), place_in ^ (bit | core))


def embed_kernel(place_ref, sizes_ref, tok_ref, got_ref, own_ref, x_ref, rown_ref, sig_ref, segq_ref, segk_ref):
    mine, place_in, group = place_ref[1], place_ref[2], place_ref[3]
    local = tok_ref.shape[0]
    half = x_ref.shape[1] // 2
    ends, starts, total = [], [], 0
    for index in range(sizes_ref.shape[1]):
        starts.append(total)
        total = total + sizes_ref[mine, index]
        ends.append(total)
    ones = jnp.exp(
        lax.broadcasted_iota(jnp.int32, (8, half), 1).astype(F32)
        * (-jnp.log(jnp.full((8, half), 10000.0, F32)) / max(half - 1, 1))
    )
    rates = ones[0:1, :]
    first_sin, first_cos = jnp.sin(rates), jnp.cos(rates)
    for part in chunks(x_ref.shape[0], ROWS):
        size = part.stop - part.start
        block = mine * group + place_in
        block = block if part.start < local else block ^ group
        at = block * local + part.start % local
        token = at + lax.broadcasted_iota(jnp.int32, (size, LANES), 0)
        segment = jnp.zeros((size, LANES), jnp.int32)
        begin = jnp.zeros((size, LANES), jnp.int32)
        for start, end in zip(starts, ends):
            segment = segment + jnp.where(token >= end, 1, 0)
            begin = jnp.maximum(begin, jnp.where(token >= start, start, 0))
        segq_ref[part, :] = segment
        angles = (token - begin).astype(F32)[:, 0:1] * rates
        if part.start < local:
            low = tok_ref[part, :]
        else:
            low = got_ref[part.start - local : part.stop - local, :]
        own_ref[part, :] = low
        for cols, moving, still, step in (
            (slice(0, half), jnp.sin(angles), 0.0, first_sin),
            (slice(half, 2 * half), jnp.cos(angles), 1.0, first_cos),
        ):
            inputs = low[:, cols].astype(F32) + (moving + still)
            x_ref[part, cols] = inputs
            rown_ref[part, cols] = inputs.astype(BF16)
            sig_ref[part, cols] = moving + step
    blocks = segk_ref.shape[1] // local
    for index in range(blocks):
        peer = mine * group + (place_in ^ (index // 2))
        peer = peer if index % 2 == 0 else peer ^ group
        token = peer * local + lax.broadcasted_iota(jnp.int32, (8, local), 1)
        segment = jnp.zeros((8, local), jnp.int32)
        for end in ends:
            segment = segment + jnp.where(token >= end, 1, 0)
        segk_ref[:, index * local : (index + 1) * local] = segment


def pull(sources, sems):
    copies = [
        pltpu.make_async_copy(source, target, sems.at[index]) for index, (source, target) in enumerate(sources)
    ]
    for copy in copies:
        copy.start()
    return copies


def sort_rows(place_ref, tok_ref, cot_ref, halt_ref, refs, sems):
    mine = place_ref[1]
    width = tok_ref.shape[2]
    send_ref, own_ref, flip_ref, flags_ref = refs
    moves = [(halt_ref, flags_ref)]
    for micro, target in ((1 - mine, send_ref), (mine, own_ref)):
        moves.append((tok_ref.at[micro], target.at[:, :width]))
        moves.append((cot_ref.at[micro], target.at[:, width : 2 * width]))
    copies = pull(moves, sems)
    flip_ref[...] = jnp.zeros_like(flip_ref)
    for copy in copies:
        copy.wait()
    for target, micro in ((own_ref, mine), (send_ref, 1 - mine)):
        for step in range(halt_ref.shape[0]):
            flip_ref[step : step + 1, :] = flags_ref[step, pl.ds(micro, 1), :].astype(F32)
        target[:, 2 * width :] = flip_ref[...].T.astype(BF16)


def sort_kernel(place_ref, tok_ref, cot_ref, halt_ref, *refs):
    sort_rows(place_ref, tok_ref, cot_ref, halt_ref, refs[:4], refs[4])


def pack_kernel(place_ref, tok_ref, cot_ref, halt_ref, q_ref, k_ref, v_ref, o_ref, win_ref, whid_ref, *rest):
    vectors_ref, rest = rest[0], rest[1:]
    sorted_refs, (block_ref, tall_ref, flip_ref, flags_ref, turn_ref, low_ref, sems) = rest[:2], rest[2:]
    rows, width = q_ref.shape
    moves = [(vectors_ref, low_ref)]
    lanes = width // LANES
    for index, source in enumerate((q_ref, k_ref, v_ref, o_ref)):
        for part in range(lanes):
            cols = slice(part * LANES, (part + 1) * LANES)
            moves.append((source.at[:, cols], block_ref.at[index * lanes + part]))
    for index in range(4):
        moves.append((win_ref.at[:, index * BLOCK : (index + 1) * BLOCK], tall_ref.at[index]))
        moves.append((whid_ref.at[index * rows : (index + 1) * rows, :], tall_ref.at[4 + index]))
    count = len(moves)
    copies = pull(moves, sems.at[:count])
    sort_rows(place_ref, tok_ref, cot_ref, halt_ref, [*sorted_refs, flip_ref, flags_ref], sems.at[count:])
    turn_ref[...] = jnp.zeros_like(turn_ref)
    for copy in copies:
        copy.wait()
    turn_ref[:rows, :] = low_ref[...].astype(F32)
    block_ref[4 * lanes] = turn_ref[...].T[:rows, :].astype(BF16)


def attend_kernel(
    fast, rown_ref, roth_ref, segq_ref, segk_ref, *rest,
):
    if fast:
        me_ref, plane, rest = rest[0], rest[1:9], rest[9:]
        wa_ref, vec_ref, q2_ref, k_ref, v_ref, p_ref, ctx_ref, q_ref, bias_ref, o_ref = rest

        def store(piece, z, line, place):
            lanes = wa_ref.shape[4] // LANES
            for chunk in range(piece.shape[1]):
                cols = slice(chunk % lanes * LANES, (chunk % lanes + 1) * LANES)
                wa_ref[chunk // lanes, line, place, :, cols] = piece[z, chunk]

        fetch(plane, (0, 0, 0, 0, 1, 1, 1, 1), (0, 2, 4, 6) * 2, 0, store, me_ref)
        vec_ref[...] = matrix(wa_ref, 4)[:, :LANES].astype(F32).T[0:8, :]
    else:
        wa_ref, q2_ref, k_ref, v_ref, p_ref, ctx_ref, q_ref, bias_ref, o_ref = rest
    set_bias(segq_ref, segk_ref, bias_ref)
    project(rown_ref, roth_ref, wa_ref, q_ref, q2_ref, k_ref, v_ref)
    attend(q2_ref, k_ref, v_ref, bias_ref, p_ref, ctx_ref, o_ref)


def norm_kernel(x_ref, ctx_ref, vec_ref, wa_ref, n1_ref, r1_ref, nlow_ref, acc_ref):
    first_norm(x_ref, ctx_ref, wa_ref, vec_ref, acc_ref, n1_ref, r1_ref, nlow_ref)


def ffn_kernel(fast, n1_ref, nlow_ref, tok_ref, sig_ref, vec_ref, *rest):
    if fast:
        me_ref, near, far, rest = rest[0], rest[1:7], rest[7:11], rest[11:]
        (win_ref, full_ref), rest = rest[:2], rest[2:]
    else:
        (win_ref, whid_ref), rest = rest[:2], rest[2:]
    (
        hid_ref, dg_ref, n2_ref, r2_ref, rate_ref, state_ref, pooled_ref, next_ref, rown_ref,
        inner_ref, acc_ref,
    ) = rest
    if fast:

        def store(piece, z, line, place):
            for chunk in range(4):
                win_ref[chunk, line, place] = piece[z, chunk]
                full_ref[line, place, chunk] = piece[z, 4 + chunk]

        fetch(near, (0, 0, 0, 1, 1, 1), (0, 2, 4, 0, 2, 4), 0, store, me_ref)
        fetch((far[0], far[2]), (0, 1), (6, 6), 0, store, me_ref)
        fetch((far[1], far[3]), (0, 1), (6, 6), 2, store, me_ref)
        whid_ref = Flat(full_ref)
    width = n1_ref.shape[1]
    feed_forward(nlow_ref, win_ref, whid_ref, inner_ref, hid_ref, dg_ref, acc_ref)
    for part in chunks(tok_ref.shape[0], ROWS):
        unit, inverse, updated, rate = second_norm(part, vec_ref, n1_ref, acc_ref)
        keep = tok_ref[part, 2 * width : 2 * width + 1].astype(F32)
        n2_ref[part, :] = unit
        r2_ref[part, :] = wide(inverse)
        rate_ref[part, :] = wide(rate)
        pooled_ref[part, :] = (keep * rate) * updated
        state = tok_ref[part, :width].astype(F32)
        state = state + keep * (updated - state)
        state_ref[part, :] = state
        inputs = state + sig_ref[part, :]
        next_ref[part, :] = inputs
        rown_ref[part, :] = inputs.astype(BF16)


def turn_kernel(
    x_ref, rown_ref, roth_ref, wa_ref, win_ref, whid_ref, vec_ref, segq_ref, segk_ref,
    state_ref, pooled_ref, tok_ref,
    out_ref, gs_ref, goth_ref, nlow_ref, hid_ref, b1_ref, b2_ref, ctx_ref, b0_ref, dqkv_ref, doth_ref, vg_ref,
    q_ref, q2_ref, k_ref, v_ref, p_ref, bias_ref, o_ref, acc_ref, n1_ref, r1_ref, inner_ref, dg_ref,
    n2_ref, r2_ref, rate_ref, gsec_ref, base_ref, sums_ref, gctx_ref, g2_ref, ds_ref,
):
    width = x_ref.shape[1]
    sums_ref[...] = jnp.zeros_like(sums_ref)
    set_bias(segq_ref, segk_ref, bias_ref)
    project(rown_ref, roth_ref, wa_ref, q_ref, q2_ref, k_ref, v_ref)
    attend(q2_ref, k_ref, v_ref, bias_ref, p_ref, ctx_ref, o_ref)
    first_norm(x_ref, ctx_ref, wa_ref, vec_ref, acc_ref, n1_ref, r1_ref, nlow_ref)
    feed_forward(nlow_ref, win_ref, whid_ref, inner_ref, hid_ref, dg_ref, acc_ref)
    for part in chunks(x_ref.shape[0], ROWS):
        unit, inverse, updated, rate = second_norm(part, vec_ref, n1_ref, acc_ref)
        keep = tok_ref[part, 2 * width + 1 : 2 * width + 2].astype(F32)
        n2_ref[part, :] = unit
        r2_ref[part, :] = wide(inverse)
        rate_ref[part, :] = wide(rate)
        state = state_ref[part, :]
        state = state + keep * (updated - state)
        out_ref[part, :] = state + (pooled_ref[part, :] + (keep * rate) * updated)
        cot = tok_ref[part, width : 2 * width].astype(F32)
        tail_back(
            part, 1, cot, cot, tok_ref, vec_ref, n2_ref, r2_ref, rate_ref, b2_ref, gsec_ref, base_ref,
            sums_ref,
        )
    feed_back(b2_ref, dg_ref, win_ref, whid_ref, inner_ref, b1_ref, acc_ref)
    middle_back(gsec_ref, acc_ref, vec_ref, n1_ref, r1_ref, b0_ref, base_ref, sums_ref)
    gctx_ref[...] = dot(b0_ref[...], matrix(wa_ref, 3), 1, 1).astype(BF16)
    split_heads(gctx_ref, g2_ref)
    pairs = range(q2_ref.shape[0])
    attend_back(pairs, g2_ref, q2_ref, k_ref, v_ref, p_ref, ctx_ref, ds_ref, o_ref, dqkv_ref, doth_ref)
    inputs_back(dqkv_ref, doth_ref, wa_ref, base_ref, gs_ref, goth_ref)
    vg_ref[...] = jnp.zeros_like(vg_ref)
    for index in range(VECS):
        vg_ref[index : index + 1, :] = jnp.sum(sums_ref[index], axis=0, keepdims=True)


def place(fast, me_ref, value, scratch_ref, outs, at):
    cols = slice(at, at + value.shape[1])
    if not fast:
        outs[0][:, cols] = value
        return
    low = value.astype(BF16)
    scratch_ref[:, :, :, : value.shape[1]] = low.reshape(scratch_ref.shape[:3] + value.shape[1:])
    for relative in range(8):
        block = scratch_ref[:, relative ^ (me_ref[0] % 8), :, : value.shape[1]]
        outs[relative % 2][relative // 2, :, :, cols] = block


def hidden_back_kernel(
    fast, me_ref, gs_ref, more_ref, tok_ref, vec_ref,
    n2_ref, r2_ref, rate_ref, hid_ref, hid1_ref, b21_ref,
    b2_ref, gsec_ref, base_ref, sums_ref,
    *rest,
):
    outs, tall_ref = rest[:-1], rest[-1]
    sums_ref[...] = jnp.zeros_like(sums_ref)
    width = gs_ref.shape[1]
    for part in chunks(gs_ref.shape[0], ROWS):
        tail_back(
            part, 0, gs_ref[part, :] + more_ref[part, :].astype(F32),
            tok_ref[part, width : 2 * width].astype(F32), tok_ref, vec_ref,
            n2_ref, r2_ref, rate_ref, b2_ref, gsec_ref, base_ref, sums_ref,
        )
    hidden_rows = hid_ref.shape[1] // 4
    for z in range(4):
        span = slice(z * hidden_rows, (z + 1) * hidden_rows)
        value = dot(hid_ref[:, span], b2_ref[...], 0, 0) + dot(hid1_ref[:, span], b21_ref[...], 0, 0)
        if fast:
            tall_ref[...] = value.astype(BF16).reshape(tall_ref.shape)
            for relative in range(8):
                outs[relative % 2][relative // 2, z] = tall_ref[relative ^ (me_ref[0] % 8)]
        else:
            outs[0][span, :] = value


def feed_back_kernel(
    b2_ref, gsec_ref, base0_ref, sums0_ref, vec_ref, win_ref, whid_ref, wa_ref, n1_ref, r1_ref, dg_ref,
    b1_ref, b0_ref, base_ref, gctx_ref, sums_ref, inner_ref, acc_ref,
):
    sums_ref[...] = sums0_ref[...]
    base_ref[...] = base0_ref[...]
    feed_back(b2_ref, dg_ref, win_ref, whid_ref, inner_ref, b1_ref, acc_ref)
    middle_back(gsec_ref, acc_ref, vec_ref, n1_ref, r1_ref, b0_ref, base_ref, sums_ref)
    gctx_ref[...] = dot(b0_ref[...], matrix(wa_ref, 3), 1, 1).astype(BF16)


def weights_back_kernel(
    fast, me_ref, b1_ref, b0_ref, sums_ref, nlow_ref, ctx_ref, nlow1_ref, b11_ref, ctx1_ref, b01_ref, vg1_ref,
    *rest,
):
    outs, (whole_ref, flip_ref) = rest[:-2], rest[-2:]
    width = ctx_ref.shape[1]
    for cols in chunks(b1_ref.shape[1], BLOCK):
        value = dot(nlow_ref[...], b1_ref[:, cols], 0, 0) + dot(nlow1_ref[...], b11_ref[:, cols], 0, 0)
        place(fast, me_ref, value, whole_ref, outs, cols.start)
    value = dot(ctx_ref[...], b0_ref[...], 0, 0) + dot(ctx1_ref[...], b01_ref[...], 0, 0)
    at = b1_ref.shape[1]
    place(fast, me_ref, value, whole_ref, outs, at)
    flip_ref[...] = jnp.zeros_like(flip_ref)
    flip_ref[0:8, :] = vg1_ref[...]
    for index in range(VECS):
        flip_ref[index : index + 1, :] += jnp.sum(sums_ref[index], axis=0, keepdims=True)
    place(fast, me_ref, flip_ref[...].T, whole_ref, outs, at + width)


def heads_back_kernel(
    gctx_ref, q2_ref, k_ref, v_ref, p_ref, ctx_ref, dqkv_ref, doth_ref, g2_ref, ds_ref, dq2_ref
):
    split_heads(gctx_ref, g2_ref)
    pairs = range(q2_ref.shape[0])
    attend_back(pairs, g2_ref, q2_ref, k_ref, v_ref, p_ref, ctx_ref, ds_ref, dq2_ref, dqkv_ref, doth_ref)


def project_back_kernel(
    fast, me_ref, base_ref, wa_ref,
    rown_ref, roth_ref, rown1_ref, roth1_ref, dqkv1_ref, doth1_ref, dqkv_ref, doth_ref,
    gs_ref, goth_ref,
    *rest,
):
    outs, whole_ref = rest[:-1], rest[-1]
    width = base_ref.shape[1]
    for index in range(3):
        cols = slice(index * width, (index + 1) * width)
        value = dot(rown_ref[...], dqkv_ref[:, cols], 0, 0) + dot(
            rown1_ref[...], dqkv1_ref[:, cols], 0, 0
        )
        if index:
            other = slice((index - 1) * width, index * width)
            value = (
                value
                + dot(roth_ref[...], doth_ref[:, other], 0, 0)
                + dot(roth1_ref[...], doth1_ref[:, other], 0, 0)
            )
        place(fast, me_ref, value, whole_ref, outs, cols.start)
    inputs_back(dqkv_ref, doth_ref, wa_ref, base_ref, gs_ref, goth_ref)


def stack_kernel(*refs):
    *parts, out_ref, sems = refs
    for copy in pull([(part, out_ref.at[index]) for index, part in enumerate(parts)], sems):
        copy.wait()


def halves_kernel(by_y_ref, by_x_ref, low_ref, high_ref, sems):
    half = low_ref.shape[0]
    moves = [(by_y_ref.at[pl.ds(0, half)], low_ref), (by_x_ref.at[pl.ds(half, half)], high_ref)]
    for copy in pull(moves, sems):
        copy.wait()


def return_kernel(info_ref, out_ref, in_ref, back_ref, out_both_ref, in_both_ref):
    local, width = back_ref.shape[0], out_ref.shape[1]
    for own_ref, target, cols in (
        (out_ref, out_both_ref, slice(0, width)),
        (in_ref, in_both_ref, slice(width, 2 * width)),
    ):
        target[info_ref[1]] = own_ref[:local, :]
        target[1 - info_ref[1]] = back_ref[:, cols].astype(F32)


def send_kernel(own_ref, more_ref, out_ref, total_ref, back_ref):
    local, width = back_ref.shape[0], own_ref.shape[1]
    for part in chunks(own_ref.shape[0], ROWS):
        total = own_ref[part, :] + more_ref[part, :].astype(F32)
        total_ref[part, :] = total
        if part.start >= local:
            target = slice(part.start - local, part.stop - local)
            back_ref[target, :width] = out_ref[part, :].astype(BF16)
            back_ref[target, width:] = total.astype(BF16)


def add_core_kernel(keep_ref, got_ref, s11a_ref, s11b_ref, s10_ref, s01_ref, s00_ref):
    half = s11a_ref.shape[0]
    for z in range(keep_ref.shape[1]):
        for index, target in ((0, s00_ref), (1, s01_ref), (2, s10_ref)):
            total = keep_ref[index, z].astype(F32) + got_ref[index, z].astype(F32)
            target[z] = total.astype(BF16)
        total = (keep_ref[3, z].astype(F32) + got_ref[3, z].astype(F32)).astype(BF16)
        if z < half:
            s11a_ref[z] = total
        else:
            s11b_ref[z - half] = total


def beside(target_ref, z, values, rows, width):
    for index in range(values.shape[0] // rows):
        target_ref[z, :, index * width : (index + 1) * width] = values[index * rows : (index + 1) * rows]


def add_half_kernel(a10_ref, ax_ref, a01_ref, ay_ref, b10_ref, bx_ref, b01_ref, by_ref, o10_ref, o01_ref):
    half = ax_ref.shape[0]
    rows, width = b10_ref.shape[1], a10_ref.shape[2]
    at = a10_ref.shape[1] // rows * width
    for z in range(2 * half):
        for tall_ref, tall_got_ref, low_ref, got_ref, out_ref, first in (
            (a10_ref, ax_ref, b10_ref, bx_ref, o10_ref, 0),
            (a01_ref, ay_ref, b01_ref, by_ref, o01_ref, half),
        ):
            if first <= z < first + half:
                tall = (tall_ref[z].astype(F32) + tall_got_ref[z - first].astype(F32)).astype(BF16)
                low = (low_ref[z].astype(F32) + got_ref[z - first].astype(F32)).astype(BF16)
            else:
                tall, low = tall_ref[z], low_ref[z]
            beside(out_ref, z, tall, rows, width)
            out_ref[z, :, at:] = low


def add_both_kernel(info_ref, a_ref, b_ref, got_x_ref, got_y_ref, own_ref, near_ref, next_ref, far_ref):
    line = info_ref[0] // 8
    rows, width = b_ref.shape[1], a_ref.shape[2]
    count = a_ref.shape[1] // rows
    for z, out_ref in enumerate((own_ref, near_ref, next_ref, far_ref)):
        at = line ^ z
        for index in range(count + 1):
            if index < count:
                cols = slice(index * width, (index + 1) * width)
                own = a_ref[at, index * rows : (index + 1) * rows]
            else:
                cols = slice(count * width, got_x_ref.shape[2])
                own = b_ref[at]
            total = own.astype(F32) + got_x_ref[at, :, cols].astype(F32) + got_y_ref[at, :, cols].astype(F32)
            out_ref[:, cols] = total.astype(BF16)


def add_pair_kernel(own_ref, got_ref, sum_ref):
    sum_ref[...] = (own_ref[...].astype(F32) + got_ref[...].astype(F32)).astype(BF16)


def add_core_all_kernel(keep_ref, got_ref, *outs):
    for z in range(keep_ref.shape[1]):
        for index, target in enumerate(outs):
            target[z] = (keep_ref[index, z].astype(F32) + got_ref[index, z].astype(F32)).astype(BF16)


def add_four_kernel(info_ref, a_ref, b_ref, c_ref, d_ref, own_ref, near_ref, next_ref, far_ref):
    line = info_ref[0] // 8
    for z, out_ref in enumerate((own_ref, near_ref, next_ref, far_ref)):
        at = line ^ z
        total = a_ref[at].astype(F32) + b_ref[at].astype(F32) + c_ref[at].astype(F32)
        out_ref[...] = (total + d_ref[at].astype(F32)).astype(BF16)


def end_both_kernel(own_ref, got_ref, far_ref, tall_ref, win_ref, wo_ref, *rest):
    vectors, flip_ref = rest[:-1], rest[-1]
    rows, width = far_ref.shape[0], tall_ref.shape[1]

    def total(cols):
        return own_ref[:, cols].astype(F32) + got_ref[:, cols].astype(F32) + far_ref[:, cols].astype(F32)

    at = tall_ref.shape[0] // rows * width
    for index in range(tall_ref.shape[0] // rows):
        tall_ref[index * rows : (index + 1) * rows, :] = total(slice(index * width, (index + 1) * width))
    for out in (win_ref, wo_ref):
        out[...] = total(slice(at, at + out.shape[1]))
        at = at + out.shape[1]
    flip_ref[...] = jnp.zeros_like(flip_ref)
    flip_ref[:rows, :] = total(slice(at, at + LANES))
    turned = flip_ref[...].T
    for index, vector in enumerate(vectors):
        vector[...] = turned[index : index + 1, :rows]


def end_kernel(a_ref, b_ref, c_ref, d_ref, *outs):
    at = 0
    for out in outs:
        cols = slice(at, at + out.shape[1])
        total = a_ref[:, cols].astype(F32) + b_ref[:, cols].astype(F32)
        out[...] = total + c_ref[:, cols].astype(F32) + d_ref[:, cols].astype(F32)
        at = at + out.shape[1]


def vm():
    return pl.BlockSpec(memory_space=pltpu.VMEM)


def run(kernel, ins, outs, scratch=(), scalars=(), loose=(), pinned=(), far=(), sems=0, micros=0.05):
    specs = [vm() for _ in ins]
    for index in scalars:
        specs[index] = pl.BlockSpec(memory_space=pltpu.SMEM)
    ins = list(ins)
    for index in loose:
        specs[index] = pl.BlockSpec(memory_space=pl.ANY)
    for index in pinned:
        specs[index] = pl.BlockSpec(memory_space=pltpu.HBM)
        ins[index] = pltpu.with_memory_space_constraint(ins[index], pltpu.HBM)
    size = sum(v.size * v.dtype.itemsize for v in ins) + sum(
        functools.reduce(lambda a, b: a * b, s, 1) * jnp.dtype(t).itemsize for s, t in outs
    )
    buffers = [pltpu.VMEM(s, t) for s, t in scratch]
    need = sum(functools.reduce(lambda a, b: a * b, s, 1) * jnp.dtype(t).itemsize for s, t in scratch)
    if sems:
        buffers.append(pltpu.SemaphoreType.DMA((sems,)))
    return pl.pallas_call(
        kernel,
        out_shape=[jax.ShapeDtypeStruct(s, t) for s, t in outs],
        in_specs=specs,
        out_specs=[pl.BlockSpec(memory_space=pl.ANY) if index in far else vm() for index in range(len(outs))],
        scratch_shapes=buffers,
        compiler_params=pltpu.CompilerParams(vmem_limit_bytes=max(need + 8 * MIB, SCOPED)),
        cost_estimate=pl.CostEstimate(
            flops=int(micros * MICRO), bytes_accessed=size, transcendentals=0
        ),
    )(*ins)


AXES = ("dp", "head")


def after(value, *others):
    return lax.optimization_barrier((value, *others))[0]


class Links:
    def __init__(self, model_rows):
        self.heads = lax.axis_size("head")
        self.pods = lax.axis_size("dp")
        self.count = self.heads * self.pods
        self.fast = self.heads == 4 and self.pods == 8 and model_rows == 16
        self.head = lax.axis_index("head")
        self.me = lax.axis_index("dp") * self.heads + self.head

    def flip(self, value, bit):
        return lax.ppermute(value, AXES, [(i, i ^ bit) for i in range(self.count)])

    def flip_head(self, value, bit):
        return lax.ppermute(value, "head", [(i, i ^ bit) for i in range(self.heads)])

    def along_z(self, block):
        return [block, *(self.flip(block, 8 * k) for k in (1, 2, 3))]

    def stack(self, parts):
        (out,) = run(
            stack_kernel, parts, [((4, *parts[0].shape), BF16)], loose=range(4), far=(0,), sems=4
        )
        return out

    def core_sums(self, keep, got):
        block = keep.shape[2:]
        whole, half = ((4, *block), BF16), ((2, *block), BF16)
        return run(add_core_kernel, [keep, got], [half, half, whole, whole, whole])

    def line_parts(self, kernel, parts, shape):
        return run(kernel, [self.info, *parts], [(shape, BF16)] * 4, scalars=(0,))

    def line_first(self, kernel, parts, shape):
        own, near, following, far = self.line_parts(kernel, parts, shape)
        return own, far, self.flip(near, 8), self.flip(following, 8)

    def line_last(self, own, far, got, got_far):
        (far,) = run(add_pair_kernel, [after(far, got), got_far], [(far.shape, BF16)])
        return own, got, self.flip(far, 24)

    def spread(self, own, group):
        held, bit = own[None], 1
        while bit < group:
            got = self.flip_head(held, bit)
            held = got if bit == 1 and group == 2 else jnp.concatenate([held, got], axis=0)
            bit = bit * 2
        if group > 2:
            held = held[1:]
        return held.reshape(-1, own.shape[1])

    def collapse(self, parts, group, rows):
        if group == 2:
            return self.flip_head(parts, 1)
        held = parts.reshape(group - 1, rows, -1)
        held = jnp.concatenate([jnp.zeros_like(held[:1]), held], axis=0).astype(F32)
        bit = group // 2
        while bit >= 1:
            held = held[:bit] + self.flip_head(held[bit : 2 * bit], bit)
            bit = bit // 2
        return held[0]


def body(
    tokens, cotangent, lengths, halting, w_query, w_key, w_value, w_out, w_in, w_hidden,
    w_halt, gain_attn, shift_attn, gain_ffn, shift_ffn,
):
    micro, local, width = tokens.shape
    links = Links(w_query.shape[0])
    fast, heads = links.fast, links.heads
    group = heads // micro
    rows, length = micro * local, local * heads
    mine = links.head // group
    wide_ff = w_in.shape[1]
    fine = width // links.count
    matrices = (w_query, w_key, w_value, w_out, w_in, w_hidden)
    vectors = (w_halt, gain_attn, shift_attn, gain_ffn, shift_ffn)
    place_array = jnp.stack([links.me, mine, links.head % group, jnp.int32(group)]).astype(jnp.int32)
    links.info = place_array

    pairs = width // LANES
    row_f, row_b = ((rows, width), F32), ((rows, width), BF16)
    stat = ((rows, LANES), F32)
    others = length - rows
    long_b = ((length, width), BF16)
    q2_t = ((pairs, 2 * rows, LANES), BF16)
    p_t = ((pairs, 2 * rows, length), BF16)
    o_t = ((2 * rows, LANES), F32)
    bias_t = ((rows, length), F32)
    inner_t = ((rows, BLOCK), F32)
    ff_b = ((rows, wide_ff), BF16)
    sums_t = ((VECS, 8, width), F32)
    ds_t = ((2 * rows, length), BF16)
    dqkv_t = ((rows, 3 * width), BF16)
    doth_t = ((others, 2 * width), BF16)
    vg_t = ((8, width), F32)
    segq_t, segk_t = ((rows, LANES), jnp.int32), ((8, length), jnp.int32)

    sort_in = [place_array, tokens, cotangent, halting]
    sort_out = [((local, 2 * width + LANES), BF16)] * 2
    sort_tmp = [((LANES, local), F32), (halting.shape, jnp.int32)]
    if fast:
        send_tok, own_tok, block_a, block_b = run(
            pack_kernel,
            [*sort_in, *matrices, jnp.pad(jnp.stack(vectors), ((0, fine - VECS), (0, LANES - fine)))],
            [*sort_out, ((4 * pairs + 1, fine, LANES), BF16), ((8, fine, BLOCK), BF16)],
            [*sort_tmp, ((LANES, LANES), F32), ((fine, LANES), BF16)],
            scalars=(0,),
            pinned=range(1, 11),
            sems=14 + 4 * pairs,
        )
        got_tok = links.flip_head(send_tok, group)
        line_a = links.along_z(block_a)
        own_a = after(links.stack(line_a), got_tok)
        by_x, by_y = links.flip(own_a, 2), links.flip(own_a, 4)
        line_b = links.along_z(after(block_b, line_a[1]))
        plane_a = [own_a, by_x, by_y, links.flip(after(by_y, line_b[3]), 2)]
    else:
        send_tok, own_tok = run(
            sort_kernel, sort_in, sort_out, sort_tmp, scalars=(0,), pinned=(1, 2, 3), sems=5
        )
        full = [lax.all_gather(part, AXES, axis=0, tiled=True) for part in matrices]
        full_v = [lax.all_gather(part, AXES, axis=0, tiled=True) for part in vectors]
        full_a = jnp.stack(full[:4])
        full_in = jnp.transpose(full[4].reshape(width, wide_ff // BLOCK, BLOCK), (1, 0, 2))
        full_hid = full[5]
        vec = jnp.pad(jnp.stack(full_v), ((0, 8 - VECS), (0, 0))).astype(F32)

        got_tok = links.flip_head(send_tok, group)
    tok, x0, rown0, sig1, segq, segk = run(
        embed_kernel,
        [place_array, lengths[:, 0], own_tok, got_tok],
        [((rows, 2 * width + LANES), BF16), row_f, row_b, row_f, segq_t, segk_t],
        scalars=(0, 1),
    )
    roth0 = links.spread(rown0, group)
    if fast:
        own_b = after(links.stack(line_b), by_x, by_y, roth0)
        near = [own_b, links.flip(own_b, 2), links.flip(own_b, 4)]
        near = near + [links.flip(piece, 1) for piece in near]
        halves = run(
            halves_kernel,
            [near[2], near[1]],
            [((2, 8, fine, BLOCK), BF16)] * 2,
            loose=(0, 1),
            far=(0, 1),
            sems=2,
        )
        far_b = [links.flip(halves[0], 2), links.flip(halves[1], 4)]
        plane_a[3] = after(plane_a[3], halves[0])
        plane_a = plane_a + [links.flip(piece, 1) for piece in plane_a]

    attend_in = [rown0, roth0, segq, segk]
    attend_out = [q2_t, long_b, long_b, p_t, row_b]
    if fast:
        full_a, vec, q2, k, v, p, ctx = run(
            functools.partial(attend_kernel, True),
            [*attend_in, links.info, *plane_a],
            [((5, 4, 8, fine, BLOCK), BF16), vg_t, *attend_out],
            [row_b, bias_t, o_t],
            scalars=(4,),
            micros=8,
        )
        full_a = full_a.reshape(5, width, BLOCK)
    else:
        q2, k, v, p, ctx = run(
            functools.partial(attend_kernel, False),
            [*attend_in, full_a],
            attend_out,
            [row_b, bias_t, o_t],
            micros=8,
        )
    n1, r1, nlow = run(norm_kernel, [x0, ctx, vec, full_a], [row_f, stat, row_b], [row_f], micros=1)
    ffn_out = [ff_b, ff_b, row_f, stat, stat, row_f, row_f, row_f, row_b]
    ffn_in = [n1, nlow, tok, sig1, vec]
    if fast:
        far_b = [after(piece, ctx) for piece in far_b]
        far_b = far_b + [links.flip(piece, 1) for piece in far_b]
        full_in, full_hid, *got = run(
            functools.partial(ffn_kernel, True),
            [*ffn_in, links.info, *near, *far_b],
            [((4, 4, 8, fine, BLOCK), BF16), ((4, 8, 4, fine, BLOCK), BF16), *ffn_out],
            [inner_t, row_f],
            scalars=(5,),
            micros=5.5,
        )
        full_in = full_in.reshape(4, width, BLOCK)
        full_hid = full_hid.reshape(wide_ff, width)
    else:
        got = run(
            functools.partial(ffn_kernel, False),
            [*ffn_in, full_in, full_hid],
            ffn_out,
            [inner_t, row_f],
            micros=5.5,
        )
    hid, dg, n2, r2, rate, state, pooled, x1, rown1 = got
    roth1 = links.spread(rown1, group)
    out, gs, goth, nlow1, hid1, b11, b21, ctx1, b01, dqkv1, doth1, vg1 = run(
        turn_kernel,
        [x1, rown1, roth1, full_a, full_in, full_hid, vec, segq, segk, state, pooled, tok],
        [row_f, row_f, ((others, width), BF16), row_b, ff_b, ff_b, row_b, row_b, row_b, dqkv_t, doth_t, vg_t],
        [
            row_b, q2_t, long_b, long_b, p_t, bias_t, o_t, row_f, row_f, stat, inner_t, ff_b,
            row_f, stat, stat, row_f, row_f, sums_t, row_b, q2_t, ds_t,
        ],
        micros=15.7,
    )
    more = links.collapse(goth, group, rows)

    b_cols = wide_ff + width + LANES
    def parts_of(shape, whole):
        return [((4, 4, *shape), BF16)] * 2 if fast else [(whole, F32)]

    hid_out = parts_of((4 * fine, width), (wide_ff, width))
    in_out = parts_of((fine, b_cols), (width, b_cols))
    attend_outs = parts_of((fine, 3 * width), (width, 3 * width))
    whole_shape = (4, 8, fine, BLOCK) if fast else (16, LANES)
    tall_shape = (8, 4 * fine, width) if fast else (16, LANES)
    b2, gsec, base, sums, *hid_parts = run(
        functools.partial(hidden_back_kernel, fast),
        [links.info, gs, more, tok, vec, n2, r2, rate, hid, hid1, b21],
        [row_b, row_f, row_f, sums_t, *hid_out],
        [(tall_shape, BF16)],
        scalars=(0,),
        micros=2,
    )
    b1, b0, base, gctx, sums = run(
        feed_back_kernel,
        [b2, gsec, base, sums, vec, full_in, full_hid, full_a, n1, r1, dg],
        [ff_b, row_b, row_f, row_b, sums_t],
        [inner_t, row_f],
        micros=2.2,
    )
    if fast:
        c_sums = links.core_sums(hid_parts[0], links.flip(hid_parts[1], 1))
        b1 = after(b1, c_sums[0])
    in_parts = run(
        functools.partial(weights_back_kernel, fast),
        [links.info, b1, b0, sums, nlow, ctx, nlow1, b11, ctx1, b01, vg1],
        in_out,
        [(whole_shape, BF16), ((LANES, width), F32)],
        scalars=(0,),
        micros=2,
    )
    if fast:
        b_sums = links.core_sums(in_parts[0], links.flip(in_parts[1], 1))
        gctx = after(gctx, b_sums[0])
    dqkv0, doth0 = run(
        heads_back_kernel,
        [gctx, q2, k, v, p, ctx],
        [dqkv_t, doth_t],
        [q2_t, ds_t, o_t],
        micros=3,
    )
    g0, goth0, *attend_parts = run(
        functools.partial(project_back_kernel, fast),
        [links.info, base, full_a, rown0, roth0, rown1, roth1, dqkv1, doth1, dqkv0, doth0],
        [row_f, ((others, width), BF16), *attend_outs],
        [(whole_shape, BF16)],
        scalars=(0,),
    )
    if fast:
        c11a, c11b, c10, c01, c00 = c_sums
        b11a, b11b, b10, b01, b00 = b_sums
        halves = [
            after(c10, g0), links.flip(c11a, 2), c01, links.flip(c11b, 4),
            b10, links.flip(b11a, 2), b01, links.flip(b11b, 4),
        ]
        both_t = ((4, fine, 4 * width + b_cols), BF16)
        both10, both01 = run(add_half_kernel, halves, [both_t] * 2)
        goth0, send_a = after(goth0, both01), after(attend_parts[1], both01)
    inputs, back = run(
        send_kernel,
        [g0, links.collapse(goth0, group, rows), out],
        [row_f, ((local, 2 * width), BF16)],
    )
    if fast:
        keep, got = after(attend_parts[0], back), links.flip(send_a, 1)
        a00, a01, a10, a11 = run(add_core_all_kernel, [keep, got], [(keep.shape[1:], BF16)] * 4)
        by_plane = [a00, links.flip(a11, 6), links.flip(a01, 2), links.flip(a10, 4)]
        both = links.line_first(
            add_both_kernel, [after(c00, a00), b00, links.flip(both01, 2), links.flip(both10, 4)], both_t[0][1:]
        )
        first_sums = both[0]
        by_plane[0] = after(by_plane[0], both[0])
        attend_sums = links.line_parts(add_four_kernel, by_plane, a00.shape[1:])
        both = links.line_last(both[0], after(both[1], attend_sums[0]), *both[2:])
        attend_sums = [attend_sums[0], *(links.flip(attend_sums[k], 8 * k) for k in (1, 2, 3))]
        back = after(back, first_sums)
        output, input_grad = run(
            return_kernel,
            [links.info, out, inputs, links.flip_head(back, group)],
            [((micro, local, width), F32)] * 2,
            scalars=(0,),
        )
        g_hidden, g_in, g_out, *g_vectors = run(
            end_both_kernel,
            [after(both[0], output), *both[1:]],
            [((4 * fine, width), F32), ((fine, wide_ff), F32), ((fine, width), F32)] + [((1, fine), F32)] * VECS,
            [((LANES, LANES), F32)],
        )
        g_query, g_key, g_value = run(
            end_kernel,
            [after(attend_sums[0], output, g_hidden), *attend_sums[1:]],
            [((fine, width), F32)] * 3,
        )
        g_vectors = [vector.reshape(fine) for vector in g_vectors]
    else:
        sums = [
            *(attend_parts[0][:, index * width : (index + 1) * width] for index in range(3)),
            in_parts[0][:, wide_ff : wide_ff + width], in_parts[0][:, :wide_ff], hid_parts[0],
            in_parts[0][:, wide_ff + width :],
        ]
        sums = [lax.psum_scatter(part, AXES, scatter_dimension=0, tiled=True) for part in sums]
        g_query, g_key, g_value, g_out, g_in, g_hidden, g_vec = sums
        g_vectors = [g_vec[:, index] for index in range(VECS)]
        output, input_grad = run(
            return_kernel,
            [links.info, out, inputs, links.flip_head(back, group)],
            [((micro, local, width), F32)] * 2,
            scalars=(0,),
        )
    return (output, input_grad, g_query, g_key, g_value, g_out, g_in, g_hidden, *g_vectors)


def solution(mesh):
    whole = P(("dp", "head"))
    matrix = P(("dp", "head"), None)
    rows = P(None, ("dp", "head"), None)
    return jax.shard_map(
        body,
        mesh=mesh,
        in_specs=(rows, rows, P(None, "dp", None), P(None, None, ("dp", "head")))
        + (matrix,) * 6
        + (whole,) * 5,
        out_specs=(rows, rows) + (matrix,) * 6 + (whole,) * 5,
        check_vma=False,
    )
```

```python
import functools

import jax
import jax.numpy as jnp
from jax import lax
from jax.experimental import pallas as pl
from jax.experimental.pallas import tpu as pltpu
from jax.sharding import PartitionSpec as P

HD = 64
EPSILON = 1e-06
F32 = jnp.float32
BF16 = jnp.bfloat16
LANES = 128
ROWS = 32
ATT_ROWS = 256
BLOCK = 512
VECS = 5
MIB = 1024 * 1024
SCOPED = 20 * MIB
MICRO = 1.15e9
GELU_A = 0.7978845608028654
GELU_B = 0.044715


def dot(a, b, ca=1, cb=0):
    return lax.dot_general(a, b, (((ca,), (cb,)), ((), ())), preferred_element_type=F32)


def chunks(total, size):
    size = min(size, total)
    return [slice(i, i + size) for i in range(0, total, size)]


def wide(column):
    return jnp.broadcast_to(column, (column.shape[0], LANES))


def mean(values):
    return jnp.sum(values, axis=-1, keepdims=True) * (1.0 / values.shape[-1])


def fold(values):
    return jnp.sum(values.reshape(values.shape[0] // 8, 8, values.shape[1]), axis=0)


class Flat:
    def __init__(self, ref):
        self.ref = ref

    def __getitem__(self, index):
        if index is Ellipsis:
            index = (slice(None), slice(None))
        value = self.ref[..., index[1]]
        return value.reshape(-1, value.shape[-1])[index[0]]


def matrix(ref, index):
    value = ref[index]
    return value.reshape(-1, value.shape[-1])


def head_mask(rows):
    lane = lax.broadcasted_iota(jnp.int32, (rows, LANES), 1)
    return lane < HD


def normalize(values):
    center = values - mean(values)
    inverse = lax.rsqrt(mean(center * center) + EPSILON)
    return center * inverse, inverse


def normalize_back(unit, inverse, grad):
    return inverse * (grad - mean(grad) - unit * mean(grad * unit))


def split_heads(values_ref, stacked_ref):
    rows = values_ref.shape[0]
    for part in chunks(rows, ATT_ROWS):
        first = head_mask(part.stop - part.start)
        for pair in range(stacked_ref.shape[0]):
            block = values_ref[part, pair * LANES : (pair + 1) * LANES].astype(F32)
            stacked_ref[pair, part, :] = jnp.where(first, block, 0.0).astype(BF16)
            stacked_ref[pair, rows + part.start : rows + part.stop, :] = jnp.where(
                first, 0.0, block
            ).astype(BF16)


def project(rown_ref, roth_ref, wa_ref, q_ref, q2_ref, k_ref, v_ref):
    rows, width = rown_ref.shape
    q_ref[...] = (
        dot(rown_ref[...], matrix(wa_ref, 0)).astype(BF16).astype(F32) * HD**-0.5
    ).astype(BF16)
    split_heads(q_ref, q2_ref)
    for at, source in ((0, rown_ref), (rows, roth_ref)):
        span = slice(at, at + source.shape[0])
        k_ref[span, :] = dot(source[...], matrix(wa_ref, 1)).astype(BF16)
        v_ref[span, :] = dot(source[...], matrix(wa_ref, 2)).astype(BF16)


def set_bias(segq_ref, segk_ref, bias_ref):
    for part in chunks(bias_ref.shape[0], ROWS):
        bias_ref[part, :] = jnp.where(segq_ref[part, 0:1] == segk_ref[0:1, :], 0.0, -1e30)


def attend(q2_ref, k_ref, v_ref, bias_ref, p_ref, ctx_ref, o_ref):
    rows, length = bias_ref.shape
    for pair in range(q2_ref.shape[0]):
        cols = slice(pair * LANES, (pair + 1) * LANES)
        for part in chunks(2 * rows, 2 * rows):
            scores = dot(q2_ref[pair, part, :], k_ref[:, cols], 1, 1)
            scores = (scores.reshape(2, rows, length) + bias_ref[...][None]).reshape(2 * rows, length)
            weights = jnp.exp(scores - jnp.max(scores, axis=-1, keepdims=True))
            inverse = 1.0 / jnp.sum(weights, axis=-1, keepdims=True)
            low = (weights * inverse).astype(BF16)
            p_ref[pair, part, :] = low
            o_ref[part, :] = dot(low, v_ref[:, cols])
        for part in chunks(rows, ATT_ROWS):
            first = head_mask(part.stop - part.start)
            second = o_ref[rows + part.start : rows + part.stop, :]
            ctx_ref[part, cols] = jnp.where(first, o_ref[part, :], second).astype(BF16)


def first_norm(x_ref, ctx_ref, wa_ref, vec_ref, acc_ref, n1_ref, r1_ref, nlow_ref):
    acc_ref[...] = dot(ctx_ref[...], matrix(wa_ref, 3))
    for part in chunks(x_ref.shape[0], ROWS):
        unit, inverse = normalize(x_ref[part, :] + acc_ref[part, :])
        n1_ref[part, :] = unit
        r1_ref[part, :] = wide(inverse)
        nlow_ref[part, :] = (unit * vec_ref[1:2, :] + vec_ref[2:3, :]).astype(BF16)


def feed_forward(nlow_ref, win_ref, whid_ref, inner_ref, hid_ref, dg_ref, acc_ref):
    rows = nlow_ref.shape[0]
    for cols in chunks(hid_ref.shape[1], BLOCK):
        inner_ref[...] = dot(nlow_ref[...], matrix(win_ref, cols.start // BLOCK))
        for part in chunks(rows, ROWS):
            x = inner_ref[part, :]
            square = x * x
            t = jnp.tanh(x * (GELU_A + GELU_A * GELU_B * square))
            half = 0.5 + 0.5 * t
            hid_ref[part, cols] = (x * half).astype(BF16)
            slope = 0.5 * x * (1.0 - t * t) * (GELU_A + 3.0 * GELU_A * GELU_B * square)
            dg_ref[part, cols] = (half + slope).astype(BF16)
    acc_ref[...] = dot(hid_ref[...], whid_ref[...])


def second_norm(part, vec_ref, n1_ref, acc_ref):
    normed = n1_ref[part, :] * vec_ref[1:2, :] + vec_ref[2:3, :]
    unit, inverse = normalize(normed + acc_ref[part, :])
    updated = unit * vec_ref[3:4, :] + vec_ref[4:5, :]
    rate = jax.nn.sigmoid(jnp.sum(updated * vec_ref[0:1, :], axis=-1, keepdims=True))
    return unit, inverse, updated, rate


def tail_back(
    part, step, gs, gp, halt_ref, vec_ref, n2_ref, r2_ref, rate_ref, b2_ref, gsec_ref, base_ref, sums_ref
):
    width = n2_ref.shape[1]
    keep = halt_ref[part, 2 * width + step : 2 * width + step + 1].astype(F32)
    unit = n2_ref[part, :]
    updated = unit * vec_ref[3:4, :] + vec_ref[4:5, :]
    rate = rate_ref[part, 0:1]
    logit = keep * jnp.sum(gp * updated, axis=-1, keepdims=True) * rate * (1.0 - rate)
    grad = keep * gs + (keep * rate) * gp + logit * vec_ref[0:1, :]
    base_ref[part, :] = gs - keep * gs
    sums_ref[0] += fold(logit * updated)
    sums_ref[3] += fold(grad * unit)
    sums_ref[4] += fold(grad)
    back = normalize_back(unit, r2_ref[part, 0:1], grad * vec_ref[3:4, :])
    gsec_ref[part, :] = back
    b2_ref[part, :] = back.astype(BF16)


def feed_back(b2_ref, dg_ref, win_ref, whid_ref, inner_ref, b1_ref, acc_ref):
    rows = b2_ref.shape[0]
    for cols in chunks(dg_ref.shape[1], BLOCK):
        inner_ref[...] = dot(b2_ref[...], whid_ref[cols, :], 1, 1)
        for part in chunks(rows, ROWS):
            b1_ref[part, cols] = (inner_ref[part, :] * dg_ref[part, cols].astype(F32)).astype(BF16)
    total = None
    for cols in chunks(dg_ref.shape[1], BLOCK):
        value = dot(b1_ref[:, cols], matrix(win_ref, cols.start // BLOCK), 1, 1)
        total = value if total is None else total + value
    acc_ref[...] = total


def middle_back(gsec_ref, acc_ref, vec_ref, n1_ref, r1_ref, b0_ref, base_ref, sums_ref):
    for part in chunks(gsec_ref.shape[0], ROWS):
        grad = gsec_ref[part, :] + acc_ref[part, :]
        unit = n1_ref[part, :]
        sums_ref[1] += fold(grad * unit)
        sums_ref[2] += fold(grad)
        back = normalize_back(unit, r1_ref[part, 0:1], grad * vec_ref[1:2, :])
        base_ref[part, :] += back
        b0_ref[part, :] = back.astype(BF16)


def attend_back(
    pairs, g2_ref, q2_ref, k_ref, v_ref, p_ref, ctx_ref, ds_ref, dq2_ref, dqkv_ref, doth_ref
):
    rows, width = ctx_ref.shape
    for pair in pairs:
        cols = slice(pair * LANES, (pair + 1) * LANES)
        for part in chunks(2 * rows, 2 * rows):
            grad = g2_ref[pair, part, :]
            both = jnp.concatenate([ctx_ref[:, cols]] * 2, axis=0)
            delta = jnp.sum(grad.astype(F32) * both.astype(F32), axis=-1, keepdims=True)
            back = dot(grad, v_ref[:, cols], 1, 1)
            low = (p_ref[pair, part, :].astype(F32) * (back - delta)).astype(BF16)
            ds_ref[part, :] = low
            dq2_ref[part, :] = dot(low, k_ref[:, cols])
        for part in chunks(rows, ATT_ROWS):
            first = head_mask(part.stop - part.start)
            second = dq2_ref[rows + part.start : rows + part.stop, :]
            dqkv_ref[part, cols] = (
                jnp.where(first, dq2_ref[part, :], second) * HD**-0.5
            ).astype(BF16)
        for index, (left, right) in enumerate(
            ((ds_ref[...], q2_ref[pair]), (p_ref[pair], g2_ref[pair]))
        ):
            both = dot(right, left, 0, 0).T.astype(BF16)
            at = index * width + pair * LANES
            dqkv_ref[:, width + at : width + at + LANES] = both[:rows]
            doth_ref[:, at : at + LANES] = both[rows:]


def inputs_back(dqkv_ref, doth_ref, wa_ref, base_ref, gs_ref, goth_ref):
    width = base_ref.shape[1]
    parts = [slice(index * width, (index + 1) * width) for index in range(3)]
    total = base_ref[...]
    for index, cols in enumerate(parts):
        total = total + dot(dqkv_ref[:, cols], matrix(wa_ref, index), 1, 1)
    gs_ref[...] = total
    total = dot(doth_ref[:, parts[0]], matrix(wa_ref, 1), 1, 1)
    goth_ref[...] = (total + dot(doth_ref[:, parts[1]], matrix(wa_ref, 2), 1, 1)).astype(BF16)


def fetch(pieces, cores, bits, start, store, me_ref):
    line, place_in = me_ref[0] // 8, me_ref[0] % 8
    for piece, core, bit in zip(pieces, cores, bits):
        for z in range(piece.shape[0]):
            store(piece, z, line ^ (start + z), place_in ^ (bit | core))


def embed_kernel(place_ref, sizes_ref, tok_ref, got_ref, own_ref, x_ref, rown_ref, sig_ref, segq_ref, segk_ref):
    mine, place_in, group = place_ref[1], place_ref[2], place_ref[3]
    local = tok_ref.shape[0]
    half = x_ref.shape[1] // 2
    ends, starts, total = [], [], 0
    for index in range(sizes_ref.shape[1]):
        starts.append(total)
        total = total + sizes_ref[mine, index]
        ends.append(total)
    ones = jnp.exp(
        lax.broadcasted_iota(jnp.int32, (8, half), 1).astype(F32)
        * (-jnp.log(jnp.full((8, half), 10000.0, F32)) / max(half - 1, 1))
    )
    rates = ones[0:1, :]
    first_sin, first_cos = jnp.sin(rates), jnp.cos(rates)
    for part in chunks(x_ref.shape[0], ROWS):
        size = part.stop - part.start
        block = mine * group + place_in
        block = block if part.start < local else block ^ group
        at = block * local + part.start % local
        token = at + lax.broadcasted_iota(jnp.int32, (size, LANES), 0)
        segment = jnp.zeros((size, LANES), jnp.int32)
        begin = jnp.zeros((size, LANES), jnp.int32)
        for start, end in zip(starts, ends):
            segment = segment + jnp.where(token >= end, 1, 0)
            begin = jnp.maximum(begin, jnp.where(token >= start, start, 0))
        segq_ref[part, :] = segment
        angles = (token - begin).astype(F32)[:, 0:1] * rates
        if part.start < local:
            low = tok_ref[part, :]
        else:
            low = got_ref[part.start - local : part.stop - local, :]
        own_ref[part, :] = low
        for cols, moving, still, step in (
            (slice(0, half), jnp.sin(angles), 0.0, first_sin),
            (slice(half, 2 * half), jnp.cos(angles), 1.0, first_cos),
        ):
            inputs = low[:, cols].astype(F32) + (moving + still)
            x_ref[part, cols] = inputs
            rown_ref[part, cols] = inputs.astype(BF16)
            sig_ref[part, cols] = moving + step
    blocks = segk_ref.shape[1] // local
    for index in range(blocks):
        peer = mine * group + (place_in ^ (index // 2))
        peer = peer if index % 2 == 0 else peer ^ group
        token = peer * local + lax.broadcasted_iota(jnp.int32, (8, local), 1)
        segment = jnp.zeros((8, local), jnp.int32)
        for end in ends:
            segment = segment + jnp.where(token >= end, 1, 0)
        segk_ref[:, index * local : (index + 1) * local] = segment


def pull(sources, sems):
    copies = [
        pltpu.make_async_copy(source, target, sems.at[index]) for index, (source, target) in enumerate(sources)
    ]
    for copy in copies:
        copy.start()
    return copies


def sort_rows(place_ref, tok_ref, cot_ref, halt_ref, refs, sems):
    mine = place_ref[1]
    width = tok_ref.shape[2]
    send_ref, own_ref, flip_ref, flags_ref = refs
    moves = [(halt_ref, flags_ref)]
    for micro, target in ((1 - mine, send_ref), (mine, own_ref)):
        moves.append((tok_ref.at[micro], target.at[:, :width]))
        moves.append((cot_ref.at[micro], target.at[:, width : 2 * width]))
    copies = pull(moves, sems)
    flip_ref[...] = jnp.zeros_like(flip_ref)
    for copy in copies:
        copy.wait()
    for target, micro in ((own_ref, mine), (send_ref, 1 - mine)):
        for step in range(halt_ref.shape[0]):
            flip_ref[step : step + 1, :] = flags_ref[step, pl.ds(micro, 1), :].astype(F32)
        target[:, 2 * width :] = flip_ref[...].T.astype(BF16)


def sort_kernel(place_ref, tok_ref, cot_ref, halt_ref, *refs):
    sort_rows(place_ref, tok_ref, cot_ref, halt_ref, refs[:4], refs[4])


def pack_kernel(place_ref, tok_ref, cot_ref, halt_ref, q_ref, k_ref, v_ref, o_ref, win_ref, whid_ref, *rest):
    vectors, rest = rest[:VECS], rest[VECS:]
    sorted_refs, (block_ref, tall_ref, flip_ref, flags_ref, turn_ref, low_ref, sems) = rest[:2], rest[2:]
    rows, width = q_ref.shape
    moves = [(vector, low_ref.at[index]) for index, vector in enumerate(vectors)]
    lanes = width // LANES
    for index, source in enumerate((q_ref, k_ref, v_ref, o_ref)):
        for part in range(lanes):
            cols = slice(part * LANES, (part + 1) * LANES)
            moves.append((source.at[:, cols], block_ref.at[index * lanes + part]))
    for index in range(4):
        moves.append((win_ref.at[:, index * BLOCK : (index + 1) * BLOCK], tall_ref.at[index]))
        moves.append((whid_ref.at[index * rows : (index + 1) * rows, :], tall_ref.at[4 + index]))
    count = len(moves)
    copies = pull(moves, sems.at[:count])
    sort_rows(place_ref, tok_ref, cot_ref, halt_ref, [*sorted_refs, flip_ref, flags_ref], sems.at[count:])
    turn_ref[...] = jnp.zeros_like(turn_ref)
    for copy in copies:
        copy.wait()
    for index in range(VECS):
        turn_ref[index : index + 1, :rows] = low_ref[index].astype(F32)
    block_ref[4 * lanes] = turn_ref[...].T[:rows, :].astype(BF16)


def attend_kernel(
    fast, rown_ref, roth_ref, segq_ref, segk_ref, *rest,
):
    if fast:
        me_ref, plane, rest = rest[0], rest[1:9], rest[9:]
        wa_ref, vec_ref, q2_ref, k_ref, v_ref, p_ref, ctx_ref, q_ref, bias_ref, o_ref = rest

        def store(piece, z, line, place):
            lanes = wa_ref.shape[4] // LANES
            for chunk in range(piece.shape[1]):
                cols = slice(chunk % lanes * LANES, (chunk % lanes + 1) * LANES)
                wa_ref[chunk // lanes, line, place, :, cols] = piece[z, chunk]

        fetch(plane, (0, 0, 0, 0, 1, 1, 1, 1), (0, 2, 4, 6) * 2, 0, store, me_ref)
        vec_ref[...] = matrix(wa_ref, 4)[:, :LANES].astype(F32).T[0:8, :]
    else:
        wa_ref, q2_ref, k_ref, v_ref, p_ref, ctx_ref, q_ref, bias_ref, o_ref = rest
    set_bias(segq_ref, segk_ref, bias_ref)
    project(rown_ref, roth_ref, wa_ref, q_ref, q2_ref, k_ref, v_ref)
    attend(q2_ref, k_ref, v_ref, bias_ref, p_ref, ctx_ref, o_ref)


def norm_kernel(x_ref, ctx_ref, vec_ref, wa_ref, n1_ref, r1_ref, nlow_ref, acc_ref):
    first_norm(x_ref, ctx_ref, wa_ref, vec_ref, acc_ref, n1_ref, r1_ref, nlow_ref)


def ffn_kernel(fast, n1_ref, nlow_ref, tok_ref, sig_ref, vec_ref, *rest):
    if fast:
        me_ref, near, far, rest = rest[0], rest[1:7], rest[7:11], rest[11:]
        (win_ref, full_ref), rest = rest[:2], rest[2:]
    else:
        (win_ref, whid_ref), rest = rest[:2], rest[2:]
    (
        hid_ref, dg_ref, n2_ref, r2_ref, rate_ref, state_ref, pooled_ref, next_ref, rown_ref,
        inner_ref, acc_ref,
    ) = rest
    if fast:

        def store(piece, z, line, place):
            for chunk in range(4):
                win_ref[chunk, line, place] = piece[z, chunk]
                full_ref[line, place, chunk] = piece[z, 4 + chunk]

        fetch(near, (0, 0, 0, 1, 1, 1), (0, 2, 4, 0, 2, 4), 0, store, me_ref)
        fetch((far[0], far[2]), (0, 1), (6, 6), 0, store, me_ref)
        fetch((far[1], far[3]), (0, 1), (6, 6), 2, store, me_ref)
        whid_ref = Flat(full_ref)
    width = n1_ref.shape[1]
    feed_forward(nlow_ref, win_ref, whid_ref, inner_ref, hid_ref, dg_ref, acc_ref)
    for part in chunks(tok_ref.shape[0], ROWS):
        unit, inverse, updated, rate = second_norm(part, vec_ref, n1_ref, acc_ref)
        keep = tok_ref[part, 2 * width : 2 * width + 1].astype(F32)
        n2_ref[part, :] = unit
        r2_ref[part, :] = wide(inverse)
        rate_ref[part, :] = wide(rate)
        pooled_ref[part, :] = (keep * rate) * updated
        state = tok_ref[part, :width].astype(F32)
        state = state + keep * (updated - state)
        state_ref[part, :] = state
        inputs = state + sig_ref[part, :]
        next_ref[part, :] = inputs
        rown_ref[part, :] = inputs.astype(BF16)


def turn_kernel(
    x_ref, rown_ref, roth_ref, wa_ref, win_ref, whid_ref, vec_ref, segq_ref, segk_ref,
    state_ref, pooled_ref, tok_ref,
    out_ref, gs_ref, goth_ref, nlow_ref, hid_ref, b1_ref, b2_ref, ctx_ref, b0_ref, dqkv_ref, doth_ref, vg_ref,
    q_ref, q2_ref, k_ref, v_ref, p_ref, bias_ref, o_ref, acc_ref, n1_ref, r1_ref, inner_ref, dg_ref,
    n2_ref, r2_ref, rate_ref, gsec_ref, base_ref, sums_ref, gctx_ref, g2_ref, ds_ref,
):
    width = x_ref.shape[1]
    sums_ref[...] = jnp.zeros_like(sums_ref)
    set_bias(segq_ref, segk_ref, bias_ref)
    project(rown_ref, roth_ref, wa_ref, q_ref, q2_ref, k_ref, v_ref)
    attend(q2_ref, k_ref, v_ref, bias_ref, p_ref, ctx_ref, o_ref)
    first_norm(x_ref, ctx_ref, wa_ref, vec_ref, acc_ref, n1_ref, r1_ref, nlow_ref)
    feed_forward(nlow_ref, win_ref, whid_ref, inner_ref, hid_ref, dg_ref, acc_ref)
    for part in chunks(x_ref.shape[0], ROWS):
        unit, inverse, updated, rate = second_norm(part, vec_ref, n1_ref, acc_ref)
        keep = tok_ref[part, 2 * width + 1 : 2 * width + 2].astype(F32)
        n2_ref[part, :] = unit
        r2_ref[part, :] = wide(inverse)
        rate_ref[part, :] = wide(rate)
        state = state_ref[part, :]
        state = state + keep * (updated - state)
        out_ref[part, :] = state + (pooled_ref[part, :] + (keep * rate) * updated)
        cot = tok_ref[part, width : 2 * width].astype(F32)
        tail_back(
            part, 1, cot, cot, tok_ref, vec_ref, n2_ref, r2_ref, rate_ref, b2_ref, gsec_ref, base_ref,
            sums_ref,
        )
    feed_back(b2_ref, dg_ref, win_ref, whid_ref, inner_ref, b1_ref, acc_ref)
    middle_back(gsec_ref, acc_ref, vec_ref, n1_ref, r1_ref, b0_ref, base_ref, sums_ref)
    gctx_ref[...] = dot(b0_ref[...], matrix(wa_ref, 3), 1, 1).astype(BF16)
    split_heads(gctx_ref, g2_ref)
    pairs = range(q2_ref.shape[0])
    attend_back(pairs, g2_ref, q2_ref, k_ref, v_ref, p_ref, ctx_ref, ds_ref, o_ref, dqkv_ref, doth_ref)
    inputs_back(dqkv_ref, doth_ref, wa_ref, base_ref, gs_ref, goth_ref)
    vg_ref[...] = jnp.zeros_like(vg_ref)
    for index in range(VECS):
        vg_ref[index : index + 1, :] = jnp.sum(sums_ref[index], axis=0, keepdims=True)


def place(fast, me_ref, value, scratch_ref, outs, at):
    cols = slice(at, at + value.shape[1])
    if not fast:
        outs[0][:, cols] = value
        return
    low = value.astype(BF16)
    scratch_ref[:, :, :, : value.shape[1]] = low.reshape(scratch_ref.shape[:3] + value.shape[1:])
    for relative in range(8):
        block = scratch_ref[:, relative ^ (me_ref[0] % 8), :, : value.shape[1]]
        outs[relative % 2][relative // 2, :, :, cols] = block


def hidden_back_kernel(
    fast, me_ref, gs_ref, more_ref, tok_ref, vec_ref,
    n2_ref, r2_ref, rate_ref, hid_ref, hid1_ref, b21_ref,
    b2_ref, gsec_ref, base_ref, sums_ref,
    *rest,
):
    outs, tall_ref = rest[:-1], rest[-1]
    sums_ref[...] = jnp.zeros_like(sums_ref)
    width = gs_ref.shape[1]
    for part in chunks(gs_ref.shape[0], ROWS):
        tail_back(
            part, 0, gs_ref[part, :] + more_ref[part, :].astype(F32),
            tok_ref[part, width : 2 * width].astype(F32), tok_ref, vec_ref,
            n2_ref, r2_ref, rate_ref, b2_ref, gsec_ref, base_ref, sums_ref,
        )
    hidden_rows = hid_ref.shape[1] // 4
    for z in range(4):
        span = slice(z * hidden_rows, (z + 1) * hidden_rows)
        value = dot(hid_ref[:, span], b2_ref[...], 0, 0) + dot(hid1_ref[:, span], b21_ref[...], 0, 0)
        if fast:
            tall_ref[...] = value.astype(BF16).reshape(tall_ref.shape)
            for relative in range(8):
                outs[relative % 2][relative // 2, z] = tall_ref[relative ^ (me_ref[0] % 8)]
        else:
            outs[0][span, :] = value


def feed_back_kernel(
    b2_ref, gsec_ref, base0_ref, sums0_ref, vec_ref, win_ref, whid_ref, wa_ref, n1_ref, r1_ref, dg_ref,
    b1_ref, b0_ref, base_ref, gctx_ref, sums_ref, inner_ref, acc_ref,
):
    sums_ref[...] = sums0_ref[...]
    base_ref[...] = base0_ref[...]
    feed_back(b2_ref, dg_ref, win_ref, whid_ref, inner_ref, b1_ref, acc_ref)
    middle_back(gsec_ref, acc_ref, vec_ref, n1_ref, r1_ref, b0_ref, base_ref, sums_ref)
    gctx_ref[...] = dot(b0_ref[...], matrix(wa_ref, 3), 1, 1).astype(BF16)


def weights_back_kernel(
    fast, me_ref, b1_ref, b0_ref, sums_ref, nlow_ref, ctx_ref, nlow1_ref, b11_ref, ctx1_ref, b01_ref, vg1_ref,
    *rest,
):
    outs, (whole_ref, flip_ref) = rest[:-2], rest[-2:]
    width = ctx_ref.shape[1]
    for cols in chunks(b1_ref.shape[1], BLOCK):
        value = dot(nlow_ref[...], b1_ref[:, cols], 0, 0) + dot(nlow1_ref[...], b11_ref[:, cols], 0, 0)
        place(fast, me_ref, value, whole_ref, outs, cols.start)
    value = dot(ctx_ref[...], b0_ref[...], 0, 0) + dot(ctx1_ref[...], b01_ref[...], 0, 0)
    at = b1_ref.shape[1]
    place(fast, me_ref, value, whole_ref, outs, at)
    flip_ref[...] = jnp.zeros_like(flip_ref)
    flip_ref[0:8, :] = vg1_ref[...]
    for index in range(VECS):
        flip_ref[index : index + 1, :] += jnp.sum(sums_ref[index], axis=0, keepdims=True)
    place(fast, me_ref, flip_ref[...].T, whole_ref, outs, at + width)


def heads_back_kernel(
    gctx_ref, q2_ref, k_ref, v_ref, p_ref, ctx_ref, dqkv_ref, doth_ref, g2_ref, ds_ref, dq2_ref
):
    split_heads(gctx_ref, g2_ref)
    pairs = range(q2_ref.shape[0])
    attend_back(pairs, g2_ref, q2_ref, k_ref, v_ref, p_ref, ctx_ref, ds_ref, dq2_ref, dqkv_ref, doth_ref)


def project_back_kernel(
    fast, me_ref, base_ref, wa_ref,
    rown_ref, roth_ref, rown1_ref, roth1_ref, dqkv1_ref, doth1_ref, dqkv_ref, doth_ref,
    gs_ref, goth_ref,
    *rest,
):
    outs, whole_ref = rest[:-1], rest[-1]
    width = base_ref.shape[1]
    for index in range(3):
        cols = slice(index * width, (index + 1) * width)
        value = dot(rown_ref[...], dqkv_ref[:, cols], 0, 0) + dot(
            rown1_ref[...], dqkv1_ref[:, cols], 0, 0
        )
        if index:
            other = slice((index - 1) * width, index * width)
            value = (
                value
                + dot(roth_ref[...], doth_ref[:, other], 0, 0)
                + dot(roth1_ref[...], doth1_ref[:, other], 0, 0)
            )
        place(fast, me_ref, value, whole_ref, outs, cols.start)
    inputs_back(dqkv_ref, doth_ref, wa_ref, base_ref, gs_ref, goth_ref)


def stack_kernel(*refs):
    *parts, out_ref, sems = refs
    for copy in pull([(part, out_ref.at[index]) for index, part in enumerate(parts)], sems):
        copy.wait()


def halves_kernel(by_y_ref, by_x_ref, low_ref, high_ref, sems):
    half = low_ref.shape[0]
    moves = [(by_y_ref.at[pl.ds(0, half)], low_ref), (by_x_ref.at[pl.ds(half, half)], high_ref)]
    for copy in pull(moves, sems):
        copy.wait()


def return_kernel(info_ref, out_ref, in_ref, back_ref, out_both_ref, in_both_ref):
    local, width = back_ref.shape[0], out_ref.shape[1]
    for own_ref, target, cols in (
        (out_ref, out_both_ref, slice(0, width)),
        (in_ref, in_both_ref, slice(width, 2 * width)),
    ):
        target[info_ref[1]] = own_ref[:local, :]
        target[1 - info_ref[1]] = back_ref[:, cols].astype(F32)


def send_kernel(own_ref, more_ref, out_ref, total_ref, back_ref):
    local, width = back_ref.shape[0], own_ref.shape[1]
    for part in chunks(own_ref.shape[0], ROWS):
        total = own_ref[part, :] + more_ref[part, :].astype(F32)
        total_ref[part, :] = total
        if part.start >= local:
            target = slice(part.start - local, part.stop - local)
            back_ref[target, :width] = out_ref[part, :].astype(BF16)
            back_ref[target, width:] = total.astype(BF16)


def add_core_kernel(keep_ref, got_ref, s11a_ref, s11b_ref, s10_ref, s01_ref, s00_ref):
    half = s11a_ref.shape[0]
    for z in range(keep_ref.shape[1]):
        for index, target in ((0, s00_ref), (1, s01_ref), (2, s10_ref)):
            total = keep_ref[index, z].astype(F32) + got_ref[index, z].astype(F32)
            target[z] = total.astype(BF16)
        total = (keep_ref[3, z].astype(F32) + got_ref[3, z].astype(F32)).astype(BF16)
        if z < half:
            s11a_ref[z] = total
        else:
            s11b_ref[z - half] = total


def beside(target_ref, z, values, rows, width):
    for index in range(values.shape[0] // rows):
        target_ref[z, :, index * width : (index + 1) * width] = values[index * rows : (index + 1) * rows]


def add_half_kernel(a10_ref, ax_ref, a01_ref, ay_ref, b10_ref, bx_ref, b01_ref, by_ref, o10_ref, o01_ref):
    half = ax_ref.shape[0]
    rows, width = b10_ref.shape[1], a10_ref.shape[2]
    at = a10_ref.shape[1] // rows * width
    for z in range(2 * half):
        for tall_ref, tall_got_ref, low_ref, got_ref, out_ref, first in (
            (a10_ref, ax_ref, b10_ref, bx_ref, o10_ref, 0),
            (a01_ref, ay_ref, b01_ref, by_ref, o01_ref, half),
        ):
            if first <= z < first + half:
                tall = (tall_ref[z].astype(F32) + tall_got_ref[z - first].astype(F32)).astype(BF16)
                low = (low_ref[z].astype(F32) + got_ref[z - first].astype(F32)).astype(BF16)
            else:
                tall, low = tall_ref[z], low_ref[z]
            beside(out_ref, z, tall, rows, width)
            out_ref[z, :, at:] = low


def add_both_kernel(info_ref, a_ref, b_ref, got_x_ref, got_y_ref, own_ref, near_ref, next_ref, far_ref):
    line = info_ref[0] // 8
    rows, width = b_ref.shape[1], a_ref.shape[2]
    count = a_ref.shape[1] // rows
    for z, out_ref in enumerate((own_ref, near_ref, next_ref, far_ref)):
        at = line ^ z
        for index in range(count + 1):
            if index < count:
                cols = slice(index * width, (index + 1) * width)
                own = a_ref[at, index * rows : (index + 1) * rows]
            else:
                cols = slice(count * width, got_x_ref.shape[2])
                own = b_ref[at]
            total = own.astype(F32) + got_x_ref[at, :, cols].astype(F32) + got_y_ref[at, :, cols].astype(F32)
            out_ref[:, cols] = total.astype(BF16)


def add_pair_kernel(own_ref, got_ref, next_ref, sum_ref):
    cols = own_ref.shape[1]
    sum_ref[:, :cols] = (own_ref[...].astype(F32) + got_ref[...].astype(F32)).astype(BF16)
    sum_ref[:, cols:] = next_ref[...]


def add_core_all_kernel(keep_ref, got_ref, *outs):
    for z in range(keep_ref.shape[1]):
        for index, target in enumerate(outs):
            target[z] = (keep_ref[index, z].astype(F32) + got_ref[index, z].astype(F32)).astype(BF16)


def add_four_kernel(info_ref, a_ref, b_ref, c_ref, d_ref, own_ref, near_ref, next_ref, far_ref):
    line = info_ref[0] // 8
    for z, out_ref in enumerate((own_ref, near_ref, next_ref, far_ref)):
        at = line ^ z
        total = a_ref[at].astype(F32) + b_ref[at].astype(F32) + c_ref[at].astype(F32)
        out_ref[...] = (total + d_ref[at].astype(F32)).astype(BF16)


def end_both_kernel(own_ref, got_ref, far_ref, tall_ref, win_ref, wo_ref, *rest):
    vectors, flip_ref = rest[:-1], rest[-1]
    rows, width = own_ref.shape[0], tall_ref.shape[1]

    def total(cols):
        return own_ref[:, cols].astype(F32) + got_ref[:, cols].astype(F32) + far_ref[:, cols].astype(F32)

    at = tall_ref.shape[0] // rows * width
    for index in range(tall_ref.shape[0] // rows):
        tall_ref[index * rows : (index + 1) * rows, :] = total(slice(index * width, (index + 1) * width))
    for out in (win_ref, wo_ref):
        out[...] = total(slice(at, at + out.shape[1]))
        at = at + out.shape[1]
    flip_ref[...] = jnp.zeros_like(flip_ref)
    flip_ref[:rows, :] = total(slice(at, at + LANES))
    turned = flip_ref[...].T
    for index, vector in enumerate(vectors):
        vector[...] = turned[index : index + 1, :rows]


def end_kernel(a_ref, b_ref, c_ref, far_ref, *outs):
    at = 0
    first = far_ref.shape[1] - a_ref.shape[1]
    for out in outs:
        cols = slice(at, at + out.shape[1])
        total = a_ref[:, cols].astype(F32) + b_ref[:, cols].astype(F32)
        total = total + c_ref[:, cols].astype(F32)
        out[...] = total + far_ref[:, first + at : first + at + out.shape[1]].astype(F32)
        at = at + out.shape[1]


def vm():
    return pl.BlockSpec(memory_space=pltpu.VMEM)


def run(kernel, ins, outs, scratch=(), scalars=(), loose=(), pinned=(), far=(), sems=0, micros=0.05):
    specs = [vm() for _ in ins]
    for index in scalars:
        specs[index] = pl.BlockSpec(memory_space=pltpu.SMEM)
    ins = list(ins)
    for index in loose:
        specs[index] = pl.BlockSpec(memory_space=pl.ANY)
    for index in pinned:
        specs[index] = pl.BlockSpec(memory_space=pltpu.HBM)
        ins[index] = pltpu.with_memory_space_constraint(ins[index], pltpu.HBM)
    size = sum(v.size * v.dtype.itemsize for v in ins) + sum(
        functools.reduce(lambda a, b: a * b, s, 1) * jnp.dtype(t).itemsize for s, t in outs
    )
    buffers = [pltpu.VMEM(s, t) for s, t in scratch]
    need = sum(functools.reduce(lambda a, b: a * b, s, 1) * jnp.dtype(t).itemsize for s, t in scratch)
    if sems:
        buffers.append(pltpu.SemaphoreType.DMA((sems,)))
    return pl.pallas_call(
        kernel,
        out_shape=[jax.ShapeDtypeStruct(s, t) for s, t in outs],
        in_specs=specs,
        out_specs=[pl.BlockSpec(memory_space=pl.ANY) if index in far else vm() for index in range(len(outs))],
        scratch_shapes=buffers,
        compiler_params=pltpu.CompilerParams(vmem_limit_bytes=max(need + 8 * MIB, SCOPED)),
        cost_estimate=pl.CostEstimate(
            flops=int(micros * MICRO), bytes_accessed=size, transcendentals=0
        ),
    )(*ins)


AXES = ("dp", "head")


def after(value, *others):
    return lax.optimization_barrier((value, *others))[0]


class Links:
    def __init__(self, model_rows):
        self.heads = lax.axis_size("head")
        self.pods = lax.axis_size("dp")
        self.count = self.heads * self.pods
        self.fast = self.heads == 4 and self.pods == 8 and model_rows == 16
        self.head = lax.axis_index("head")
        self.me = lax.axis_index("dp") * self.heads + self.head

    def flip(self, value, bit):
        return lax.ppermute(value, AXES, [(i, i ^ bit) for i in range(self.count)])

    def flip_head(self, value, bit):
        return lax.ppermute(value, "head", [(i, i ^ bit) for i in range(self.heads)])

    def along_z(self, block):
        return [block, *(self.flip(block, 8 * k) for k in (1, 2, 3))]

    def stack(self, parts):
        (out,) = run(
            stack_kernel, parts, [((4, *parts[0].shape), BF16)], loose=range(4), far=(0,), sems=4
        )
        return out

    def core_sums(self, keep, got):
        block = keep.shape[2:]
        whole, half = ((4, *block), BF16), ((2, *block), BF16)
        return run(add_core_kernel, [keep, got], [half, half, whole, whole, whole])

    def line_parts(self, kernel, parts, shape):
        return run(kernel, [self.info, *parts], [(shape, BF16)] * 4, scalars=(0,))

    def line_first(self, kernel, parts, shape):
        own, near, following, far = self.line_parts(kernel, parts, shape)
        return own, far, self.flip(near, 8), self.flip(following, 8)

    def line_last(self, far, got, got_far, beside):
        shape = (far.shape[0], far.shape[1] + beside.shape[1])
        (far,) = run(add_pair_kernel, [after(far, got), got_far, beside], [(shape, BF16)])
        return self.flip(far, 24)

    def spread(self, own, group):
        held, bit = own[None], 1
        while bit < group:
            got = self.flip_head(held, bit)
            held = got if bit == 1 and group == 2 else jnp.concatenate([held, got], axis=0)
            bit = bit * 2
        if group > 2:
            held = held[1:]
        return held.reshape(-1, own.shape[1])

    def collapse(self, parts, group, rows):
        if group == 2:
            return self.flip_head(parts, 1)
        held = parts.reshape(group - 1, rows, -1)
        held = jnp.concatenate([jnp.zeros_like(held[:1]), held], axis=0).astype(F32)
        bit = group // 2
        while bit >= 1:
            held = held[:bit] + self.flip_head(held[bit : 2 * bit], bit)
            bit = bit // 2
        return held[0]


def body(
    tokens, cotangent, lengths, halting, w_query, w_key, w_value, w_out, w_in, w_hidden,
    w_halt, gain_attn, shift_attn, gain_ffn, shift_ffn,
):
    micro, local, width = tokens.shape
    links = Links(w_query.shape[0])
    fast, heads = links.fast, links.heads
    group = heads // micro
    rows, length = micro * local, local * heads
    mine = links.head // group
    wide_ff = w_in.shape[1]
    fine = width // links.count
    matrices = (w_query, w_key, w_value, w_out, w_in, w_hidden)
    vectors = (w_halt, gain_attn, shift_attn, gain_ffn, shift_ffn)
    place_array = jnp.stack([links.me, mine, links.head % group, jnp.int32(group)]).astype(jnp.int32)
    links.info = place_array

    pairs = width // LANES
    row_f, row_b = ((rows, width), F32), ((rows, width), BF16)
    stat = ((rows, LANES), F32)
    others = length - rows
    long_b = ((length, width), BF16)
    q2_t = ((pairs, 2 * rows, LANES), BF16)
    p_t = ((pairs, 2 * rows, length), BF16)
    o_t = ((2 * rows, LANES), F32)
    bias_t = ((rows, length), F32)
    inner_t = ((rows, BLOCK), F32)
    ff_b = ((rows, wide_ff), BF16)
    sums_t = ((VECS, 8, width), F32)
    ds_t = ((2 * rows, length), BF16)
    dqkv_t = ((rows, 3 * width), BF16)
    doth_t = ((others, 2 * width), BF16)
    vg_t = ((8, width), F32)
    segq_t, segk_t = ((rows, LANES), jnp.int32), ((8, length), jnp.int32)

    sort_in = [place_array, tokens, cotangent, halting]
    sort_out = [((local, 2 * width + LANES), BF16)] * 2
    sort_tmp = [((LANES, local), F32), (halting.shape, jnp.int32)]
    if fast:
        send_tok, own_tok, block_a, block_b = run(
            pack_kernel,
            [*sort_in, *matrices, *(vector[None] for vector in vectors)],
            [*sort_out, ((4 * pairs + 1, fine, LANES), BF16), ((8, fine, BLOCK), BF16)],
            [*sort_tmp, ((LANES, LANES), F32), ((VECS, 1, fine), BF16)],
            scalars=(0,),
            pinned=range(1, 15),
            sems=18 + 4 * pairs,
        )
        got_tok = links.flip_head(send_tok, group)
        line_a = links.along_z(block_a)
        own_a = after(links.stack(line_a), got_tok)
        by_x, by_y = links.flip(own_a, 2), links.flip(own_a, 4)
        line_b = links.along_z(after(block_b, line_a[1]))
        plane_a = [own_a, by_x, by_y, links.flip(after(by_y, line_b[3]), 2)]
    else:
        send_tok, own_tok = run(
            sort_kernel, sort_in, sort_out, sort_tmp, scalars=(0,), pinned=(1, 2, 3), sems=5
        )
        full = [lax.all_gather(part, AXES, axis=0, tiled=True) for part in matrices]
        full_v = [lax.all_gather(part, AXES, axis=0, tiled=True) for part in vectors]
        full_a = jnp.stack(full[:4])
        full_in = jnp.transpose(full[4].reshape(width, wide_ff // BLOCK, BLOCK), (1, 0, 2))
        full_hid = full[5]
        vec = jnp.pad(jnp.stack(full_v), ((0, 8 - VECS), (0, 0))).astype(F32)

        got_tok = links.flip_head(send_tok, group)
    tok, x0, rown0, sig1, segq, segk = run(
        embed_kernel,
        [place_array, lengths[:, 0], own_tok, got_tok],
        [((rows, 2 * width + LANES), BF16), row_f, row_b, row_f, segq_t, segk_t],
        scalars=(0, 1),
    )
    roth0 = links.spread(rown0, group)
    if fast:
        own_b = after(links.stack(line_b), by_x, by_y)
        near = [own_b, links.flip(own_b, 2), links.flip(own_b, 4)]
        near = near + [links.flip(piece, 1) for piece in near]
        halves = run(
            halves_kernel,
            [after(near[2], roth0), near[1]],
            [((2, 8, fine, BLOCK), BF16)] * 2,
            loose=(0, 1),
            far=(0, 1),
            sems=2,
        )
        far_b = [links.flip(halves[0], 2), links.flip(halves[1], 4)]
        plane_a[3] = after(plane_a[3], halves[0])
        plane_a = plane_a + [links.flip(piece, 1) for piece in plane_a]

    attend_in = [rown0, roth0, segq, segk]
    attend_out = [q2_t, long_b, long_b, p_t, row_b]
    if fast:
        full_a, vec, q2, k, v, p, ctx = run(
            functools.partial(attend_kernel, True),
            [*attend_in, links.info, *plane_a],
            [((5, 4, 8, fine, BLOCK), BF16), vg_t, *attend_out],
            [row_b, bias_t, o_t],
            scalars=(4,),
            micros=8,
        )
        full_a = full_a.reshape(5, width, BLOCK)
    else:
        q2, k, v, p, ctx = run(
            functools.partial(attend_kernel, False),
            [*attend_in, full_a],
            attend_out,
            [row_b, bias_t, o_t],
            micros=8,
        )
    n1, r1, nlow = run(norm_kernel, [x0, ctx, vec, full_a], [row_f, stat, row_b], [row_f], micros=1)
    ffn_out = [ff_b, ff_b, row_f, stat, stat, row_f, row_f, row_f, row_b]
    ffn_in = [n1, nlow, tok, sig1, vec]
    if fast:
        far_b = [after(piece, ctx) for piece in far_b]
        far_b = far_b + [links.flip(piece, 1) for piece in far_b]
        full_in, full_hid, *got = run(
            functools.partial(ffn_kernel, True),
            [*ffn_in, links.info, *near, *far_b],
            [((4, 4, 8, fine, BLOCK), BF16), ((4, 8, 4, fine, BLOCK), BF16), *ffn_out],
            [inner_t, row_f],
            scalars=(5,),
            micros=5.5,
        )
        full_in = full_in.reshape(4, width, BLOCK)
        full_hid = full_hid.reshape(wide_ff, width)
    else:
        got = run(
            functools.partial(ffn_kernel, False),
            [*ffn_in, full_in, full_hid],
            ffn_out,
            [inner_t, row_f],
            micros=5.5,
        )
    hid, dg, n2, r2, rate, state, pooled, x1, rown1 = got
    roth1 = links.spread(rown1, group)
    out, gs, goth, nlow1, hid1, b11, b21, ctx1, b01, dqkv1, doth1, vg1 = run(
        turn_kernel,
        [x1, rown1, roth1, full_a, full_in, full_hid, vec, segq, segk, state, pooled, tok],
        [row_f, row_f, ((others, width), BF16), row_b, ff_b, ff_b, row_b, row_b, row_b, dqkv_t, doth_t, vg_t],
        [
            row_b, q2_t, long_b, long_b, p_t, bias_t, o_t, row_f, row_f, stat, inner_t, ff_b,
            row_f, stat, stat, row_f, row_f, sums_t, row_b, q2_t, ds_t,
        ],
        micros=15.7,
    )
    more = links.collapse(goth, group, rows)

    b_cols = wide_ff + width + LANES
    def parts_of(shape, whole):
        return [((4, 4, *shape), BF16)] * 2 if fast else [(whole, F32)]

    hid_out = parts_of((4 * fine, width), (wide_ff, width))
    in_out = parts_of((fine, b_cols), (width, b_cols))
    attend_outs = parts_of((fine, 3 * width), (width, 3 * width))
    whole_shape = (4, 8, fine, BLOCK) if fast else (16, LANES)
    tall_shape = (8, 4 * fine, width) if fast else (16, LANES)
    b2, gsec, base, sums, *hid_parts = run(
        functools.partial(hidden_back_kernel, fast),
        [links.info, gs, more, tok, vec, n2, r2, rate, hid, hid1, b21],
        [row_b, row_f, row_f, sums_t, *hid_out],
        [(tall_shape, BF16)],
        scalars=(0,),
        micros=2,
    )
    b1, b0, base, gctx, sums = run(
        feed_back_kernel,
        [b2, gsec, base, sums, vec, full_in, full_hid, full_a, n1, r1, dg],
        [ff_b, row_b, row_f, row_b, sums_t],
        [inner_t, row_f],
        micros=2.2,
    )
    if fast:
        c_sums = links.core_sums(hid_parts[0], links.flip(hid_parts[1], 1))
        b1 = after(b1, c_sums[0])
    in_parts = run(
        functools.partial(weights_back_kernel, fast),
        [links.info, b1, b0, sums, nlow, ctx, nlow1, b11, ctx1, b01, vg1],
        in_out,
        [(whole_shape, BF16), ((LANES, width), F32)],
        scalars=(0,),
        micros=2,
    )
    if fast:
        b_sums = links.core_sums(in_parts[0], links.flip(in_parts[1], 1))
        gctx = after(gctx, b_sums[0])
    dqkv0, doth0 = run(
        heads_back_kernel,
        [gctx, q2, k, v, p, ctx],
        [dqkv_t, doth_t],
        [q2_t, ds_t, o_t],
        micros=3,
    )
    g0, goth0, *attend_parts = run(
        functools.partial(project_back_kernel, fast),
        [links.info, base, full_a, rown0, roth0, rown1, roth1, dqkv1, doth1, dqkv0, doth0],
        [row_f, ((others, width), BF16), *attend_outs],
        [(whole_shape, BF16)],
        scalars=(0,),
    )
    if fast:
        c11a, c11b, c10, c01, c00 = c_sums
        b11a, b11b, b10, b01, b00 = b_sums
        halves = [
            after(c10, g0), links.flip(c11a, 2), c01, links.flip(c11b, 4),
            b10, links.flip(b11a, 2), b01, links.flip(b11b, 4),
        ]
        both_t = ((4, fine, 4 * width + b_cols), BF16)
        both10, both01 = run(add_half_kernel, halves, [both_t] * 2)
        goth0, send_a = after(goth0, both01), after(attend_parts[1], both01)
    inputs, back = run(
        send_kernel,
        [g0, links.collapse(goth0, group, rows), out],
        [row_f, ((local, 2 * width), BF16)],
    )
    if fast:
        keep, got = after(attend_parts[0], back), links.flip(send_a, 1)
        a00, a01, a10, a11 = run(add_core_all_kernel, [keep, got], [(keep.shape[1:], BF16)] * 4)
        by_plane = [a00, links.flip(a11, 6), links.flip(a01, 2), links.flip(a10, 4)]
        both = links.line_first(
            add_both_kernel, [after(c00, a00), b00, links.flip(both01, 2), links.flip(both10, 4)], both_t[0][1:]
        )
        first_sums = both[0]
        by_plane[0] = after(by_plane[0], both[0])
        attend_sums = links.line_parts(add_four_kernel, by_plane, a00.shape[1:])
        far = links.line_last(after(both[1], attend_sums[0]), *both[2:], attend_sums[3])
        both = [both[0], both[2], far]
        attend_sums = [attend_sums[0], *(links.flip(attend_sums[k], 8 * k) for k in (1, 2)), far]
        back = after(back, first_sums)
        output, input_grad = run(
            return_kernel,
            [links.info, out, inputs, links.flip_head(back, group)],
            [((micro, local, width), F32)] * 2,
            scalars=(0,),
        )
        g_hidden, g_in, g_out, *g_vectors = run(
            end_both_kernel,
            [after(both[0], output), *both[1:]],
            [((4 * fine, width), F32), ((fine, wide_ff), F32), ((fine, width), F32)] + [((1, fine), F32)] * VECS,
            [((LANES, LANES), F32)],
        )
        g_query, g_key, g_value = run(
            end_kernel,
            [after(attend_sums[0], output, g_hidden), *attend_sums[1:]],
            [((fine, width), F32)] * 3,
        )
        g_vectors = [vector.reshape(fine) for vector in g_vectors]
    else:
        sums = [
            *(attend_parts[0][:, index * width : (index + 1) * width] for index in range(3)),
            in_parts[0][:, wide_ff : wide_ff + width], in_parts[0][:, :wide_ff], hid_parts[0],
            in_parts[0][:, wide_ff + width :],
        ]
        sums = [lax.psum_scatter(part, AXES, scatter_dimension=0, tiled=True) for part in sums]
        g_query, g_key, g_value, g_out, g_in, g_hidden, g_vec = sums
        g_vectors = [g_vec[:, index] for index in range(VECS)]
        output, input_grad = run(
            return_kernel,
            [links.info, out, inputs, links.flip_head(back, group)],
            [((micro, local, width), F32)] * 2,
            scalars=(0,),
        )
    return (output, input_grad, g_query, g_key, g_value, g_out, g_in, g_hidden, *g_vectors)


def solution(mesh):
    whole = P(("dp", "head"))
    matrix = P(("dp", "head"), None)
    rows = P(None, ("dp", "head"), None)
    return jax.shard_map(
        body,
        mesh=mesh,
        in_specs=(rows, rows, P(None, "dp", None), P(None, None, ("dp", "head")))
        + (matrix,) * 6
        + (whole,) * 5,
        out_specs=(rows, rows) + (matrix,) * 6 + (whole,) * 5,
        check_vma=False,
    )
```

```python
import functools

import jax
import jax.numpy as jnp
from jax import lax
from jax.experimental import pallas as pl
from jax.experimental.pallas import tpu as pltpu
from jax.sharding import PartitionSpec as P

HD = 64
EPSILON = 1e-06
F32 = jnp.float32
BF16 = jnp.bfloat16
LANES = 128
ROWS = 32
ATT_ROWS = 256
BLOCK = 512
VECS = 5
MIB = 1024 * 1024
SCOPED = 20 * MIB
MICRO = 1.15e9
GELU_A = 0.7978845608028654
GELU_B = 0.044715


def dot(a, b, ca=1, cb=0):
    return lax.dot_general(a, b, (((ca,), (cb,)), ((), ())), preferred_element_type=F32)


def chunks(total, size):
    size = min(size, total)
    return [slice(i, i + size) for i in range(0, total, size)]


def wide(column):
    return jnp.broadcast_to(column, (column.shape[0], LANES))


def mean(values):
    return jnp.sum(values, axis=-1, keepdims=True) * (1.0 / values.shape[-1])


def fold(values):
    return jnp.sum(values.reshape(values.shape[0] // 8, 8, values.shape[1]), axis=0)


class Flat:
    def __init__(self, ref):
        self.ref = ref

    def __getitem__(self, index):
        if index is Ellipsis:
            index = (slice(None), slice(None))
        value = self.ref[..., index[1]]
        return value.reshape(-1, value.shape[-1])[index[0]]


def matrix(ref, index):
    value = ref[index]
    return value.reshape(-1, value.shape[-1])


def head_mask(rows):
    lane = lax.broadcasted_iota(jnp.int32, (rows, LANES), 1)
    return lane < HD


def normalize(values):
    center = values - mean(values)
    inverse = lax.rsqrt(mean(center * center) + EPSILON)
    return center * inverse, inverse


def normalize_back(unit, inverse, grad):
    return inverse * (grad - mean(grad) - unit * mean(grad * unit))


def split_heads(values_ref, stacked_ref):
    rows = values_ref.shape[0]
    for part in chunks(rows, ATT_ROWS):
        first = head_mask(part.stop - part.start)
        for pair in range(stacked_ref.shape[0]):
            block = values_ref[part, pair * LANES : (pair + 1) * LANES].astype(F32)
            stacked_ref[pair, part, :] = jnp.where(first, block, 0.0).astype(BF16)
            stacked_ref[pair, rows + part.start : rows + part.stop, :] = jnp.where(
                first, 0.0, block
            ).astype(BF16)


def project(rown_ref, roth_ref, wa_ref, q_ref, q2_ref, k_ref, v_ref):
    rows, width = rown_ref.shape
    q_ref[...] = (
        dot(rown_ref[...], matrix(wa_ref, 0)).astype(BF16).astype(F32) * HD**-0.5
    ).astype(BF16)
    split_heads(q_ref, q2_ref)
    for at, source in ((0, rown_ref), (rows, roth_ref)):
        span = slice(at, at + source.shape[0])
        k_ref[span, :] = dot(source[...], matrix(wa_ref, 1)).astype(BF16)
        v_ref[span, :] = dot(source[...], matrix(wa_ref, 2)).astype(BF16)


def set_bias(segq_ref, segk_ref, bias_ref):
    for part in chunks(bias_ref.shape[0], ROWS):
        bias_ref[part, :] = jnp.where(segq_ref[part, 0:1] == segk_ref[0:1, :], 0.0, -1e30)


def attend(q2_ref, k_ref, v_ref, bias_ref, p_ref, ctx_ref, o_ref):
    rows, length = bias_ref.shape
    for pair in range(q2_ref.shape[0]):
        cols = slice(pair * LANES, (pair + 1) * LANES)
        for part in chunks(2 * rows, 2 * rows):
            scores = dot(q2_ref[pair, part, :], k_ref[:, cols], 1, 1)
            scores = (scores.reshape(2, rows, length) + bias_ref[...][None]).reshape(2 * rows, length)
            weights = jnp.exp(scores - jnp.max(scores, axis=-1, keepdims=True))
            inverse = 1.0 / jnp.sum(weights, axis=-1, keepdims=True)
            low = (weights * inverse).astype(BF16)
            p_ref[pair, part, :] = low
            o_ref[part, :] = dot(low, v_ref[:, cols])
        for part in chunks(rows, ATT_ROWS):
            first = head_mask(part.stop - part.start)
            second = o_ref[rows + part.start : rows + part.stop, :]
            ctx_ref[part, cols] = jnp.where(first, o_ref[part, :], second).astype(BF16)


def first_norm(x_ref, ctx_ref, wa_ref, vec_ref, acc_ref, n1_ref, r1_ref, nlow_ref):
    acc_ref[...] = dot(ctx_ref[...], matrix(wa_ref, 3))
    for part in chunks(x_ref.shape[0], ROWS):
        unit, inverse = normalize(x_ref[part, :] + acc_ref[part, :])
        n1_ref[part, :] = unit
        r1_ref[part, :] = wide(inverse)
        nlow_ref[part, :] = (unit * vec_ref[1:2, :] + vec_ref[2:3, :]).astype(BF16)


def feed_forward(nlow_ref, win_ref, whid_ref, inner_ref, hid_ref, dg_ref, acc_ref):
    rows = nlow_ref.shape[0]
    for cols in chunks(hid_ref.shape[1], BLOCK):
        inner_ref[...] = dot(nlow_ref[...], matrix(win_ref, cols.start // BLOCK))
        for part in chunks(rows, ROWS):
            x = inner_ref[part, :]
            square = x * x
            t = jnp.tanh(x * (GELU_A + GELU_A * GELU_B * square))
            half = 0.5 + 0.5 * t
            hid_ref[part, cols] = (x * half).astype(BF16)
            slope = 0.5 * x * (1.0 - t * t) * (GELU_A + 3.0 * GELU_A * GELU_B * square)
            dg_ref[part, cols] = (half + slope).astype(BF16)
    acc_ref[...] = dot(hid_ref[...], whid_ref[...])


def second_norm(part, vec_ref, n1_ref, acc_ref):
    normed = n1_ref[part, :] * vec_ref[1:2, :] + vec_ref[2:3, :]
    unit, inverse = normalize(normed + acc_ref[part, :])
    updated = unit * vec_ref[3:4, :] + vec_ref[4:5, :]
    rate = jax.nn.sigmoid(jnp.sum(updated * vec_ref[0:1, :], axis=-1, keepdims=True))
    return unit, inverse, updated, rate


def tail_back(
    part, step, gs, gp, halt_ref, vec_ref, n2_ref, r2_ref, rate_ref, b2_ref, gsec_ref, base_ref, sums_ref
):
    width = n2_ref.shape[1]
    keep = halt_ref[part, 2 * width + step : 2 * width + step + 1].astype(F32)
    unit = n2_ref[part, :]
    updated = unit * vec_ref[3:4, :] + vec_ref[4:5, :]
    rate = rate_ref[part, 0:1]
    logit = keep * jnp.sum(gp * updated, axis=-1, keepdims=True) * rate * (1.0 - rate)
    grad = keep * gs + (keep * rate) * gp + logit * vec_ref[0:1, :]
    base_ref[part, :] = gs - keep * gs
    sums_ref[0] += fold(logit * updated)
    sums_ref[3] += fold(grad * unit)
    sums_ref[4] += fold(grad)
    back = normalize_back(unit, r2_ref[part, 0:1], grad * vec_ref[3:4, :])
    gsec_ref[part, :] = back
    b2_ref[part, :] = back.astype(BF16)


def feed_back(b2_ref, dg_ref, win_ref, whid_ref, inner_ref, b1_ref, acc_ref):
    rows = b2_ref.shape[0]
    for cols in chunks(dg_ref.shape[1], BLOCK):
        inner_ref[...] = dot(b2_ref[...], whid_ref[cols, :], 1, 1)
        for part in chunks(rows, ROWS):
            b1_ref[part, cols] = (inner_ref[part, :] * dg_ref[part, cols].astype(F32)).astype(BF16)
    total = None
    for cols in chunks(dg_ref.shape[1], BLOCK):
        value = dot(b1_ref[:, cols], matrix(win_ref, cols.start // BLOCK), 1, 1)
        total = value if total is None else total + value
    acc_ref[...] = total


def middle_back(gsec_ref, acc_ref, vec_ref, n1_ref, r1_ref, b0_ref, base_ref, sums_ref):
    for part in chunks(gsec_ref.shape[0], ROWS):
        grad = gsec_ref[part, :] + acc_ref[part, :]
        unit = n1_ref[part, :]
        sums_ref[1] += fold(grad * unit)
        sums_ref[2] += fold(grad)
        back = normalize_back(unit, r1_ref[part, 0:1], grad * vec_ref[1:2, :])
        base_ref[part, :] += back
        b0_ref[part, :] = back.astype(BF16)


def attend_back(
    pairs, g2_ref, q2_ref, k_ref, v_ref, p_ref, ctx_ref, ds_ref, dq2_ref, dqkv_ref, doth_ref
):
    rows, width = ctx_ref.shape
    for pair in pairs:
        cols = slice(pair * LANES, (pair + 1) * LANES)
        for part in chunks(2 * rows, 2 * rows):
            grad = g2_ref[pair, part, :]
            both = jnp.concatenate([ctx_ref[:, cols]] * 2, axis=0)
            delta = jnp.sum(grad.astype(F32) * both.astype(F32), axis=-1, keepdims=True)
            back = dot(grad, v_ref[:, cols], 1, 1)
            low = (p_ref[pair, part, :].astype(F32) * (back - delta)).astype(BF16)
            ds_ref[part, :] = low
            dq2_ref[part, :] = dot(low, k_ref[:, cols])
        for part in chunks(rows, ATT_ROWS):
            first = head_mask(part.stop - part.start)
            second = dq2_ref[rows + part.start : rows + part.stop, :]
            dqkv_ref[part, cols] = (
                jnp.where(first, dq2_ref[part, :], second) * HD**-0.5
            ).astype(BF16)
        for index, (left, right) in enumerate(
            ((ds_ref[...], q2_ref[pair]), (p_ref[pair], g2_ref[pair]))
        ):
            both = dot(right, left, 0, 0).T.astype(BF16)
            at = index * width + pair * LANES
            dqkv_ref[:, width + at : width + at + LANES] = both[:rows]
            doth_ref[:, at : at + LANES] = both[rows:]


def inputs_back(dqkv_ref, doth_ref, wa_ref, base_ref, gs_ref, goth_ref):
    width = base_ref.shape[1]
    parts = [slice(index * width, (index + 1) * width) for index in range(3)]
    total = base_ref[...]
    for index, cols in enumerate(parts):
        total = total + dot(dqkv_ref[:, cols], matrix(wa_ref, index), 1, 1)
    gs_ref[...] = total
    total = dot(doth_ref[:, parts[0]], matrix(wa_ref, 1), 1, 1)
    goth_ref[...] = (total + dot(doth_ref[:, parts[1]], matrix(wa_ref, 2), 1, 1)).astype(BF16)


def fetch(pieces, cores, bits, start, store, me_ref):
    line, place_in = me_ref[0] // 8, me_ref[0] % 8
    for piece, core, bit in zip(pieces, cores, bits):
        for z in range(piece.shape[0]):
            store(piece, z, line ^ (start + z), place_in ^ (bit | core))


def embed_kernel(place_ref, sizes_ref, tok_ref, got_ref, own_ref, x_ref, rown_ref, sig_ref, segq_ref, segk_ref):
    mine, place_in, group = place_ref[1], place_ref[2], place_ref[3]
    local = tok_ref.shape[0]
    half = x_ref.shape[1] // 2
    ends, starts, total = [], [], 0
    for index in range(sizes_ref.shape[1]):
        starts.append(total)
        total = total + sizes_ref[mine, index]
        ends.append(total)
    ones = jnp.exp(
        lax.broadcasted_iota(jnp.int32, (8, half), 1).astype(F32)
        * (-jnp.log(jnp.full((8, half), 10000.0, F32)) / max(half - 1, 1))
    )
    rates = ones[0:1, :]
    first_sin, first_cos = jnp.sin(rates), jnp.cos(rates)
    for part in chunks(x_ref.shape[0], ROWS):
        size = part.stop - part.start
        block = mine * group + place_in
        block = block if part.start < local else block ^ group
        at = block * local + part.start % local
        token = at + lax.broadcasted_iota(jnp.int32, (size, LANES), 0)
        segment = jnp.zeros((size, LANES), jnp.int32)
        begin = jnp.zeros((size, LANES), jnp.int32)
        for start, end in zip(starts, ends):
            segment = segment + jnp.where(token >= end, 1, 0)
            begin = jnp.maximum(begin, jnp.where(token >= start, start, 0))
        segq_ref[part, :] = segment
        angles = (token - begin).astype(F32)[:, 0:1] * rates
        if part.start < local:
            low = tok_ref[part, :]
        else:
            low = got_ref[part.start - local : part.stop - local, :]
        own_ref[part, :] = low
        for cols, moving, still, step in (
            (slice(0, half), jnp.sin(angles), 0.0, first_sin),
            (slice(half, 2 * half), jnp.cos(angles), 1.0, first_cos),
        ):
            inputs = low[:, cols].astype(F32) + (moving + still)
            x_ref[part, cols] = inputs
            rown_ref[part, cols] = inputs.astype(BF16)
            sig_ref[part, cols] = moving + step
    blocks = segk_ref.shape[1] // local
    for index in range(blocks):
        peer = mine * group + (place_in ^ (index // 2))
        peer = peer if index % 2 == 0 else peer ^ group
        token = peer * local + lax.broadcasted_iota(jnp.int32, (8, local), 1)
        segment = jnp.zeros((8, local), jnp.int32)
        for end in ends:
            segment = segment + jnp.where(token >= end, 1, 0)
        segk_ref[:, index * local : (index + 1) * local] = segment


def pull(sources, sems):
    copies = [
        pltpu.make_async_copy(source, target, sems.at[index]) for index, (source, target) in enumerate(sources)
    ]
    for copy in copies:
        copy.start()
    return copies


def sort_rows(place_ref, tok_ref, cot_ref, halt_ref, refs, sems):
    mine = place_ref[1]
    width = tok_ref.shape[2]
    send_ref, own_ref, flip_ref, flags_ref = refs
    moves = [(halt_ref, flags_ref)]
    for micro, target in ((1 - mine, send_ref), (mine, own_ref)):
        moves.append((tok_ref.at[micro], target.at[:, :width]))
        moves.append((cot_ref.at[micro], target.at[:, width : 2 * width]))
    copies = pull(moves, sems)
    flip_ref[...] = jnp.zeros_like(flip_ref)
    for copy in copies:
        copy.wait()
    for target, micro in ((own_ref, mine), (send_ref, 1 - mine)):
        for step in range(halt_ref.shape[0]):
            flip_ref[step : step + 1, :] = flags_ref[step, pl.ds(micro, 1), :].astype(F32)
        target[:, 2 * width :] = flip_ref[...].T.astype(BF16)


def sort_kernel(place_ref, tok_ref, cot_ref, halt_ref, *refs):
    sort_rows(place_ref, tok_ref, cot_ref, halt_ref, refs[:4], refs[4])


def pack_kernel(place_ref, tok_ref, cot_ref, halt_ref, q_ref, k_ref, v_ref, o_ref, win_ref, whid_ref, *rest):
    vectors, rest = rest[:VECS], rest[VECS:]
    sorted_refs, (block_ref, tall_ref, flip_ref, flags_ref, turn_ref, low_ref, sems) = rest[:2], rest[2:]
    rows, width = q_ref.shape
    moves = [(vector, low_ref.at[index]) for index, vector in enumerate(vectors)]
    lanes = width // LANES
    for index, source in enumerate((q_ref, k_ref, v_ref, o_ref)):
        for part in range(lanes):
            cols = slice(part * LANES, (part + 1) * LANES)
            moves.append((source.at[:, cols], block_ref.at[index * lanes + part]))
    for index in range(4):
        moves.append((win_ref.at[:, index * BLOCK : (index + 1) * BLOCK], tall_ref.at[index]))
        moves.append((whid_ref.at[index * rows : (index + 1) * rows, :], tall_ref.at[4 + index]))
    count = len(moves)
    copies = pull(moves, sems.at[:count])
    sort_rows(place_ref, tok_ref, cot_ref, halt_ref, [*sorted_refs, flip_ref, flags_ref], sems.at[count:])
    turn_ref[...] = jnp.zeros_like(turn_ref)
    for copy in copies:
        copy.wait()
    for index in range(VECS):
        turn_ref[index : index + 1, :rows] = low_ref[index].astype(F32)
    block_ref[4 * lanes] = turn_ref[...].T[:rows, :].astype(BF16)


def attend_kernel(
    fast, rown_ref, roth_ref, segq_ref, segk_ref, *rest,
):
    if fast:
        me_ref, plane, rest = rest[0], rest[1:9], rest[9:]
        wa_ref, vec_ref, q2_ref, k_ref, v_ref, p_ref, ctx_ref, q_ref, bias_ref, o_ref = rest

        def store(piece, z, line, place):
            lanes = wa_ref.shape[4] // LANES
            for chunk in range(piece.shape[1]):
                cols = slice(chunk % lanes * LANES, (chunk % lanes + 1) * LANES)
                wa_ref[chunk // lanes, line, place, :, cols] = piece[z, chunk]

        fetch(plane, (0, 0, 0, 0, 1, 1, 1, 1), (0, 2, 4, 6) * 2, 0, store, me_ref)
        vec_ref[...] = matrix(wa_ref, 4)[:, :LANES].astype(F32).T[0:8, :]
    else:
        wa_ref, q2_ref, k_ref, v_ref, p_ref, ctx_ref, q_ref, bias_ref, o_ref = rest
    set_bias(segq_ref, segk_ref, bias_ref)
    project(rown_ref, roth_ref, wa_ref, q_ref, q2_ref, k_ref, v_ref)
    attend(q2_ref, k_ref, v_ref, bias_ref, p_ref, ctx_ref, o_ref)


def norm_kernel(x_ref, ctx_ref, vec_ref, wa_ref, n1_ref, r1_ref, nlow_ref, acc_ref):
    first_norm(x_ref, ctx_ref, wa_ref, vec_ref, acc_ref, n1_ref, r1_ref, nlow_ref)


def ffn_kernel(fast, n1_ref, nlow_ref, tok_ref, sig_ref, vec_ref, *rest):
    if fast:
        me_ref, near, far, rest = rest[0], rest[1:7], rest[7:11], rest[11:]
        (win_ref, full_ref), rest = rest[:2], rest[2:]
    else:
        (win_ref, whid_ref), rest = rest[:2], rest[2:]
    (
        hid_ref, dg_ref, n2_ref, r2_ref, rate_ref, state_ref, pooled_ref, next_ref, rown_ref,
        inner_ref, acc_ref,
    ) = rest
    if fast:

        def store(piece, z, line, place):
            for chunk in range(4):
                win_ref[chunk, line, place] = piece[z, chunk]
                full_ref[line, place, chunk] = piece[z, 4 + chunk]

        fetch(near, (0, 0, 0, 1, 1, 1), (0, 2, 4, 0, 2, 4), 0, store, me_ref)
        fetch((far[0], far[2]), (0, 1), (6, 6), 0, store, me_ref)
        fetch((far[1], far[3]), (0, 1), (6, 6), 2, store, me_ref)
        whid_ref = Flat(full_ref)
    width = n1_ref.shape[1]
    feed_forward(nlow_ref, win_ref, whid_ref, inner_ref, hid_ref, dg_ref, acc_ref)
    for part in chunks(tok_ref.shape[0], ROWS):
        unit, inverse, updated, rate = second_norm(part, vec_ref, n1_ref, acc_ref)
        keep = tok_ref[part, 2 * width : 2 * width + 1].astype(F32)
        n2_ref[part, :] = unit
        r2_ref[part, :] = wide(inverse)
        rate_ref[part, :] = wide(rate)
        pooled_ref[part, :] = (keep * rate) * updated
        state = tok_ref[part, :width].astype(F32)
        state = state + keep * (updated - state)
        state_ref[part, :] = state
        inputs = state + sig_ref[part, :]
        next_ref[part, :] = inputs
        rown_ref[part, :] = inputs.astype(BF16)


def turn_kernel(
    x_ref, rown_ref, roth_ref, wa_ref, win_ref, whid_ref, vec_ref, segq_ref, segk_ref,
    state_ref, pooled_ref, tok_ref,
    out_ref, gs_ref, goth_ref, nlow_ref, hid_ref, b1_ref, b2_ref, ctx_ref, b0_ref, dqkv_ref, doth_ref, vg_ref,
    q_ref, q2_ref, k_ref, v_ref, p_ref, bias_ref, o_ref, acc_ref, n1_ref, r1_ref, inner_ref, dg_ref,
    n2_ref, r2_ref, rate_ref, gsec_ref, base_ref, sums_ref, gctx_ref, g2_ref, ds_ref,
):
    width = x_ref.shape[1]
    sums_ref[...] = jnp.zeros_like(sums_ref)
    set_bias(segq_ref, segk_ref, bias_ref)
    project(rown_ref, roth_ref, wa_ref, q_ref, q2_ref, k_ref, v_ref)
    attend(q2_ref, k_ref, v_ref, bias_ref, p_ref, ctx_ref, o_ref)
    first_norm(x_ref, ctx_ref, wa_ref, vec_ref, acc_ref, n1_ref, r1_ref, nlow_ref)
    feed_forward(nlow_ref, win_ref, whid_ref, inner_ref, hid_ref, dg_ref, acc_ref)
    for part in chunks(x_ref.shape[0], ROWS):
        unit, inverse, updated, rate = second_norm(part, vec_ref, n1_ref, acc_ref)
        keep = tok_ref[part, 2 * width + 1 : 2 * width + 2].astype(F32)
        n2_ref[part, :] = unit
        r2_ref[part, :] = wide(inverse)
        rate_ref[part, :] = wide(rate)
        state = state_ref[part, :]
        state = state + keep * (updated - state)
        out_ref[part, :] = state + (pooled_ref[part, :] + (keep * rate) * updated)
        cot = tok_ref[part, width : 2 * width].astype(F32)
        tail_back(
            part, 1, cot, cot, tok_ref, vec_ref, n2_ref, r2_ref, rate_ref, b2_ref, gsec_ref, base_ref,
            sums_ref,
        )
    feed_back(b2_ref, dg_ref, win_ref, whid_ref, inner_ref, b1_ref, acc_ref)
    middle_back(gsec_ref, acc_ref, vec_ref, n1_ref, r1_ref, b0_ref, base_ref, sums_ref)
    gctx_ref[...] = dot(b0_ref[...], matrix(wa_ref, 3), 1, 1).astype(BF16)
    split_heads(gctx_ref, g2_ref)
    pairs = range(q2_ref.shape[0])
    attend_back(pairs, g2_ref, q2_ref, k_ref, v_ref, p_ref, ctx_ref, ds_ref, o_ref, dqkv_ref, doth_ref)
    inputs_back(dqkv_ref, doth_ref, wa_ref, base_ref, gs_ref, goth_ref)
    vg_ref[...] = jnp.zeros_like(vg_ref)
    for index in range(VECS):
        vg_ref[index : index + 1, :] = jnp.sum(sums_ref[index], axis=0, keepdims=True)


def place(fast, me_ref, value, scratch_ref, outs, at):
    cols = slice(at, at + value.shape[1])
    if not fast:
        outs[0][:, cols] = value
        return
    low = value.astype(BF16)
    scratch_ref[:, :, :, : value.shape[1]] = low.reshape(scratch_ref.shape[:3] + value.shape[1:])
    for relative in range(8):
        block = scratch_ref[:, relative ^ (me_ref[0] % 8), :, : value.shape[1]]
        outs[relative % 2][relative // 2, :, :, cols] = block


def hidden_back_kernel(
    fast, me_ref, gs_ref, more_ref, tok_ref, vec_ref,
    n2_ref, r2_ref, rate_ref, hid_ref, hid1_ref, b21_ref,
    b2_ref, gsec_ref, base_ref, sums_ref,
    *rest,
):
    outs, tall_ref = rest[:-1], rest[-1]
    sums_ref[...] = jnp.zeros_like(sums_ref)
    width = gs_ref.shape[1]
    for part in chunks(gs_ref.shape[0], ROWS):
        tail_back(
            part, 0, gs_ref[part, :] + more_ref[part, :].astype(F32),
            tok_ref[part, width : 2 * width].astype(F32), tok_ref, vec_ref,
            n2_ref, r2_ref, rate_ref, b2_ref, gsec_ref, base_ref, sums_ref,
        )
    hidden_rows = hid_ref.shape[1] // 4
    for z in range(4):
        span = slice(z * hidden_rows, (z + 1) * hidden_rows)
        value = dot(hid_ref[:, span], b2_ref[...], 0, 0) + dot(hid1_ref[:, span], b21_ref[...], 0, 0)
        if fast:
            tall_ref[...] = value.astype(BF16).reshape(tall_ref.shape)
            for relative in range(8):
                outs[relative % 2][relative // 2, z] = tall_ref[relative ^ (me_ref[0] % 8)]
        else:
            outs[0][span, :] = value


def feed_back_kernel(
    b2_ref, gsec_ref, base0_ref, sums0_ref, vec_ref, win_ref, whid_ref, wa_ref, n1_ref, r1_ref, dg_ref,
    b1_ref, b0_ref, base_ref, gctx_ref, sums_ref, inner_ref, acc_ref,
):
    sums_ref[...] = sums0_ref[...]
    base_ref[...] = base0_ref[...]
    feed_back(b2_ref, dg_ref, win_ref, whid_ref, inner_ref, b1_ref, acc_ref)
    middle_back(gsec_ref, acc_ref, vec_ref, n1_ref, r1_ref, b0_ref, base_ref, sums_ref)
    gctx_ref[...] = dot(b0_ref[...], matrix(wa_ref, 3), 1, 1).astype(BF16)


def weights_back_kernel(
    fast, me_ref, b1_ref, b0_ref, sums_ref, nlow_ref, ctx_ref, nlow1_ref, b11_ref, ctx1_ref, b01_ref, vg1_ref,
    *rest,
):
    outs, (whole_ref, flip_ref) = rest[:-2], rest[-2:]
    width = ctx_ref.shape[1]
    for cols in chunks(b1_ref.shape[1], BLOCK):
        value = dot(nlow_ref[...], b1_ref[:, cols], 0, 0) + dot(nlow1_ref[...], b11_ref[:, cols], 0, 0)
        place(fast, me_ref, value, whole_ref, outs, cols.start)
    value = dot(ctx_ref[...], b0_ref[...], 0, 0) + dot(ctx1_ref[...], b01_ref[...], 0, 0)
    at = b1_ref.shape[1]
    place(fast, me_ref, value, whole_ref, outs, at)
    flip_ref[...] = jnp.zeros_like(flip_ref)
    flip_ref[0:8, :] = vg1_ref[...]
    for index in range(VECS):
        flip_ref[index : index + 1, :] += jnp.sum(sums_ref[index], axis=0, keepdims=True)
    place(fast, me_ref, flip_ref[...].T, whole_ref, outs, at + width)


def heads_back_kernel(
    gctx_ref, q2_ref, k_ref, v_ref, p_ref, ctx_ref, dqkv_ref, doth_ref, g2_ref, ds_ref, dq2_ref
):
    split_heads(gctx_ref, g2_ref)
    pairs = range(q2_ref.shape[0])
    attend_back(pairs, g2_ref, q2_ref, k_ref, v_ref, p_ref, ctx_ref, ds_ref, dq2_ref, dqkv_ref, doth_ref)


def project_back_kernel(
    fast, me_ref, base_ref, wa_ref,
    rown_ref, roth_ref, rown1_ref, roth1_ref, dqkv1_ref, doth1_ref, dqkv_ref, doth_ref,
    gs_ref, goth_ref,
    *rest,
):
    outs, whole_ref = rest[:-1], rest[-1]
    width = base_ref.shape[1]
    for index in range(3):
        cols = slice(index * width, (index + 1) * width)
        value = dot(rown_ref[...], dqkv_ref[:, cols], 0, 0) + dot(
            rown1_ref[...], dqkv1_ref[:, cols], 0, 0
        )
        if index:
            other = slice((index - 1) * width, index * width)
            value = (
                value
                + dot(roth_ref[...], doth_ref[:, other], 0, 0)
                + dot(roth1_ref[...], doth1_ref[:, other], 0, 0)
            )
        place(fast, me_ref, value, whole_ref, outs, cols.start)
    inputs_back(dqkv_ref, doth_ref, wa_ref, base_ref, gs_ref, goth_ref)


def stack_kernel(*refs):
    *parts, out_ref, sems = refs
    for copy in pull([(part, out_ref.at[index]) for index, part in enumerate(parts)], sems):
        copy.wait()


def halves_kernel(by_y_ref, by_x_ref, low_ref, high_ref, sems):
    half = low_ref.shape[0]
    moves = [(by_y_ref.at[pl.ds(0, half)], low_ref), (by_x_ref.at[pl.ds(half, half)], high_ref)]
    for copy in pull(moves, sems):
        copy.wait()


def return_kernel(info_ref, out_ref, in_ref, back_ref, out_both_ref, in_both_ref):
    local, width = back_ref.shape[0], out_ref.shape[1]
    for own_ref, target, cols in (
        (out_ref, out_both_ref, slice(0, width)),
        (in_ref, in_both_ref, slice(width, 2 * width)),
    ):
        target[info_ref[1]] = own_ref[:local, :]
        target[1 - info_ref[1]] = back_ref[:, cols].astype(F32)


def send_kernel(own_ref, more_ref, out_ref, total_ref, back_ref):
    local, width = back_ref.shape[0], own_ref.shape[1]
    for part in chunks(own_ref.shape[0], ROWS):
        total = own_ref[part, :] + more_ref[part, :].astype(F32)
        total_ref[part, :] = total
        if part.start >= local:
            target = slice(part.start - local, part.stop - local)
            back_ref[target, :width] = out_ref[part, :].astype(BF16)
            back_ref[target, width:] = total.astype(BF16)


def add_core_kernel(keep_ref, got_ref, s11a_ref, s11b_ref, s10_ref, s01_ref, s00_ref):
    half = s11a_ref.shape[0]
    for z in range(keep_ref.shape[1]):
        for index, target in ((0, s00_ref), (1, s01_ref), (2, s10_ref)):
            total = keep_ref[index, z].astype(F32) + got_ref[index, z].astype(F32)
            target[z] = total.astype(BF16)
        total = (keep_ref[3, z].astype(F32) + got_ref[3, z].astype(F32)).astype(BF16)
        if z < half:
            s11a_ref[z] = total
        else:
            s11b_ref[z - half] = total


def beside(target_ref, z, values, rows, width):
    for index in range(values.shape[0] // rows):
        target_ref[z, :, index * width : (index + 1) * width] = values[index * rows : (index + 1) * rows]


def add_half_kernel(a10_ref, ax_ref, a01_ref, ay_ref, b10_ref, bx_ref, b01_ref, by_ref, o10_ref, o01_ref):
    half = ax_ref.shape[0]
    rows, width = b10_ref.shape[1], a10_ref.shape[2]
    at = a10_ref.shape[1] // rows * width
    for z in range(2 * half):
        for tall_ref, tall_got_ref, low_ref, got_ref, out_ref, first in (
            (a10_ref, ax_ref, b10_ref, bx_ref, o10_ref, 0),
            (a01_ref, ay_ref, b01_ref, by_ref, o01_ref, half),
        ):
            if first <= z < first + half:
                tall = (tall_ref[z].astype(F32) + tall_got_ref[z - first].astype(F32)).astype(BF16)
                low = (low_ref[z].astype(F32) + got_ref[z - first].astype(F32)).astype(BF16)
            else:
                tall, low = tall_ref[z], low_ref[z]
            beside(out_ref, z, tall, rows, width)
            out_ref[z, :, at:] = low


def add_both_kernel(info_ref, a_ref, b_ref, got_x_ref, got_y_ref, own_ref, near_ref, next_ref, far_ref):
    line = info_ref[0] // 8
    rows, width = b_ref.shape[1], a_ref.shape[2]
    count = a_ref.shape[1] // rows
    for z, out_ref in enumerate((own_ref, near_ref, next_ref, far_ref)):
        at = line ^ z
        for index in range(count + 1):
            if index < count:
                cols = slice(index * width, (index + 1) * width)
                own = a_ref[at, index * rows : (index + 1) * rows]
            else:
                cols = slice(count * width, got_x_ref.shape[2])
                own = b_ref[at]
            total = own.astype(F32) + got_x_ref[at, :, cols].astype(F32) + got_y_ref[at, :, cols].astype(F32)
            out_ref[:, cols] = total.astype(BF16)


def add_pair_kernel(own_ref, got_ref, sum_ref):
    sum_ref[...] = (own_ref[...].astype(F32) + got_ref[...].astype(F32)).astype(BF16)


def add_core_all_kernel(keep_ref, got_ref, *outs):
    for z in range(keep_ref.shape[1]):
        for index, target in enumerate(outs):
            target[z] = (keep_ref[index, z].astype(F32) + got_ref[index, z].astype(F32)).astype(BF16)


def add_four_kernel(info_ref, a_ref, b_ref, c_ref, d_ref, own_ref, near_ref, next_ref, far_ref):
    line = info_ref[0] // 8
    for z, out_ref in enumerate((own_ref, near_ref, next_ref, far_ref)):
        at = line ^ z
        total = a_ref[at].astype(F32) + b_ref[at].astype(F32) + c_ref[at].astype(F32)
        out_ref[...] = (total + d_ref[at].astype(F32)).astype(BF16)


def end_both_kernel(own_ref, got_ref, far_ref, tall_ref, win_ref, wo_ref, *rest):
    vectors, flip_ref = rest[:-1], rest[-1]
    rows, width = far_ref.shape[0], tall_ref.shape[1]

    def total(cols):
        return own_ref[:, cols].astype(F32) + got_ref[:, cols].astype(F32) + far_ref[:, cols].astype(F32)

    at = tall_ref.shape[0] // rows * width
    for index in range(tall_ref.shape[0] // rows):
        tall_ref[index * rows : (index + 1) * rows, :] = total(slice(index * width, (index + 1) * width))
    for out in (win_ref, wo_ref):
        out[...] = total(slice(at, at + out.shape[1]))
        at = at + out.shape[1]
    flip_ref[...] = jnp.zeros_like(flip_ref)
    flip_ref[:rows, :] = total(slice(at, at + LANES))
    turned = flip_ref[...].T
    for index, vector in enumerate(vectors):
        vector[...] = turned[index : index + 1, :rows]


def end_kernel(a_ref, b_ref, c_ref, d_ref, *outs):
    at = 0
    for out in outs:
        cols = slice(at, at + out.shape[1])
        total = a_ref[:, cols].astype(F32) + b_ref[:, cols].astype(F32)
        out[...] = total + c_ref[:, cols].astype(F32) + d_ref[:, cols].astype(F32)
        at = at + out.shape[1]


def vm():
    return pl.BlockSpec(memory_space=pltpu.VMEM)


def run(kernel, ins, outs, scratch=(), scalars=(), loose=(), pinned=(), far=(), sems=0, micros=0.05):
    specs = [vm() for _ in ins]
    for index in scalars:
        specs[index] = pl.BlockSpec(memory_space=pltpu.SMEM)
    ins = list(ins)
    for index in loose:
        specs[index] = pl.BlockSpec(memory_space=pl.ANY)
    for index in pinned:
        specs[index] = pl.BlockSpec(memory_space=pltpu.HBM)
        ins[index] = pltpu.with_memory_space_constraint(ins[index], pltpu.HBM)
    size = sum(v.size * v.dtype.itemsize for v in ins) + sum(
        functools.reduce(lambda a, b: a * b, s, 1) * jnp.dtype(t).itemsize for s, t in outs
    )
    buffers = [pltpu.VMEM(s, t) for s, t in scratch]
    need = sum(functools.reduce(lambda a, b: a * b, s, 1) * jnp.dtype(t).itemsize for s, t in scratch)
    if sems:
        buffers.append(pltpu.SemaphoreType.DMA((sems,)))
    return pl.pallas_call(
        kernel,
        out_shape=[jax.ShapeDtypeStruct(s, t) for s, t in outs],
        in_specs=specs,
        out_specs=[pl.BlockSpec(memory_space=pl.ANY) if index in far else vm() for index in range(len(outs))],
        scratch_shapes=buffers,
        compiler_params=pltpu.CompilerParams(vmem_limit_bytes=max(need + 8 * MIB, SCOPED)),
        cost_estimate=pl.CostEstimate(
            flops=int(micros * MICRO), bytes_accessed=size, transcendentals=0
        ),
    )(*ins)


AXES = ("dp", "head")


def after(value, *others):
    return lax.optimization_barrier((value, *others))[0]


class Links:
    def __init__(self, model_rows):
        self.heads = lax.axis_size("head")
        self.pods = lax.axis_size("dp")
        self.count = self.heads * self.pods
        self.fast = self.heads == 4 and self.pods == 8 and model_rows == 16
        self.head = lax.axis_index("head")
        self.me = lax.axis_index("dp") * self.heads + self.head

    def flip(self, value, bit):
        return lax.ppermute(value, AXES, [(i, i ^ bit) for i in range(self.count)])

    def flip_head(self, value, bit):
        return lax.ppermute(value, "head", [(i, i ^ bit) for i in range(self.heads)])

    def along_z(self, block):
        return [block, *(self.flip(block, 8 * k) for k in (1, 2, 3))]

    def stack(self, parts):
        (out,) = run(
            stack_kernel, parts, [((4, *parts[0].shape), BF16)], loose=range(4), far=(0,), sems=4
        )
        return out

    def core_sums(self, keep, got):
        block = keep.shape[2:]
        whole, half = ((4, *block), BF16), ((2, *block), BF16)
        return run(add_core_kernel, [keep, got], [half, half, whole, whole, whole])

    def line_parts(self, kernel, parts, shape):
        return run(kernel, [self.info, *parts], [(shape, BF16)] * 4, scalars=(0,))

    def line_first(self, kernel, parts, shape):
        own, near, following, far = self.line_parts(kernel, parts, shape)
        return own, far, self.flip(near, 8), self.flip(following, 8)

    def line_last(self, own, far, got, got_far):
        (far,) = run(add_pair_kernel, [after(far, got), got_far], [(far.shape, BF16)])
        return own, got, self.flip(far, 24)

    def spread(self, own, group):
        held, bit = own[None], 1
        while bit < group:
            got = self.flip_head(held, bit)
            held = got if bit == 1 and group == 2 else jnp.concatenate([held, got], axis=0)
            bit = bit * 2
        if group > 2:
            held = held[1:]
        return held.reshape(-1, own.shape[1])

    def collapse(self, parts, group, rows):
        if group == 2:
            return self.flip_head(parts, 1)
        held = parts.reshape(group - 1, rows, -1)
        held = jnp.concatenate([jnp.zeros_like(held[:1]), held], axis=0).astype(F32)
        bit = group // 2
        while bit >= 1:
            held = held[:bit] + self.flip_head(held[bit : 2 * bit], bit)
            bit = bit // 2
        return held[0]


def body(
    tokens, cotangent, lengths, halting, w_query, w_key, w_value, w_out, w_in, w_hidden,
    w_halt, gain_attn, shift_attn, gain_ffn, shift_ffn,
):
    micro, local, width = tokens.shape
    links = Links(w_query.shape[0])
    fast, heads = links.fast, links.heads
    group = heads // micro
    rows, length = micro * local, local * heads
    mine = links.head // group
    wide_ff = w_in.shape[1]
    fine = width // links.count
    matrices = (w_query, w_key, w_value, w_out, w_in, w_hidden)
    vectors = (w_halt, gain_attn, shift_attn, gain_ffn, shift_ffn)
    place_array = jnp.stack([links.me, mine, links.head % group, jnp.int32(group)]).astype(jnp.int32)
    links.info = place_array

    pairs = width // LANES
    row_f, row_b = ((rows, width), F32), ((rows, width), BF16)
    stat = ((rows, LANES), F32)
    others = length - rows
    long_b = ((length, width), BF16)
    q2_t = ((pairs, 2 * rows, LANES), BF16)
    p_t = ((pairs, 2 * rows, length), BF16)
    o_t = ((2 * rows, LANES), F32)
    bias_t = ((rows, length), F32)
    inner_t = ((rows, BLOCK), F32)
    ff_b = ((rows, wide_ff), BF16)
    sums_t = ((VECS, 8, width), F32)
    ds_t = ((2 * rows, length), BF16)
    dqkv_t = ((rows, 3 * width), BF16)
    doth_t = ((others, 2 * width), BF16)
    vg_t = ((8, width), F32)
    segq_t, segk_t = ((rows, LANES), jnp.int32), ((8, length), jnp.int32)

    sort_in = [place_array, tokens, cotangent, halting]
    sort_out = [((local, 2 * width + LANES), BF16)] * 2
    sort_tmp = [((LANES, local), F32), (halting.shape, jnp.int32)]
    if fast:
        send_tok, own_tok, block_a, block_b = run(
            pack_kernel,
            [*sort_in, *matrices, *(vector[None] for vector in vectors)],
            [*sort_out, ((4 * pairs + 1, fine, LANES), BF16), ((8, fine, BLOCK), BF16)],
            [*sort_tmp, ((LANES, LANES), F32), ((VECS, 1, fine), BF16)],
            scalars=(0,),
            pinned=range(1, 15),
            sems=18 + 4 * pairs,
        )
        got_tok = links.flip_head(send_tok, group)
        line_a = links.along_z(block_a)
        own_a = after(links.stack(line_a), got_tok)
        by_x, by_y = links.flip(own_a, 2), links.flip(own_a, 4)
        line_b = links.along_z(after(block_b, line_a[1]))
        plane_a = [own_a, by_x, by_y, links.flip(after(by_y, line_b[3]), 2)]
    else:
        send_tok, own_tok = run(
            sort_kernel, sort_in, sort_out, sort_tmp, scalars=(0,), pinned=(1, 2, 3), sems=5
        )
        full = [lax.all_gather(part, AXES, axis=0, tiled=True) for part in matrices]
        full_v = [lax.all_gather(part, AXES, axis=0, tiled=True) for part in vectors]
        full_a = jnp.stack(full[:4])
        full_in = jnp.transpose(full[4].reshape(width, wide_ff // BLOCK, BLOCK), (1, 0, 2))
        full_hid = full[5]
        vec = jnp.pad(jnp.stack(full_v), ((0, 8 - VECS), (0, 0))).astype(F32)

        got_tok = links.flip_head(send_tok, group)
    tok, x0, rown0, sig1, segq, segk = run(
        embed_kernel,
        [place_array, lengths[:, 0], own_tok, got_tok],
        [((rows, 2 * width + LANES), BF16), row_f, row_b, row_f, segq_t, segk_t],
        scalars=(0, 1),
    )
    roth0 = links.spread(rown0, group)
    if fast:
        own_b = after(links.stack(line_b), by_x, by_y, roth0)
        near = [own_b, links.flip(own_b, 2), links.flip(own_b, 4)]
        near = near + [links.flip(piece, 1) for piece in near]
        halves = run(
            halves_kernel,
            [near[2], near[1]],
            [((2, 8, fine, BLOCK), BF16)] * 2,
            loose=(0, 1),
            far=(0, 1),
            sems=2,
        )
        far_b = [links.flip(halves[0], 2), links.flip(halves[1], 4)]
        plane_a[3] = after(plane_a[3], halves[0])
        plane_a = plane_a + [links.flip(piece, 1) for piece in plane_a]

    attend_in = [rown0, roth0, segq, segk]
    attend_out = [q2_t, long_b, long_b, p_t, row_b]
    if fast:
        full_a, vec, q2, k, v, p, ctx = run(
            functools.partial(attend_kernel, True),
            [*attend_in, links.info, *plane_a],
            [((5, 4, 8, fine, BLOCK), BF16), vg_t, *attend_out],
            [row_b, bias_t, o_t],
            scalars=(4,),
        )
        full_a = full_a.reshape(5, width, BLOCK)
    else:
        q2, k, v, p, ctx = run(
            functools.partial(attend_kernel, False),
            [*attend_in, full_a],
            attend_out,
            [row_b, bias_t, o_t],
            micros=8,
        )
    n1, r1, nlow = run(norm_kernel, [x0, ctx, vec, full_a], [row_f, stat, row_b], [row_f], micros=1)
    ffn_out = [ff_b, ff_b, row_f, stat, stat, row_f, row_f, row_f, row_b]
    ffn_in = [n1, nlow, tok, sig1, vec]
    if fast:
        far_b = [after(piece, ctx) for piece in far_b]
        far_b = far_b + [links.flip(piece, 1) for piece in far_b]
        full_in, full_hid, *got = run(
            functools.partial(ffn_kernel, True),
            [*ffn_in, links.info, *near, *far_b],
            [((4, 4, 8, fine, BLOCK), BF16), ((4, 8, 4, fine, BLOCK), BF16), *ffn_out],
            [inner_t, row_f],
            scalars=(5,),
            micros=5.5,
        )
        full_in = full_in.reshape(4, width, BLOCK)
        full_hid = full_hid.reshape(wide_ff, width)
    else:
        got = run(
            functools.partial(ffn_kernel, False),
            [*ffn_in, full_in, full_hid],
            ffn_out,
            [inner_t, row_f],
            micros=5.5,
        )
    hid, dg, n2, r2, rate, state, pooled, x1, rown1 = got
    roth1 = links.spread(rown1, group)
    out, gs, goth, nlow1, hid1, b11, b21, ctx1, b01, dqkv1, doth1, vg1 = run(
        turn_kernel,
        [x1, rown1, roth1, full_a, full_in, full_hid, vec, segq, segk, state, pooled, tok],
        [row_f, row_f, ((others, width), BF16), row_b, ff_b, ff_b, row_b, row_b, row_b, dqkv_t, doth_t, vg_t],
        [
            row_b, q2_t, long_b, long_b, p_t, bias_t, o_t, row_f, row_f, stat, inner_t, ff_b,
            row_f, stat, stat, row_f, row_f, sums_t, row_b, q2_t, ds_t,
        ],
        micros=15.7,
    )
    more = links.collapse(goth, group, rows)

    b_cols = wide_ff + width + LANES
    def parts_of(shape, whole):
        return [((4, 4, *shape), BF16)] * 2 if fast else [(whole, F32)]

    hid_out = parts_of((4 * fine, width), (wide_ff, width))
    in_out = parts_of((fine, b_cols), (width, b_cols))
    attend_outs = parts_of((fine, 3 * width), (width, 3 * width))
    whole_shape = (4, 8, fine, BLOCK) if fast else (16, LANES)
    tall_shape = (8, 4 * fine, width) if fast else (16, LANES)
    b2, gsec, base, sums, *hid_parts = run(
        functools.partial(hidden_back_kernel, fast),
        [links.info, gs, more, tok, vec, n2, r2, rate, hid, hid1, b21],
        [row_b, row_f, row_f, sums_t, *hid_out],
        [(tall_shape, BF16)],
        scalars=(0,),
        micros=2,
    )
    b1, b0, base, gctx, sums = run(
        feed_back_kernel,
        [b2, gsec, base, sums, vec, full_in, full_hid, full_a, n1, r1, dg],
        [ff_b, row_b, row_f, row_b, sums_t],
        [inner_t, row_f],
        micros=2.2,
    )
    if fast:
        c_sums = links.core_sums(hid_parts[0], links.flip(hid_parts[1], 1))
        b1 = after(b1, c_sums[0])
    in_parts = run(
        functools.partial(weights_back_kernel, fast),
        [links.info, b1, b0, sums, nlow, ctx, nlow1, b11, ctx1, b01, vg1],
        in_out,
        [(whole_shape, BF16), ((LANES, width), F32)],
        scalars=(0,),
        micros=2,
    )
    if fast:
        b_sums = links.core_sums(in_parts[0], links.flip(in_parts[1], 1))
        gctx = after(gctx, b_sums[0])
    dqkv0, doth0 = run(
        heads_back_kernel,
        [gctx, q2, k, v, p, ctx],
        [dqkv_t, doth_t],
        [q2_t, ds_t, o_t],
        micros=3,
    )
    g0, goth0, *attend_parts = run(
        functools.partial(project_back_kernel, fast),
        [links.info, base, full_a, rown0, roth0, rown1, roth1, dqkv1, doth1, dqkv0, doth0],
        [row_f, ((others, width), BF16), *attend_outs],
        [(whole_shape, BF16)],
        scalars=(0,),
    )
    if fast:
        c11a, c11b, c10, c01, c00 = c_sums
        b11a, b11b, b10, b01, b00 = b_sums
        halves = [
            after(c10, g0), links.flip(c11a, 2), c01, links.flip(c11b, 4),
            b10, links.flip(b11a, 2), b01, links.flip(b11b, 4),
        ]
        both_t = ((4, fine, 4 * width + b_cols), BF16)
        both10, both01 = run(add_half_kernel, halves, [both_t] * 2)
        goth0, send_a = after(goth0, both01), after(attend_parts[1], both01)
    inputs, back = run(
        send_kernel,
        [g0, links.collapse(goth0, group, rows), out],
        [row_f, ((local, 2 * width), BF16)],
    )
    if fast:
        keep, got = after(attend_parts[0], back), links.flip(send_a, 1)
        a00, a01, a10, a11 = run(add_core_all_kernel, [keep, got], [(keep.shape[1:], BF16)] * 4)
        by_plane = [a00, links.flip(a11, 6), links.flip(a01, 2), links.flip(a10, 4)]
        both = links.line_first(
            add_both_kernel, [after(c00, a00), b00, links.flip(both01, 2), links.flip(both10, 4)], both_t[0][1:]
        )
        first_sums = both[0]
        by_plane[0] = after(by_plane[0], both[0])
        attend_sums = links.line_parts(add_four_kernel, by_plane, a00.shape[1:])
        both = links.line_last(both[0], after(both[1], attend_sums[0]), *both[2:])
        attend_sums = [attend_sums[0], *(links.flip(attend_sums[k], 8 * k) for k in (1, 2, 3))]
        back = after(back, first_sums)
        output, input_grad = run(
            return_kernel,
            [links.info, out, inputs, links.flip_head(back, group)],
            [((micro, local, width), F32)] * 2,
            scalars=(0,),
        )
        g_hidden, g_in, g_out, *g_vectors = run(
            end_both_kernel,
            [after(both[0], output), *both[1:]],
            [((4 * fine, width), F32), ((fine, wide_ff), F32), ((fine, width), F32)] + [((1, fine), F32)] * VECS,
            [((LANES, LANES), F32)],
        )
        g_query, g_key, g_value = run(
            end_kernel,
            [after(attend_sums[0], output, g_hidden), *attend_sums[1:]],
            [((fine, width), F32)] * 3,
        )
        g_vectors = [vector.reshape(fine) for vector in g_vectors]
    else:
        sums = [
            *(attend_parts[0][:, index * width : (index + 1) * width] for index in range(3)),
            in_parts[0][:, wide_ff : wide_ff + width], in_parts[0][:, :wide_ff], hid_parts[0],
            in_parts[0][:, wide_ff + width :],
        ]
        sums = [lax.psum_scatter(part, AXES, scatter_dimension=0, tiled=True) for part in sums]
        g_query, g_key, g_value, g_out, g_in, g_hidden, g_vec = sums
        g_vectors = [g_vec[:, index] for index in range(VECS)]
        output, input_grad = run(
            return_kernel,
            [links.info, out, inputs, links.flip_head(back, group)],
            [((micro, local, width), F32)] * 2,
            scalars=(0,),
        )
    return (output, input_grad, g_query, g_key, g_value, g_out, g_in, g_hidden, *g_vectors)


def solution(mesh):
    whole = P(("dp", "head"))
    matrix = P(("dp", "head"), None)
    rows = P(None, ("dp", "head"), None)
    return jax.shard_map(
        body,
        mesh=mesh,
        in_specs=(rows, rows, P(None, "dp", None), P(None, None, ("dp", "head")))
        + (matrix,) * 6
        + (whole,) * 5,
        out_specs=(rows, rows) + (matrix,) * 6 + (whole,) * 5,
        check_vma=False,
    )
```
